32 devices in a mesh: dp: 8 (over y, x, core), tp: 4 (over z).
Axes of the slice: x: 2, y: 2, z: 4, core: 2. Of those that a mesh axis runs over, the one named last changes fastest.
Arguments:
- tokens: bfloat16 [32, 1024, 768], P('dp', 'tp'), may hold values from -6 to 6
- lengths: int32 [32], P('dp'), may hold values from 64 to 1024, as said below
- w_qkv: bfloat16 [3, 768, 768], P(None, 'dp', 'tp'), may hold values from -0.21875 to 0.21875
- w_out: bfloat16 [768, 768], P('tp', 'dp'), may hold values from -1.75 to 1.75
- w_gate_up: bfloat16 [2, 768, 2048], P(None, 'dp', 'tp'), may hold values from -0.21875 to 0.21875
- w_down: bfloat16 [2048, 768], P('tp', 'dp'), may hold values from -0.1875 to 0.1875
- gains: float32 [2, 768], P(None, ('dp', 'tp')), may hold values from 0.5 to 1.5
- cotangent: bfloat16 [32, 1024, 768], P('dp', 'tp'), may hold values from -6 to 6
Outputs:
- layer_out: bfloat16 [32, 1024, 768], P('dp', 'tp')
- grad_tokens: float32 [32, 1024, 768], P('dp', 'tp')
- grad_w_qkv: float32 [3, 768, 768], P(None, 'dp', 'tp')
- grad_w_out: float32 [768, 768], P('tp', 'dp')
- grad_w_gate_up: float32 [2, 768, 2048], P(None, 'dp', 'tp')
- grad_w_down: float32 [2048, 768], P('tp', 'dp')
- grad_gains: float32 [2, 768], P(None, ('dp', 'tp'))
The draws below stay inside these ranges and needn't reach their ends.
Inputs may be any that keep to these rules, and one draw needn't show every extreme that they name: `lengths`: valid tokens of each sequence, counted from its start; among the 4 sequences of each index of dp at least one has all 1024.
All inputs are finite; a program needn't handle non-finite values.
Results may differ from the reference program's by a relative error of at most 0.023.
Values may be sent and summed in bfloat16 or wider, within the bound.
A program may use at most 192 MiB of HBM per device.

```python
import jax
import jax.numpy as jnp
from jax import lax

D = 768
HEADS = 12
HEAD = 64
FF = 2048
SEQS_DEV = 4
LEN = 1024
MIN_LEN = 64
BATCH = 32


def draw_lengths(key, part):
    key = jax.random.fold_in(key, 7)
    key_coin, key_shift, key_extra, key_pick = jax.random.split(key, 4)
    groups = BATCH // SEQS_DEV
    coin = jax.random.randint(key_coin, (BATCH,), 0, 10)
    shift = jax.random.randint(key_shift, (BATCH,), 1, 5)
    base = jnp.right_shift(jnp.full((BATCH,), LEN, jnp.int32), shift.astype(jnp.int32))
    extra = jax.random.randint(key_extra, (BATCH,), 0, LEN) % base
    short = jnp.maximum(base + extra, MIN_LEN)
    drawn = jnp.where(coin < 6, LEN, short).reshape(groups, SEQS_DEV)
    pick = jax.random.randint(key_pick, (groups,), 0, SEQS_DEV)
    slot = jnp.arange(SEQS_DEV)
    full = slot[None, :] == pick[:, None]
    least = (slot[None, :] == (pick[:, None] + 1) % SEQS_DEV) & (jnp.arange(groups)[:, None] == 0)
    drawn = jnp.where(least, MIN_LEN, drawn)
    drawn = jnp.where(full, LEN, drawn)
    return drawn.reshape(BATCH).astype(jnp.int32)


def levels(rng, extent, shards, low, top_value):
    loudness, own = 1.0, jax.random.fold_in(rng, 6)
    for dim, parts in shards:
        steps = jnp.exp(jax.random.uniform(jax.random.fold_in(own, dim), (parts,), jnp.float32, low / len(shards), top_value / len(shards)))
        loudness = loudness * jnp.repeat(steps, extent[dim] // parts).reshape([-1 if axis == dim else 1 for axis in range(len(extent))])
    return loudness


def centred(stream_key, dims, deviation, most, cuts=(), kind=jnp.bfloat16):
    factor_of = levels(stream_key, dims, cuts, -0.22, 0.18) if cuts else 1.0
    array = jax.random.normal(stream_key, dims, jnp.float32) * deviation * factor_of
    return jnp.minimum(jnp.maximum(array, -most), most).astype(kind)


def setup_inputs(seed: int = 0) -> dict:
    arg_keys = jax.random.split(jax.random.key(seed), 9)
    tokens = centred(arg_keys[0], (BATCH, LEN, D), 1.0, 6.0, ((0, 8), (1, 4)))
    lengths = draw_lengths(jax.random.fold_in(arg_keys[8], 71), 0)
    w_qkv = centred(arg_keys[2], (3, D, D), D ** -0.5, 0.21875, ((1, 8), (2, 4)))
    w_out = centred(arg_keys[3], (D, D), (D // 64) ** -0.5, 1.75, ((0, 4), (1, 8)))
    w_gate_up = centred(arg_keys[4], (2, D, FF), D ** -0.5, 0.21875, ((1, 8), (2, 4)))
    w_down = centred(arg_keys[5], (FF, D), (FF // 2) ** -0.5, 0.1875, ((0, 4), (1, 8)))
    gains = jnp.clip(1.0 + 0.1 * jax.random.normal(arg_keys[6], (2, D), jnp.float32), 0.5, 1.5)
    cotangent = centred(arg_keys[7], (BATCH, LEN, D), 1.0, 6.0, ((0, 8), (1, 4)))
    return dict(tokens=tokens, lengths=lengths, w_qkv=w_qkv, w_out=w_out, w_gate_up=w_gate_up, w_down=w_down, gains=gains, cotangent=cotangent)


eps = 1e-06
masked_score = -1e+30

@jax.custom_vjp
def low(v):
    return lax.optimization_barrier(v.astype(jnp.bfloat16)).astype(jnp.float32)

@jax.custom_vjp
def low_back(v):
    return v

def low_keep(v):
    return (low(v), None)

def low_pass(kept, grad):
    return (grad,)

def back_keep(v):
    return (v, None)

def backward_reduced(kept, grad):
    return (low(grad),)
low.defvjp(low_keep, low_pass)
low_back.defvjp(back_keep, backward_reduced)

def rope_tables(length, width):
    half = width // 2
    freqs = 10000.0 ** (-2.0 * jnp.arange(half, dtype=jnp.float32) / width)
    angles = jnp.arange(length, dtype=jnp.float32)[:, None] * freqs[None, :]
    angles = jnp.concatenate([angles, angles], axis=1)
    return (jnp.cos(angles), jnp.sin(angles))

def rotate(values, cosine, sine):
    half = values.shape[-1] // 2
    turned = jnp.concatenate([-values[..., half:], values[..., :half]], axis=-1)
    return values * cosine + turned * sine

def attend_group(queries, keys, values, lengths):
    rows = min(512, LEN)
    count = LEN // rows
    scale = HEAD ** (-0.5)
    group = queries.shape[0]
    q_blocks = jnp.moveaxis(queries.reshape(group, HEADS, count, rows, HEAD), 2, 0)
    starts = (jnp.arange(count) * rows).astype(jnp.int32)

    def one_block(item):
        block, start = item
        query_pos = start + jnp.arange(rows).astype(jnp.int32)
        key_pos = jnp.arange(LEN).astype(jnp.int32)
        allowed = (key_pos[None, None, :] <= query_pos[None, :, None]) & (key_pos[None, None, :] < lengths[:, None, None])
        scores = jnp.einsum('shqd,shkd->shqk', block, keys, precision=lax.Precision.HIGHEST) * scale
        scores = low_back(scores)
        scores = jnp.where(allowed[:, None], scores, masked_score)
        probs = low(jax.nn.softmax(scores, axis=-1))
        return jnp.einsum('shqk,shkd->shqd', probs, values, precision=lax.Precision.HIGHEST)
    blocks = lax.map(jax.checkpoint(one_block), (q_blocks, starts))
    return jnp.moveaxis(blocks, 0, 2).reshape(queries.shape)

def project(left_operand, right_operand):
    return jnp.einsum('jgb,bx->jgx', left_operand, right_operand, precision=lax.Precision.HIGHEST)

def layer(x, w_qkv, w_out, w_gate_up, w_down, gains, valid, lengths):
    group = x.shape[0]
    cosine, sine = rope_tables(LEN, HEAD)
    cosine = cosine[:, None, :]
    sine = sine[:, None, :]
    scale1 = lax.rsqrt(lax.optimization_barrier(jnp.mean(x * x, axis=-1, keepdims=True)) + eps)
    normed1 = low(x * scale1 * gains[0])
    raw_q = low_back(project(normed1, w_qkv[0])).reshape(group, LEN, HEADS, HEAD)
    raw_k = low_back(project(normed1, w_qkv[1])).reshape(group, LEN, HEADS, HEAD)
    raw_v = low_back(project(normed1, w_qkv[2])).reshape(group, LEN, HEADS, HEAD)
    queries = jnp.transpose(low(rotate(raw_q, cosine, sine)), (0, 2, 1, 3))
    keys = jnp.transpose(low(rotate(raw_k, cosine, sine)), (0, 2, 1, 3))
    values = jnp.transpose(low(raw_v), (0, 2, 1, 3))
    context = attend_group(queries, keys, values, lengths)
    context = jnp.transpose(context, (0, 2, 1, 3)).reshape(group, LEN, D)
    context = low(low_back(context))
    attn_out = low_back(project(context, w_out))
    hidden = x + valid[..., None] * attn_out
    scale2 = lax.rsqrt(lax.optimization_barrier(jnp.mean(hidden * hidden, axis=-1, keepdims=True)) + eps)
    normed2 = low(hidden * scale2 * gains[1])
    gate = low_back(project(normed2, w_gate_up[0]))
    up = low_back(project(normed2, w_gate_up[1]))
    activated = low(jax.nn.silu(gate) * up)
    mlp_out = low_back(project(activated, w_down))
    return hidden + valid[..., None] * mlp_out

def reference(tokens, lengths, w_qkv, w_out, w_gate_up, w_down, gains, cotangent):
    groups = BATCH // SEQS_DEV
    inputs = tokens.astype(jnp.float32).reshape(groups, SEQS_DEV, LEN, D)
    grads_in = cotangent.astype(jnp.float32).reshape(groups, SEQS_DEV, LEN, D)
    group_lengths = lengths.reshape(groups, SEQS_DEV)
    params = (w_qkv.astype(jnp.float32), w_out.astype(jnp.float32), w_gate_up.astype(jnp.float32), w_down.astype(jnp.float32), gains.astype(jnp.float32))

    def step(totals, item):
        x_group, grad_group, length_group = item
        valid = (jnp.arange(LEN).astype(jnp.int32)[None, :] < length_group[:, None]).astype(jnp.float32)

        def forward(x_in, wq_in, wo_in, wg_in, wd_in, gain_in):
            return layer(x_in, wq_in, wo_in, wg_in, wd_in, gain_in, valid, length_group)
        result, pullback = jax.vjp(forward, x_group, params[0], params[1], params[2], params[3], params[4])
        grads = pullback(grad_group)
        totals = tuple((total + grad for total, grad in zip(totals, grads[1:])))
        return (totals, (result.astype(jnp.bfloat16), grads[0]))
    zeros = tuple((jnp.zeros_like(param) for param in params))
    totals, (results, d_inputs) = lax.scan(step, zeros, (inputs, grads_in, group_lengths))
    return (results.reshape(BATCH, LEN, D), d_inputs.reshape(BATCH, LEN, D), totals[0], totals[1], totals[2], totals[3], totals[4])
```

```python
import jax
import jax.numpy as jnp
from jax import lax
from jax.sharding import PartitionSpec as P

HEAD = 64
EPS = 1e-06
MASKED = -1e30
F32 = jnp.float32
BF16 = jnp.bfloat16


def rope_tables(length, width):
    half = width // 2
    freqs = 10000.0 ** (-2.0 * jnp.arange(half, dtype=F32) / width)
    angles = jnp.arange(length, dtype=F32)[:, None] * freqs[None, :]
    angles = jnp.concatenate([angles, angles], axis=1)
    return jnp.cos(angles), jnp.sin(angles)


def rotate(values, cosine, sine):
    half = values.shape[-1] // 2
    turned = jnp.concatenate([-values[..., half:], values[..., :half]], axis=-1)
    return values * cosine + turned * sine


def unrotate(grads, cosine, sine):
    half = grads.shape[-1] // 2
    scaled = grads * sine
    turned = jnp.concatenate([scaled[..., half:], -scaled[..., :half]], axis=-1)
    return grads * cosine + turned


def dot(spec, a, b):
    return jnp.einsum(spec, a, b, preferred_element_type=F32)


def pack_weights(w_qkv, w_out, w_gate_up, w_down):
    attn = jnp.concatenate([w_qkv[0], w_qkv[1], w_qkv[2], w_out.T], axis=1)
    mlp = jnp.concatenate([w_gate_up[0], w_gate_up[1], w_down.T], axis=1)
    return attn, mlp


def unpack_grads(g_attn, g_mlp, hw, fw):
    g_qkv = jnp.stack([g_attn[:, i * hw : (i + 1) * hw] for i in range(3)])
    g_gate_up = jnp.stack([g_mlp[:, i * fw : (i + 1) * fw] for i in range(2)])
    return g_qkv, g_attn[:, 3 * hw :].T, g_gate_up, g_mlp[:, 2 * fw :].T


def gather_all(shard):
    cols = lax.all_gather(shard, "tp", axis=0)
    return lax.all_gather(cols, "dp", axis=1, tiled=True)


def scatter_all(full):
    rows = lax.psum_scatter(full, "dp", scatter_dimension=1, tiled=True)
    return lax.psum_scatter(rows, "tp", scatter_dimension=0, tiled=False)


def to_sequences(local):
    return lax.all_to_all(local, "tp", split_axis=0, concat_axis=1, tiled=True)


def to_positions(whole):
    return lax.all_to_all(whole, "tp", split_axis=1, concat_axis=0, tiled=True)


def compute(x16, cot16, lengths, w_attn, w_mlp, gains):
    n, t, d = x16.shape
    tp = w_attn.shape[0]
    hw, fw = w_attn.shape[2] // 4, w_mlp.shape[2] // 3
    heads = hw // HEAD
    scale = HEAD**-0.5
    x = x16.astype(F32)
    dout = cot16.astype(F32)
    pos = jnp.arange(t)
    valid = (pos[None, :] < lengths[:, None]).astype(F32)[..., None]
    cosine, sine = rope_tables(t, HEAD)
    r1 = lax.rsqrt(jnp.mean(x * x, axis=-1, keepdims=True) + EPS)
    xhat1 = x * r1
    n1 = (xhat1 * gains[0]).astype(BF16)
    raw = dot("ntd,zdcje->czjnte", n1, w_attn[:, :, : 3 * hw].reshape(tp, d, 3, heads, HEAD))
    q = rotate(raw[0], cosine, sine).astype(BF16)
    k = rotate(raw[1], cosine, sine).astype(BF16)
    v = raw[2].astype(BF16)
    ok = (pos[None, :] <= pos[:, None])[None] & (pos[None, None, :] < lengths[:, None, None])

    def attend(item):
        qh, kh, vh = item
        s = jnp.where(ok, dot("nqe,nke->nqk", qh, kh) * scale, MASKED)
        top = jnp.max(s, axis=-1, keepdims=True)
        e = jnp.exp(s - top)
        total = jnp.sum(e, axis=-1, keepdims=True)
        p = (e / total).astype(BF16)
        return dot("nqk,nke->nqe", p, vh).astype(BF16), top + jnp.log(total)

    flat = lambda a: a.reshape((tp * heads,) + a.shape[2:])
    ctx, lse = lax.map(attend, (flat(q), flat(k), flat(v)))
    ctx_t = jnp.transpose(ctx.reshape(tp, heads, n, t, HEAD), (2, 3, 0, 1, 4)).reshape(n, t, tp, hw)
    w_o = w_attn[:, :, 3 * hw :]
    attn = dot("ntze,zde->ntd", ctx_t, w_o)
    hidden = x + valid * attn
    r2 = lax.rsqrt(jnp.mean(hidden * hidden, axis=-1, keepdims=True) + EPS)
    xhat2 = hidden * r2
    n2 = (xhat2 * gains[1]).astype(BF16)
    dm = (valid * dout).astype(BF16)
    mlp = jnp.zeros((n, t, d), F32)
    dn2 = jnp.zeros((n, t, d), F32)
    g_mlp = []
    for z in range(tp):
        wg, wu, wd = (w_mlp[z, :, i * fw : (i + 1) * fw] for i in range(3))
        gate = dot("ntd,df->ntf", n2, wg)
        up = dot("ntd,df->ntf", n2, wu)
        s = jax.nn.sigmoid(gate)
        sw = gate * s
        act = (sw * up).astype(BF16)
        mlp += dot("ntf,df->ntd", act, wd)
        d_act = dot("ntd,df->ntf", dm, wd)
        dg = (d_act * up * s * (1.0 + gate * (1.0 - s))).astype(BF16)
        du = (d_act * sw).astype(BF16)
        dn2 += dot("ntf,df->ntd", dg, wg) + dot("ntf,df->ntd", du, wu)
        g_mlp.append(
            jnp.concatenate(
                [dot("ntd,ntf->df", n2, dg), dot("ntd,ntf->df", n2, du), dot("ntd,ntf->df", dm, act)], axis=1
            )
        )
    layer_out = (hidden + valid * mlp).astype(BF16)
    e2 = dn2 * gains[1]
    d_hidden = dout + r2 * (e2 - xhat2 * jnp.mean(e2 * xhat2, axis=-1, keepdims=True))
    gg2 = jnp.sum(dn2 * xhat2, axis=(0, 1))
    d_attn = (valid * d_hidden).astype(BF16)
    g_o = dot("ntd,ntze->zde", d_attn, ctx_t)
    d_ctx = dot("ntd,zdje->zjnte", d_attn, w_o.reshape(tp, d, heads, HEAD)).astype(BF16)

    def back(item):
        qh, kh, vh, l, g = item
        p = jnp.where(ok, jnp.exp(dot("nqe,nke->nqk", qh, kh) * scale - l), 0.0)
        dp = dot("nqe,nke->nqk", g, vh)
        delta = jnp.sum(p * dp, axis=-1, keepdims=True)
        ds = (p * (dp - delta)).astype(BF16)
        return (
            dot("nqk,nke->nqe", ds, kh) * scale,
            dot("nqk,nqe->nke", ds, qh) * scale,
            dot("nqk,nqe->nke", p.astype(BF16), g),
        )

    dq, dk, dv = lax.map(back, (flat(q), flat(k), flat(v), lse, flat(d_ctx)))
    d_qkv = jnp.stack([unrotate(dq, cosine, sine), unrotate(dk, cosine, sine), dv]).astype(BF16)
    d_qkv = jnp.transpose(d_qkv.reshape(3, tp, heads, n, t, HEAD), (3, 4, 1, 0, 2, 5)).reshape(n, t, tp, 3 * hw)
    g_qkv = dot("ntd,ntze->zde", n1, d_qkv)
    dn1 = dot("ntze,zde->ntd", d_qkv, w_attn[:, :, : 3 * hw])
    e1 = dn1 * gains[0]
    grad_x = d_hidden + r1 * (e1 - xhat1 * jnp.mean(e1 * xhat1, axis=-1, keepdims=True))
    gg1 = jnp.sum(dn1 * xhat1, axis=(0, 1))
    g_attn = jnp.concatenate([g_qkv, g_o], axis=2)
    return layer_out, grad_x, g_attn, jnp.stack(g_mlp), jnp.stack([gg1, gg2])


def body(tokens, lengths, w_qkv, w_out, w_gate_up, w_down, gains, cotangent):
    tp = lax.axis_size("tp")
    batch = tokens.shape[0]
    n = batch // tp
    hw, fw = w_qkv.shape[2], w_gate_up.shape[2]
    full_gains = lax.all_gather(gains, ("dp", "tp"), axis=1, tiled=True)
    attn, mlp = pack_weights(w_qkv, w_out, w_gate_up, w_down)
    x16 = to_sequences(tokens)
    w_attn = gather_all(attn)
    w_mlp = gather_all(mlp)
    cot16 = to_sequences(cotangent)
    own = lax.dynamic_slice_in_dim(lengths, lax.axis_index("tp") * n, n)
    layer_out, grad_x, g_attn, g_mlp, g_gains = compute(x16, cot16, own, w_attn, w_mlp, full_gains)
    out = to_positions(layer_out)
    gx = to_positions(grad_x.astype(BF16)).astype(F32)
    s_mlp = scatter_all(g_mlp)
    s_attn = scatter_all(g_attn)
    s_gains = lax.psum_scatter(g_gains, ("dp", "tp"), scatter_dimension=1, tiled=True)
    g_qkv, g_out, g_gate_up, g_down = unpack_grads(s_attn, s_mlp, hw, fw)
    return out, gx, g_qkv, g_out, g_gate_up, g_down, s_gains


def solution(mesh):
    act = P("dp", "tp", None)
    ins = (act, P("dp"), P(None, "dp", "tp"), P("tp", "dp"), P(None, "dp", "tp"), P("tp", "dp"), P(None, ("dp", "tp")), act)
    outs = (act, act, P(None, "dp", "tp"), P("tp", "dp"), P(None, "dp", "tp"), P("tp", "dp"), P(None, ("dp", "tp")))
    return jax.shard_map(body, mesh=mesh, in_specs=ins, out_specs=outs, check_vma=False)
```

```python
import numpy as np
import jax
import jax.numpy as jnp
from jax import lax
from jax.experimental import pallas as pl
from jax.experimental.pallas import tpu as pltpu
from jax.sharding import PartitionSpec as P

F32 = jnp.float32
BF16 = jnp.bfloat16
HEAD = 64
EPS = 1e-6
LOG2E = 1.4426950408889634
C2 = LOG2E * HEAD**-0.5
NEG = -1e30
BLK = 256


def dg(a, b, ca, cb):
    return lax.dot_general(a, b, (((ca,), (cb,)), ((), ())), preferred_element_type=F32)


def nn(a, b):
    return dg(a, b, 1, 0)


def nt(a, b):
    return dg(a, b, 1, 1)


def tn(a, b):
    return dg(a, b, 0, 0)


def rows_of(m):
    return pl.ds(pl.multiple_of(m * BLK, BLK), BLK)


def half_lane():
    return lax.broadcasted_iota(jnp.int32, (1, 128), 1) % HEAD < HEAD // 2


def head_lane(h):
    lane = lax.broadcasted_iota(jnp.int32, (1, 128), 1)
    return lane < HEAD if h == 0 else lane >= HEAD


def turned(v):
    return jnp.where(half_lane(), pltpu.roll(v, 96, 1), pltpu.roll(v, 32, 1))


def norm_rows(x, gain):
    r = lax.rsqrt(jnp.mean(x * x, axis=-1, keepdims=True) + EPS)
    return x * r, r


def qkv_stage(t, d, x_ref, gains_ref, wa_ref, cos_ref, sin_ref, n1_ref, q_ref, k_ref, v_ref):
    @pl.loop(0, t // BLK)
    def _(m):
        rs = rows_of(m)
        unit, _ = norm_rows(x_ref[rs, :].astype(F32), None)
        n1_ref[rs, :] = (unit * gains_ref[0:1, :]).astype(BF16)

    for c, out in enumerate((q_ref, k_ref, v_ref)):

        @pl.loop(0, d // 256)
        def _(j, c=c, out=out):
            cols = pl.ds(pl.multiple_of(c * d + j * 256, 256), 256)
            raw = nn(n1_ref[...], wa_ref[:, cols])
            for s in range(2):
                part = raw[:, s * 128 : (s + 1) * 128]
                if c < 2:
                    part = part * cos_ref[...] + turned(part) * sin_ref[...]
                out[:, pl.ds(pl.multiple_of(j * 256 + s * 128, 128), 128)] = part.astype(BF16)


def key_bias(t, length):
    pos = lax.broadcasted_iota(jnp.int32, (t, 1), 0)
    return jnp.where(pos < length, 0.0, NEG).astype(BF16)


def causal_block():
    key = lax.broadcasted_iota(jnp.int32, (BLK, BLK), 0)
    query = lax.broadcasted_iota(jnp.int32, (BLK, BLK), 1)
    return key <= query


def score_operands(h, qp, kp, bias):
    mine = head_lane(h)
    lane = lax.broadcasted_iota(jnp.int32, (1, 128), 1)
    spare = lane == (HEAD if h == 0 else 0)
    zero = jnp.zeros((), BF16)
    q_m = jnp.where(mine, qp, zero)
    k_m = jnp.where(mine, kp, zero)
    q_s = jnp.where(spare, jnp.ones((), BF16), q_m)
    k_s = jnp.where(spare, bias, k_m)
    return q_m, k_m, q_s, k_s


def mask_diag(s, i):
    if i == 0:
        return jnp.where(causal_block(), s, NEG)
    return jnp.concatenate([s[: i * BLK], jnp.where(causal_block(), s[i * BLK :], NEG)], axis=0)


def attend_stage(t, d, length, q_ref, k_ref, v_ref, ctxt_ref, lse_ref):
    bias = key_bias(t, length)

    @pl.loop(0, d // 128)
    def _(p):
        cols = pl.ds(pl.multiple_of(p * 128, 128), 128)
        qp, kp, vp = q_ref[:, cols], k_ref[:, cols], v_ref[:, cols]
        for h in range(2):
            _, _, q_s, k_s = score_operands(h, qp, kp, bias)
            for i in range(t // BLK):
                n = (i + 1) * BLK
                s = mask_diag(nt(k_s[:n], q_s[i * BLK : n]), i)
                top = jnp.max(s, axis=0, keepdims=True)
                e = jnp.exp2((s - top) * C2)
                total = jnp.sum(e, axis=0, keepdims=True)
                o = tn(vp[:n], e.astype(BF16))[h * HEAD : (h + 1) * HEAD] / total
                ctxt_ref[pl.ds(pl.multiple_of(p * 128 + h * HEAD, HEAD), HEAD), i * BLK : n] = o.astype(BF16)
                lse_ref[pl.ds(p * 2 + h, 1), i * BLK : n] = top * C2 + jnp.log2(total)


def out_stage(t, d, length, x_ref, wa_ref, ctxt_ref, hid_ref):
    @pl.loop(0, d // 256)
    def _(j):
        cols = pl.ds(pl.multiple_of(j * 256, 256), 256)
        out = dg(ctxt_ref[...], wa_ref[cols, 3 * d : 4 * d], 0, 1)
        pos = lax.broadcasted_iota(jnp.int32, (t, 1), 0)
        hid_ref[:, cols] = x_ref[:, cols].astype(F32) + jnp.where(pos < length, out, 0.0)


def k1(len_ref, x_ref, gains_ref, wa_ref, cos_ref, sin_ref, q_ref, k_ref, v_ref, ctxt_ref, lse_ref, hid_ref, n1_ref, stages=(1, 1, 1)):
    t, d = x_ref.shape
    length = len_ref[0]
    if stages[0]:
        qkv_stage(t, d, x_ref, gains_ref, wa_ref, cos_ref, sin_ref, n1_ref, q_ref, k_ref, v_ref)
    if stages[1]:
        attend_stage(t, d, length, q_ref, k_ref, v_ref, ctxt_ref, lse_ref)
    if stages[2]:
        out_stage(t, d, length, x_ref, wa_ref, ctxt_ref, hid_ref)


def token_mask(m, length):
    pos = m * BLK + lax.broadcasted_iota(jnp.int32, (BLK, 1), 0)
    return pos < length


def mlp_chunk(t, d, f, wm, gm, n2_ref, dm_ref, n2t_ref, dmt_ref, act_ref, dgu_ref, mlp_ref, dn2_ref, first):
    w = 256
    for j in range(f // w):
        lo, hi = j * w, (j + 1) * w
        gate = nn(n2_ref[...], wm[:, lo:hi])
        up = nn(n2_ref[...], wm[:, f + lo : f + hi])
        d_act = nn(dm_ref[...], wm[:, 2 * f + lo : 2 * f + hi])
        s = 1.0 / (1.0 + jnp.exp2(gate * (-LOG2E)))
        sw = gate * s
        act_ref[:, lo:hi] = (sw * up).astype(BF16)
        dgu_ref[:, lo:hi] = (d_act * up * (s + sw * (1.0 - s))).astype(BF16)
        dgu_ref[:, f + lo : f + hi] = (d_act * sw).astype(BF16)

    for j in range(d // 256):
        cols = slice(j * 256, (j + 1) * 256)
        a = nt(act_ref[...], wm[cols, 2 * f :])
        b = nt(dgu_ref[...], wm[cols, : 2 * f])
        if first:
            mlp_ref[:, cols] = a
            dn2_ref[:, cols] = b
        else:
            mlp_ref[:, cols] += a
            dn2_ref[:, cols] += b
    for j in range(2 * f // 256):
        cols = slice(j * 256, (j + 1) * 256)
        gm[:, cols] = nn(n2t_ref[...], dgu_ref[:, cols]).astype(BF16)
    for j in range(f // 256):
        cols = slice(j * 256, (j + 1) * 256)
        gm[:, 2 * f + j * 256 : 2 * f + (j + 1) * 256] = nn(dmt_ref[...], act_ref[:, cols]).astype(BF16)


def k2(len_ref, cot_ref, gains_ref, hid_ref, wm_ref, lo_ref, dh_ref, da_ref, gm_ref, gg_ref,
       n2_ref, dm_ref, n2t_ref, dmt_ref, act_ref, dgu_ref, mlp_ref, dn2_ref):
    t, d = cot_ref.shape
    tp, _, f3 = wm_ref.shape
    f = f3 // 3
    length = len_ref[0]

    @pl.loop(0, t // BLK)
    def _(m):
        rs = rows_of(m)
        unit, _ = norm_rows(hid_ref[rs, :], None)
        n2 = (unit * gains_ref[1:2, :]).astype(BF16)
        n2_ref[rs, :] = n2
        n2t_ref[:, rs] = n2.T
        dm = jnp.where(token_mask(m, length), cot_ref[rs, :], jnp.zeros((), BF16))
        dm_ref[rs, :] = dm
        dmt_ref[:, rs] = dm.T

    mlp_ref[...] = jnp.zeros_like(mlp_ref)
    dn2_ref[...] = jnp.zeros_like(dn2_ref)

    @pl.loop(0, tp)
    def _(z):
        mlp_chunk(t, d, f, wm_ref.at[z], gm_ref.at[z], n2_ref, dm_ref, n2t_ref, dmt_ref, act_ref, dgu_ref, mlp_ref, dn2_ref, False)

    gg_ref[...] = jnp.zeros_like(gg_ref)

    @pl.loop(0, t // BLK)
    def _(m):
        rs = rows_of(m)
        hid = hid_ref[rs, :]
        ok = token_mask(m, length)
        lo_ref[rs, :] = (hid + jnp.where(ok, mlp_ref[rs, :], 0.0)).astype(BF16)
        unit, r = norm_rows(hid, None)
        dn2 = dn2_ref[rs, :]
        gg_ref[...] += jnp.sum(dn2 * unit, axis=0, keepdims=True)
        e2 = dn2 * gains_ref[1:2, :]
        dh = cot_ref[rs, :].astype(F32) + r * (e2 - unit * jnp.mean(e2 * unit, axis=-1, keepdims=True))
        dh_ref[rs, :] = dh
        da_ref[rs, :] = jnp.where(ok, dh, 0.0).astype(BF16)


def k3(len_ref, x_ref, gains_ref, wa_ref, cos_ref, sin_ref, q_ref, k_ref, v_ref, ctxt_ref, lse_ref, dh_ref, da_ref,
       gx_ref, ga_ref, gg_ref, n1_ref, n1t_ref, dat_ref, dctx_ref, dlt_ref, dqkv_ref, dk_acc, dv_acc, dn1_ref, stages=(1, 1, 1)):
    t, d = x_ref.shape
    length = len_ref[0]

    if stages[0]:
        dat_ref[...] = da_ref[...].T

        @pl.loop(0, d // 256)
        def _(j):
            rs = pl.ds(pl.multiple_of(j * 256, 256), 256)
            cols = pl.ds(pl.multiple_of(3 * d + j * 256, 256), 256)
            ga_ref[:, cols] = nt(dat_ref[...], ctxt_ref[rs, :]).astype(BF16)
            dctx = nn(da_ref[...], wa_ref[:, cols]).astype(BF16)
            dctx_ref[:, rs] = dctx
            prod = dctx.T.astype(F32) * ctxt_ref[rs, :].astype(F32)
            for h in range(4):
                dlt_ref[pl.ds(j * 4 + h, 1), :] = jnp.sum(prod[h * HEAD : (h + 1) * HEAD], axis=0, keepdims=True)

    if stages[1]:
        bias = key_bias(t, length)

        @pl.loop(0, d // 128)
        def _(p):
            cols = pl.ds(pl.multiple_of(p * 128, 128), 128)
            qp, kp, vp, gp = q_ref[:, cols], k_ref[:, cols], v_ref[:, cols], dctx_ref[:, cols]
            dk_acc[...] = jnp.zeros_like(dk_acc)
            dv_acc[...] = jnp.zeros_like(dv_acc)
            ops = [score_operands(h, qp, kp, bias) for h in range(2)]
            for i in range(t // BLK):
                n = (i + 1) * BLK
                qs = slice(i * BLK, n)
                dq = None
                for h in range(2):
                    q_m, k_m, q_s, k_s = ops[h]
                    g_m = jnp.where(head_lane(h), gp[qs], jnp.zeros((), BF16))
                    s = mask_diag(nt(k_s[:n], q_s[qs]), i)
                    pr = jnp.exp2(s * C2 - lse_ref[pl.ds(p * 2 + h, 1), qs])
                    dp = nt(vp[:n], g_m)
                    ds = (pr * (dp - dlt_ref[pl.ds(p * 2 + h, 1), qs])).astype(BF16)
                    dv_acc[:n, :] += nn(pr.astype(BF16), g_m)
                    dk_acc[:n, :] += nn(ds, q_m[qs])
                    part = tn(ds, k_m[:n])
                    dq = part if dq is None else dq + part
                dq = dq * (HEAD**-0.5)
                dqkv_ref[qs, cols] = (dq * cos_ref[qs, :] - turned(dq) * sin_ref[qs, :]).astype(BF16)
            dk = dk_acc[...] * (HEAD**-0.5)
            dqkv_ref[:, pl.ds(pl.multiple_of(d + p * 128, 128), 128)] = (dk * cos_ref[...] - turned(dk) * sin_ref[...]).astype(BF16)
            dqkv_ref[:, pl.ds(pl.multiple_of(2 * d + p * 128, 128), 128)] = dv_acc[...].astype(BF16)

    if stages[2]:
        @pl.loop(0, t // BLK)
        def _(m):
            rs = rows_of(m)
            unit, _ = norm_rows(x_ref[rs, :].astype(F32), None)
            n1t_ref[:, rs] = (unit * gains_ref[0:1, :]).astype(BF16).T

        @pl.loop(0, 3 * d // 256)
        def _(j):
            cols = pl.ds(pl.multiple_of(j * 256, 256), 256)
            ga_ref[:, cols] = nn(n1t_ref[...], dqkv_ref[:, cols]).astype(BF16)

        @pl.loop(0, d // 256)
        def _(j):
            cols = pl.ds(pl.multiple_of(j * 256, 256), 256)
            dn1_ref[:, cols] = nt(dqkv_ref[...], wa_ref[cols, : 3 * d])

        gg_ref[...] = jnp.zeros_like(gg_ref)

        @pl.loop(0, t // BLK)
        def _(m):
            rs = rows_of(m)
            unit, r = norm_rows(x_ref[rs, :].astype(F32), None)
            dn1 = dn1_ref[rs, :]
            gg_ref[...] += jnp.sum(dn1 * unit, axis=0, keepdims=True)
            e1 = dn1 * gains_ref[0:1, :]
            gx_ref[rs, :] = (dh_ref[rs, :] + r * (e1 - unit * jnp.mean(e1 * unit, axis=-1, keepdims=True))).astype(BF16)


def rope_np(t):
    half = HEAD // 2
    freqs = np.float32(10000.0) ** (np.float32(-2.0) * np.arange(half, dtype=np.float32) / np.float32(HEAD))
    ang = np.arange(t, dtype=np.float32)[:, None] * freqs[None, :].astype(np.float32)
    c, s = np.cos(ang), np.sin(ang)
    return np.concatenate([c, c, c, c], 1).astype(np.float32), np.concatenate([-s, s, -s, s], 1).astype(np.float32)


VM = pl.BlockSpec(memory_space=pltpu.VMEM)
SM = pl.BlockSpec(memory_space=pltpu.SMEM)


def call(kernel, ins, outs, scratch):
    return pl.pallas_call(
        kernel,
        out_shape=[jax.ShapeDtypeStruct(s, dt) for s, dt in outs],
        in_specs=[SM] + [VM] * (len(ins) - 1),
        out_specs=[VM] * len(outs),
        scratch_shapes=[pltpu.VMEM(s, dt) for s, dt in scratch],
        compiler_params=pltpu.CompilerParams(vmem_limit_bytes=60 * 2**20),
    )(*ins)


def one_sequence(length, x, cot, gains, wa, wm, cosine, sine):
    t, d = x.shape
    f = wm.shape[2] // 3
    heads = -(-d // HEAD // 8) * 8
    td, dt = ((t, d), BF16), ((d, t), BF16)
    q, k, v, ctxt, lse, hid = call(
        k1, (length, x, gains, wa, cosine, sine), (td, td, td, dt, ((heads, t), F32), ((t, d), F32)), (td,)
    )
    lo, dh, da, gm, gg2 = call(
        k2,
        (length, cot, gains, hid, wm),
        (td, ((t, d), F32), td, (wm.shape, BF16), ((1, d), F32)),
        (td, td, dt, dt, ((t, f), BF16), ((t, 2 * f), BF16), ((t, d), F32), ((t, d), F32)),
    )
    gx, ga, gg1 = call(
        k3,
        (length, x, gains, wa, cosine, sine, q, k, v, ctxt, lse, dh, da),
        (td, ((d, 4 * d), BF16), ((1, d), F32)),
        (td, dt, dt, td, ((heads, t), F32), ((t, 3 * d), BF16), ((t, 128), F32), ((t, 128), F32), ((t, d), F32)),
    )
    return lo, gx, ga, gm, jnp.concatenate([gg1, gg2])


def pack_weights(w_qkv, w_out, w_gate_up, w_down):
    attn = jnp.stack([w_qkv[0], w_qkv[1], w_qkv[2], w_out.T], axis=1)
    mlp = jnp.concatenate([w_gate_up[0], w_gate_up[1], w_down.T], axis=1)
    return attn, mlp


def unpack_grads(g_attn, g_mlp, fw):
    g_qkv = jnp.transpose(g_attn[:, :3], (1, 0, 2))
    g_gate_up = jnp.stack([g_mlp[:, i * fw : (i + 1) * fw] for i in range(2)])
    return g_qkv, g_attn[:, 3].T, g_gate_up, g_mlp[:, 2 * fw :].T


def to_sequences(local):
    return lax.all_to_all(local, "tp", split_axis=0, concat_axis=1, tiled=True)


def to_positions(whole):
    return lax.all_to_all(whole, "tp", split_axis=1, concat_axis=0, tiled=True)


def body(tokens, lengths, w_qkv, w_out, w_gate_up, w_down, gains, cotangent):
    tp = lax.axis_size("tp")
    batch, part, d = tokens.shape
    n, t = batch // tp, part * tp
    fw = w_gate_up.shape[2]
    cosine, sine = map(jnp.asarray, rope_np(t))
    full_gains = lax.all_gather(gains, ("dp", "tp"), axis=1, tiled=True)
    full_gains = jnp.pad(full_gains, ((0, 6), (0, 0)))
    attn, mlp = pack_weights(w_qkv, w_out, w_gate_up, w_down)
    x16 = to_sequences(tokens)
    wa = lax.all_gather(attn, "tp", axis=2, tiled=True).reshape(attn.shape[0], 4 * d)
    wa = lax.all_gather(wa, "dp", axis=0, tiled=True)
    wm = lax.all_gather(lax.all_gather(mlp, "tp", axis=0), "dp", axis=1, tiled=True)
    cot16 = to_sequences(cotangent)
    own = lax.dynamic_slice_in_dim(lengths, lax.axis_index("tp") * n, n)
    los, gxs, ga, gm, gg = [], [], 0.0, 0.0, 0.0
    for i in range(n):
        lo, gx, a, m, g = one_sequence(own[i : i + 1], x16[i], cot16[i], full_gains, wa, wm, cosine, sine)
        los.append(lo)
        gxs.append(gx)
        ga, gm, gg = ga + a.astype(F32), gm + m.astype(F32), gg + g
    out = to_positions(jnp.stack(los))
    gx = to_positions(jnp.stack(gxs)).astype(F32)
    s_mlp = lax.psum_scatter(lax.psum_scatter(gm, "dp", scatter_dimension=1, tiled=True), "tp", scatter_dimension=0)
    s_attn = lax.psum_scatter(ga, "dp", scatter_dimension=0, tiled=True)
    s_attn = lax.psum_scatter(s_attn.reshape(-1, 4, d), "tp", scatter_dimension=2, tiled=True)
    s_gains = lax.psum_scatter(gg, ("dp", "tp"), scatter_dimension=1, tiled=True)
    return (out, gx) + unpack_grads(s_attn, s_mlp, fw) + (s_gains,)


def solution(mesh):
    act = P("dp", "tp", None)
    cols, rows, gain = P(None, "dp", "tp"), P("tp", "dp"), P(None, ("dp", "tp"))
    return jax.shard_map(
        body,
        mesh=mesh,
        in_specs=(act, P("dp"), cols, rows, cols, rows, gain, act),
        out_specs=(act, act, cols, rows, cols, rows, gain),
        check_vma=False,
    )
```

```python
import functools

import numpy as np
import jax
import jax.numpy as jnp
from jax import lax
from jax.experimental import pallas as pl
from jax.experimental.pallas import tpu as pltpu
from jax.sharding import PartitionSpec as P

F32 = jnp.float32
BF16 = jnp.bfloat16
HEAD = 64
EPS = 1e-6
LOG2E = 1.4426950408889634
C2 = LOG2E * HEAD**-0.5
NEG = -1e30
BLK = 256


def dg(a, b, ca, cb):
    return lax.dot_general(a, b, (((ca,), (cb,)), ((), ())), preferred_element_type=F32)


def nn(a, b):
    return dg(a, b, 1, 0)


def nt(a, b):
    return dg(a, b, 1, 1)


def tn(a, b):
    return dg(a, b, 0, 0)


def rows_of(m):
    return pl.ds(pl.multiple_of(m * BLK, BLK), BLK)


def wa_cols(wa_ref, cols):
    part = wa_ref[:, :, :, cols]
    return part.reshape(-1, part.shape[-1])


def half_lane():
    return lax.broadcasted_iota(jnp.int32, (1, 128), 1) % HEAD < HEAD // 2


def head_lane(h):
    lane = lax.broadcasted_iota(jnp.int32, (1, 128), 1)
    return lane < HEAD if h == 0 else lane >= HEAD


def turned(v):
    return jnp.where(half_lane(), pltpu.roll(v, 96, 1), pltpu.roll(v, 32, 1))


def norm_rows(x, gain):
    r = lax.rsqrt(jnp.mean(x * x, axis=-1, keepdims=True) + EPS)
    return x * r, r


def norm_stage(t, x_ref, gains_ref, n1_ref):
    @pl.loop(0, t // BLK)
    def _(m):
        rs = rows_of(m)
        unit, _ = norm_rows(x_ref[rs, :].astype(F32), None)
        n1_ref[rs, :] = (unit * gains_ref[0:1, :]).astype(BF16)


def qkv_stage(t, d, n1_ref, wa_ref, cos_ref, sin_ref, q_ref, k_ref, v_ref):
    for c, out in enumerate((q_ref, k_ref, v_ref)):

        @pl.loop(0, d // 256)
        def _(j, c=c, out=out):
            cols = pl.ds(pl.multiple_of(c * d + j * 256, 256), 256)
            raw = nn(n1_ref[...], wa_cols(wa_ref, cols))
            for s in range(2):
                part = raw[:, s * 128 : (s + 1) * 128]
                if c < 2:
                    part = part * cos_ref[...] + turned(part) * sin_ref[...]
                out[:, pl.ds(pl.multiple_of(j * 256 + s * 128, 128), 128)] = part.astype(BF16)


def key_bias(t, length):
    pos = lax.broadcasted_iota(jnp.int32, (t, 1), 0)
    return jnp.where(pos < length, 0.0, NEG).astype(BF16)


def causal_block():
    key = lax.broadcasted_iota(jnp.int32, (BLK, BLK), 0)
    query = lax.broadcasted_iota(jnp.int32, (BLK, BLK), 1)
    return key <= query


def score_operands(h, qp, kp, bias):
    mine = head_lane(h)
    lane = lax.broadcasted_iota(jnp.int32, (1, 128), 1)
    spare = lane == (HEAD if h == 0 else 0)
    zero = jnp.zeros((), BF16)
    q_m = jnp.where(mine, qp, zero)
    k_m = jnp.where(mine, kp, zero)
    q_s = jnp.where(spare, jnp.ones((), BF16), q_m)
    k_s = jnp.where(spare, bias, k_m)
    return q_m, k_m, q_s, k_s


def mask_diag(s, i):
    if i == 0:
        return jnp.where(causal_block(), s, NEG)
    return jnp.concatenate([s[: i * BLK], jnp.where(causal_block(), s[i * BLK :], NEG)], axis=0)


def attend_stage(t, d, length, q_ref, k_ref, v_ref, ctxt_ref, lse_ref, first, last):
    bias = key_bias(t, length)

    @pl.loop(first, last)
    def _(p):
        cols = pl.ds(pl.multiple_of(p * 128, 128), 128)
        qp, kp, vp = q_ref[:, cols], k_ref[:, cols], v_ref[:, cols]
        for h in range(2):
            _, _, q_s, k_s = score_operands(h, qp, kp, bias)
            for i in range(t // BLK):
                n = (i + 1) * BLK
                s = mask_diag(nt(k_s[:n], q_s[i * BLK : n]), i)
                top = jnp.max(s, axis=0, keepdims=True)
                e = jnp.exp2((s - top) * C2)
                total = jnp.sum(e, axis=0, keepdims=True)
                o = tn(vp[:n], e.astype(BF16))[h * HEAD : (h + 1) * HEAD] / total
                ctxt_ref[pl.ds(pl.multiple_of(p * 128 + h * HEAD, HEAD), HEAD), i * BLK : n] = o.astype(BF16)
                lse_ref[pl.ds(p * 2 + h, 1), i * BLK : n] = top * C2 + jnp.log2(total)


def out_stage(t, d, length, x_ref, wa_ref, ctxt_ref, hid_ref):
    out = dg(ctxt_ref[...], wa_cols(wa_ref, slice(3 * d, 4 * d)), 0, 1)
    pos = lax.broadcasted_iota(jnp.int32, (t, 1), 0)
    hid_ref[...] = x_ref[...].astype(F32) + jnp.where(pos < length, out, 0.0)


def k1_alone(len_ref, x_ref, gains_ref, wa_ref, cos_ref, sin_ref, q_ref, k_ref, v_ref, ctxt_ref, lse_ref, hid_ref, n1_ref):
    t, d = x_ref.shape
    length = len_ref[0]
    norm_stage(t, x_ref, gains_ref, n1_ref)
    qkv_stage(t, d, n1_ref, wa_ref, cos_ref, sin_ref, q_ref, k_ref, v_ref)
    attend_stage(t, d, length, q_ref, k_ref, v_ref, ctxt_ref, lse_ref, 0, d // 128)
    out_stage(t, d, length, x_ref, wa_ref, ctxt_ref, hid_ref)


def token_mask(m, length):
    pos = m * BLK + lax.broadcasted_iota(jnp.int32, (BLK, 1), 0)
    return pos < length


def mlp_chunk(t, d, f, wm, gm, n2_ref, dm_ref, n2t_ref, dmt_ref, act_ref, dgu_ref, mlp_ref, dn2_ref):
    w = 256

    def wcols(lo, hi):
        return wm[:, :, :, lo:hi].reshape(d, hi - lo)

    def put(lo, hi, value):
        gm[:, :, :, lo:hi] = value.astype(BF16).reshape(gm.shape[:3] + (hi - lo,))

    for j in range(f // w):
        lo, hi = j * w, (j + 1) * w
        gate = nn(n2_ref[...], wcols(lo, hi))
        up = nn(n2_ref[...], wcols(f + lo, f + hi))
        d_act = nn(dm_ref[...], wcols(2 * f + lo, 2 * f + hi))
        s = 1.0 / (1.0 + jnp.exp2(gate * (-LOG2E)))
        sw = gate * s
        act_ref[:, lo:hi] = (sw * up).astype(BF16)
        dgu_ref[:, lo:hi] = (d_act * up * (s + sw * (1.0 - s))).astype(BF16)
        dgu_ref[:, f + lo : f + hi] = (d_act * sw).astype(BF16)

    mlp_ref[...] += nt(act_ref[...], wcols(2 * f, 3 * f))
    dn2_ref[...] += nt(dgu_ref[...], wcols(0, 2 * f))
    for j in range(2 * f // w):
        put(j * w, (j + 1) * w, nn(n2t_ref[...], dgu_ref[:, j * w : (j + 1) * w]))
    for j in range(f // w):
        put(2 * f + j * w, 2 * f + (j + 1) * w, nn(dmt_ref[...], act_ref[:, j * w : (j + 1) * w]))


def k2(len_ref, cot_ref, gains_ref, hid_ref, wm_ref, lo_ref, dh_ref, da_ref, gm_ref, gg_ref,
       n2_ref, dm_ref, n2t_ref, dmt_ref, act_ref, dgu_ref, mlp_ref, dn2_ref):
    t, d = cot_ref.shape
    tp, f = wm_ref.shape[0], wm_ref.shape[-1] // 3
    length = len_ref[0]

    @pl.loop(0, t // BLK)
    def _(m):
        rs = rows_of(m)
        unit, _ = norm_rows(hid_ref[rs, :], None)
        n2 = (unit * gains_ref[1:2, :]).astype(BF16)
        n2_ref[rs, :] = n2
        n2t_ref[:, rs] = n2.T
        dm = jnp.where(token_mask(m, length), cot_ref[rs, :], jnp.zeros((), BF16))
        dm_ref[rs, :] = dm
        dmt_ref[:, rs] = dm.T

    mlp_ref[...] = jnp.zeros_like(mlp_ref)
    dn2_ref[...] = jnp.zeros_like(dn2_ref)

    @pl.loop(0, tp)
    def _(z):
        mlp_chunk(t, d, f, wm_ref.at[z], gm_ref.at[z], n2_ref, dm_ref, n2t_ref, dmt_ref, act_ref, dgu_ref, mlp_ref, dn2_ref)

    gg_ref[...] = jnp.zeros_like(gg_ref)

    @pl.loop(0, t // BLK)
    def _(m):
        rs = rows_of(m)
        hid = hid_ref[rs, :]
        ok = token_mask(m, length)
        lo_ref[rs, :] = (hid + jnp.where(ok, mlp_ref[rs, :], 0.0)).astype(BF16)
        unit, r = norm_rows(hid, None)
        dn2 = dn2_ref[rs, :]
        gg_ref[...] += jnp.sum(dn2 * unit, axis=0, keepdims=True)
        e2 = dn2 * gains_ref[1:2, :]
        dh = cot_ref[rs, :].astype(F32) + r * (e2 - unit * jnp.mean(e2 * unit, axis=-1, keepdims=True))
        dh_ref[rs, :] = dh
        da_ref[rs, :] = jnp.where(ok, dh, 0.0).astype(BF16)


def k3(len_ref, x_ref, gains_ref, wa_ref, cos_ref, sin_ref, q_ref, k_ref, v_ref, ctxt_ref, lse_ref, dh_ref, da_ref,
       gx_ref, ga_ref, gg_ref, n1_ref, n1t_ref, dat_ref, dctx_ref, dlt_ref, dqkv_ref, dk_acc, dv_acc, dn1_ref):
    t, d = x_ref.shape
    length = len_ref[0]

    dat_ref[...] = da_ref[...].T

    @pl.loop(0, d // 256)
    def _(j):
        rs = pl.ds(pl.multiple_of(j * 256, 256), 256)
        cols = pl.ds(pl.multiple_of(3 * d + j * 256, 256), 256)
        ga_ref[:, :, :, cols] = nt(dat_ref[...], ctxt_ref[rs, :]).astype(BF16).reshape(ga_ref.shape[:3] + (256,))
        dctx = nn(da_ref[...], wa_cols(wa_ref, cols)).astype(BF16)
        dctx_ref[:, rs] = dctx
        prod = dctx.T.astype(F32) * ctxt_ref[rs, :].astype(F32)
        for h in range(4):
            dlt_ref[pl.ds(j * 4 + h, 1), :] = jnp.sum(prod[h * HEAD : (h + 1) * HEAD], axis=0, keepdims=True)

    bias = key_bias(t, length)

    @pl.loop(0, d // 128)
    def _(p):
        cols = pl.ds(pl.multiple_of(p * 128, 128), 128)
        qp, kp, vp, gp = q_ref[:, cols], k_ref[:, cols], v_ref[:, cols], dctx_ref[:, cols]
        dk_acc[...] = jnp.zeros_like(dk_acc)
        dv_acc[...] = jnp.zeros_like(dv_acc)
        ops = [score_operands(h, qp, kp, bias) for h in range(2)]
        for i in range(t // BLK):
            n = (i + 1) * BLK
            qs = slice(i * BLK, n)
            dq = None
            for h in range(2):
                q_m, k_m, q_s, k_s = ops[h]
                g_m = jnp.where(head_lane(h), gp[qs], jnp.zeros((), BF16))
                s = mask_diag(nt(k_s[:n], q_s[qs]), i)
                pr = jnp.exp2(s * C2 - lse_ref[pl.ds(p * 2 + h, 1), qs])
                dp = nt(vp[:n], g_m)
                ds = (pr * (dp - dlt_ref[pl.ds(p * 2 + h, 1), qs])).astype(BF16)
                dv_acc[:n, :] += nn(pr.astype(BF16), g_m)
                dk_acc[:n, :] += nn(ds, q_m[qs])
                part = tn(ds, k_m[:n])
                dq = part if dq is None else dq + part
            dq = dq * (HEAD**-0.5)
            dqkv_ref[qs, cols] = (dq * cos_ref[qs, :] - turned(dq) * sin_ref[qs, :]).astype(BF16)
        dk = dk_acc[...] * (HEAD**-0.5)
        dqkv_ref[:, pl.ds(pl.multiple_of(d + p * 128, 128), 128)] = (dk * cos_ref[...] - turned(dk) * sin_ref[...]).astype(BF16)
        dqkv_ref[:, pl.ds(pl.multiple_of(2 * d + p * 128, 128), 128)] = dv_acc[...].astype(BF16)

    @pl.loop(0, t // BLK)
    def _(m):
        rs = rows_of(m)
        unit, _ = norm_rows(x_ref[rs, :].astype(F32), None)
        n1t_ref[:, rs] = (unit * gains_ref[0:1, :]).astype(BF16).T

    @pl.loop(0, 3 * d // 256)
    def _(j):
        cols = pl.ds(pl.multiple_of(j * 256, 256), 256)
        ga_ref[:, :, :, cols] = nn(n1t_ref[...], dqkv_ref[:, cols]).astype(BF16).reshape(ga_ref.shape[:3] + (256,))

    dn1_ref[...] = nt(dqkv_ref[...], wa_cols(wa_ref, slice(0, 3 * d)))

    gg_ref[...] = jnp.zeros_like(gg_ref)

    @pl.loop(0, t // BLK)
    def _(m):
        rs = rows_of(m)
        unit, r = norm_rows(x_ref[rs, :].astype(F32), None)
        dn1 = dn1_ref[rs, :]
        gg_ref[...] += jnp.sum(dn1 * unit, axis=0, keepdims=True)
        e1 = dn1 * gains_ref[0:1, :]
        gx_ref[rs, :] = (dh_ref[rs, :] + r * (e1 - unit * jnp.mean(e1 * unit, axis=-1, keepdims=True))).astype(BF16)


def rope_np(t):
    half = HEAD // 2
    freqs = np.float32(10000.0) ** (np.float32(-2.0) * np.arange(half, dtype=np.float32) / np.float32(HEAD))
    ang = np.arange(t, dtype=np.float32)[:, None] * freqs[None, :].astype(np.float32)
    c, s = np.cos(ang), np.sin(ang)
    return np.concatenate([c, c, c, c], 1).astype(np.float32), np.concatenate([-s, s, -s, s], 1).astype(np.float32)


MESH = pl.DeviceIdType.MESH
Z = 4


def flip(d, bit):
    return d + bit - 2 * bit * lax.rem(d // bit, 2)


class Net:
    def __init__(self, send, recv, local):
        self.d, self.z = lax.axis_index("dp"), lax.axis_index("tp")
        self.yx, self.c = self.d // 2, lax.rem(self.d, 2)
        self.x, self.y, self.core = ((flip(self.d, b), self.z) for b in (2, 4, 1))
        self.send, self.recv, self.local = send, recv, local
        self.copies, self.own = {}, {}

    def peer(self, r):
        return lax.rem(self.z + r, Z)

    def source(self, r):
        return lax.rem(self.z + Z - r, Z)

    def barrier(self):
        sem = pltpu.get_barrier_semaphore()
        for dev in (self.x, self.y, self.core) + tuple((self.d, self.peer(r)) for r in range(1, Z)):
            pl.semaphore_signal(sem, inc=1, device_id=dev, device_id_type=MESH)
        pl.semaphore_wait(sem, 6)

    def start(self, name, src, dst, dev):
        i = len(self.copies)
        copy = pltpu.make_async_remote_copy(
            src_ref=src, dst_ref=dst, send_sem=self.send.at[i], recv_sem=self.recv.at[i], device_id=dev, device_id_type=MESH
        )
        copy.start()
        self.copies[name] = copy

    def keep(self, name, src, dst):
        copy = pltpu.make_async_copy(src, dst, self.local.at[len(self.own)])
        copy.start()
        self.own[name] = copy

    def got(self, *names):
        for name in names:
            self.copies[name].wait_recv()

    def kept(self, name):
        self.own[name].wait()

    def finish(self):
        for copy in self.copies.values():
            copy.wait_send()


def spread(net, tag, own, slab, halves):
    net.start(tag + "x", own, slab(net.yx), net.x)
    net.start(tag + "y", own, slab(net.yx), net.y)


def relay(net, tag, slab, halves):
    kx, ky = flip(net.yx, 1), flip(net.yx, 2)
    net.got(tag + "x")
    net.start(tag + "l", slab(kx).at[:, halves[0]], slab(kx).at[:, halves[0]], net.y)
    net.got(tag + "y")
    net.start(tag + "r", slab(ky).at[:, halves[1]], slab(ky).at[:, halves[1]], net.x)


def all_sum(net, tag, own, boxes):
    for r in range(1, Z):
        net.start(f"{tag}z{r}", own, boxes.at[r - 1], (net.d, net.peer(r)))
    yield
    net.got(*(f"{tag}z{r}" for r in range(1, Z)))
    boxes[6] = own[...] + (boxes[0] + boxes[1] + boxes[2])
    net.start(tag + "x", boxes.at[6], boxes.at[3], net.x)
    yield
    net.got(tag + "x")
    boxes[7] = boxes[6] + boxes[3]
    net.start(tag + "y", boxes.at[7], boxes.at[4], net.y)
    yield
    net.got(tag + "y")
    boxes[8] = boxes[7] + boxes[4]
    net.start(tag + "c", boxes.at[8], boxes.at[5], net.core)
    yield
    net.got(tag + "c")
    boxes[9] = boxes[8] + boxes[5]
    yield


def lane_pairs(stage, hw):
    low = lax.broadcasted_iota(jnp.int32, (1, 128), 1) < HEAD
    parts = [[stage[z][:, c * 128 : (c + 1) * 128] for z in range(Z)] for c in range(4)]
    for j in range(Z // 2):
        for g in range(2):
            cols = slice(512 + g * 128, 640 + g * 128)
            a, b = stage[2 * j][:, cols].astype(F32), stage[2 * j + 1][:, cols].astype(F32)
            parts[2 * g].append(jnp.where(low, a, pltpu.roll(b, HEAD, 1)).astype(BF16))
            parts[2 * g + 1].append(jnp.where(low, pltpu.roll(a, HEAD, 1), b).astype(BF16))
    return parts


def k1(len_ref, tok_ref, cot_ref, was_ref, wms_ref, gs_ref, cos_ref, sin_ref,
       x_ref, cotw_ref, wa_ref, wm_ref, gains_ref, q_ref, k_ref, v_ref, ctxt_ref, lse_ref, hid_ref,
       n1_ref, stage_ref, boxes_ref, send, recv, local):
    t, d = x_ref.shape
    part = t // Z
    rows = wms_ref.shape[0]
    length = len_ref[0]
    net = Net(send, recv, local)
    z, yx, c = net.z, net.yx, net.c
    mine = pl.ds(pl.multiple_of(z * part, part), part)
    a_half = (slice(0, 2 * d), slice(2 * d, 4 * d))
    f3 = wms_ref.shape[1]
    m_half = (slice(0, f3 // 2), slice(f3 // 2, f3))
    a_slab = lambda k: wa_ref.at[k, c]
    m_slab = lambda w: lambda k: wm_ref.at[w, k, c]

    net.barrier()
    gains_steps = all_sum(net, "g", gs_ref, boxes_ref)
    next(gains_steps)
    for r in range(1, Z):
        net.start(f"az{r}", was_ref, stage_ref.at[z], (net.d, net.peer(r)))
    net.keep("a", was_ref, stage_ref.at[z])
    net.keep("m", wms_ref, wm_ref.at[z, yx, c])
    spread(net, "m0", wms_ref, m_slab(z), m_half)
    for r in range(1, Z):
        net.start(f"t{r}", tok_ref.at[net.peer(r)], x_ref.at[mine], (net.d, net.peer(r)))
    net.keep("t", tok_ref.at[z], x_ref.at[mine])
    next(gains_steps)

    net.got(*(f"az{r}" for r in range(1, Z)))
    net.kept("a")
    for i, heads in enumerate(lane_pairs(stage_ref, 4 * d // Z)):
        for j, value in enumerate(heads):
            wa_ref[yx, c, :, i * d + j * 128 : i * d + (j + 1) * 128] = value
    spread(net, "a", wa_ref.at[yx, c], a_slab, a_half)
    net.start("ac0", wa_ref.at[yx, c], wa_ref.at[yx, c], net.core)
    next(gains_steps)
    next(gains_steps)
    relay(net, "m0", m_slab(z), m_half)
    next(gains_steps)
    gains_ref[...] = boxes_ref[9]
    net.got(*(f"t{r}" for r in range(1, Z)))
    net.kept("t")
    for r in range(1, Z):
        net.start(f"mz{r}", wms_ref, wm_ref.at[z, yx, c], (net.d, net.peer(r)))
    norm_stage(t, x_ref, gains_ref, n1_ref)
    relay(net, "a", a_slab, a_half)
    net.start("ac1", wa_ref.at[flip(yx, 1), c], wa_ref.at[flip(yx, 1), c], net.core)
    net.start("ac2", wa_ref.at[flip(yx, 2), c], wa_ref.at[flip(yx, 2), c], net.core)
    net.got("al", "ar")
    kd = flip(flip(yx, 1), 2)
    net.start("ac3", wa_ref.at[kd, c], wa_ref.at[kd, c], net.core)
    net.got("m0l", "m0r")
    net.kept("m")
    net.start("m0c", wm_ref.at[z, :, c], wm_ref.at[z, :, c], net.core)
    net.got("ac0", "ac1", "ac2", "ac3")
    qkv_stage(t, d, n1_ref, wa_ref, cos_ref, sin_ref, q_ref, k_ref, v_ref)
    attend = functools.partial(attend_stage, t, d, length, q_ref, k_ref, v_ref, ctxt_ref, lse_ref)
    attend(0, 3)
    for r in range(1, Z):
        w = net.source(r)
        net.got(f"mz{r}")
        spread(net, f"m{r}", wm_ref.at[w, yx, c], m_slab(w), m_half)
    for r in range(1, Z):
        net.start(f"c{r}", cot_ref.at[net.peer(r)], cotw_ref.at[mine], (net.d, net.peer(r)))
    net.keep("c", cot_ref.at[z], cotw_ref.at[mine])
    attend(3, d // 128)
    out_stage(t, d, length, x_ref, wa_ref, ctxt_ref, hid_ref)
    for r in range(1, Z):
        relay(net, f"m{r}", m_slab(net.source(r)), m_half)
    for r in range(1, Z):
        w = net.source(r)
        net.got(f"m{r}l", f"m{r}r")
        net.start(f"m{r}c", wm_ref.at[w, :, c], wm_ref.at[w, :, c], net.core)
    net.got(*(f"m{r}c" for r in range(Z)), *(f"c{r}" for r in range(1, Z)))
    net.kept("c")
    net.finish()


VM = pl.BlockSpec(memory_space=pltpu.VMEM)
SM = pl.BlockSpec(memory_space=pltpu.SMEM)


def call(kernel, ins, outs, scratch):
    return pl.pallas_call(
        kernel,
        out_shape=[jax.ShapeDtypeStruct(s, dt) for s, dt in outs],
        in_specs=[SM] + [VM] * (len(ins) - 1),
        out_specs=[VM] * len(outs),
        scratch_shapes=[pltpu.VMEM(s, dt) for s, dt in scratch],
        compiler_params=pltpu.CompilerParams(vmem_limit_bytes=60 * 2**20),
    )(*ins)


def backward(length, x, cot, gains, wa, wm, cosine, sine, q, k, v, ctxt, lse, hid):
    t, d = x.shape
    f = wm.shape[-1] // 3
    heads = lse.shape[0]
    td, dt = ((t, d), BF16), ((d, t), BF16)
    lo, dh, da, gm, gg2 = call(
        k2,
        (length, cot, gains, hid, wm),
        (td, ((t, d), F32), td, (wm.shape, BF16), ((1, d), F32)),
        (td, td, dt, dt, ((t, f), BF16), ((t, 2 * f), BF16), ((t, d), F32), ((t, d), F32)),
    )
    gx, ga, gg1 = call(
        k3,
        (length, x, gains, wa, cosine, sine, q, k, v, ctxt, lse, dh, da),
        (td, (wa.shape, BF16), ((1, d), F32)),
        (td, dt, dt, td, ((heads, t), F32), ((t, 3 * d), BF16), ((t, 128), F32), ((t, 128), F32), ((t, d), F32)),
    )
    return lo, gx, ga, gm, jnp.concatenate([gg1, gg2])


def one_sequence(length, x, cot, gains, wa, wm, cosine, sine):
    t, d = x.shape
    heads = -(-d // HEAD // 8) * 8
    td, dt = ((t, d), BF16), ((d, t), BF16)
    kept = call(k1_alone, (length, x, gains, wa, cosine, sine), (td, td, td, dt, ((heads, t), F32), ((t, d), F32)), (td,))
    return backward(length, x, cot, gains, wa, wm, cosine, sine, *kept)


def pack_weights(w_qkv, w_out, w_gate_up, w_down):
    attn = jnp.stack([w_qkv[0], w_qkv[1], w_qkv[2], w_out.T], axis=1)
    mlp = jnp.concatenate([w_gate_up[0], w_gate_up[1], w_down.T], axis=1)
    return attn, mlp


def unpack_grads(g_attn, g_mlp, fw):
    g_qkv = jnp.transpose(g_attn[:, :3], (1, 0, 2))
    g_gate_up = jnp.stack([g_mlp[:, i * fw : (i + 1) * fw] for i in range(2)])
    return g_qkv, g_attn[:, 3].T, g_gate_up, g_mlp[:, 2 * fw :].T


def to_sequences(local):
    return lax.all_to_all(local, "tp", split_axis=0, concat_axis=1, tiled=True)


def to_positions(whole):
    return lax.all_to_all(whole, "tp", split_axis=1, concat_axis=0, tiled=True)


def fused_forward(length, tokens, cotangent, attn, mlp, gains, cosine, sine):
    batch, part, d = tokens.shape
    t, rows, hw = part * Z, attn.shape[0], attn.shape[2]
    heads = -(-d // HEAD // 8) * 8
    pairs = 2 * HEAD
    was = jnp.concatenate(
        [attn[:, :, :pairs].reshape(rows, 4 * pairs), attn[:, :, pairs:].reshape(rows, 4 * HEAD)], axis=1
    )
    spot = (lax.axis_index("dp") * Z + lax.axis_index("tp")) * gains.shape[1]
    gs = lax.dynamic_update_slice(jnp.zeros((8, d), F32), gains, (0, spot))
    f3 = mlp.shape[1]
    td, dt = ((t, d), BF16), ((d, t), BF16)
    outs = (
        td, td, ((4, 2, rows, 4 * d), BF16), ((Z, 4, 2, rows, f3), BF16), ((8, d), F32),
        td, td, td, dt, ((heads, t), F32), ((t, d), F32),
    )
    hbm = pl.BlockSpec(memory_space=pl.ANY)
    out_specs = [VM, hbm, VM, hbm] + [VM] * 7
    return pl.pallas_call(
        k1,
        out_shape=[jax.ShapeDtypeStruct(s, dt_) for s, dt_ in outs],
        in_specs=[SM, hbm, hbm, VM, hbm, VM, VM, VM],
        out_specs=out_specs,
        scratch_shapes=[
            pltpu.VMEM((t, d), BF16),
            pltpu.VMEM((Z, rows, d), BF16),
            pltpu.VMEM((10, 8, d), F32),
            pltpu.SemaphoreType.DMA((64,)),
            pltpu.SemaphoreType.DMA((64,)),
            pltpu.SemaphoreType.DMA((8,)),
        ],
        compiler_params=pltpu.CompilerParams(collective_id=0, has_side_effects=True, vmem_limit_bytes=60 * 2**20),
    )(length, tokens, cotangent, was, mlp, gs, cosine, sine)


def fits(mesh_dp, tokens, w_qkv, w_gate_up):
    tp = lax.axis_size("tp")
    rows, hw = w_qkv.shape[1:]
    return (
        mesh_dp == 8 and tp == Z and tokens.shape[0] == Z and hw == 3 * HEAD and rows % 16 == 0
        and w_gate_up.shape[2] % 256 == 0 and tokens.shape[1] % BLK == 0
    )


def body(tokens, lengths, w_qkv, w_out, w_gate_up, w_down, gains, cotangent):
    tp, dp = lax.axis_size("tp"), lax.axis_size("dp")
    batch, part, d = tokens.shape
    n, t = batch // tp, part * tp
    fw = w_gate_up.shape[2]
    cosine, sine = map(jnp.asarray, rope_np(t))
    attn, mlp = pack_weights(w_qkv, w_out, w_gate_up, w_down)
    own = lax.dynamic_slice_in_dim(lengths, lax.axis_index("tp") * n, n)
    if fits(dp, tokens, w_qkv, w_gate_up):
        x, cot, wa, wm, full_gains, *kept = fused_forward(own, tokens, cotangent, attn, mlp, gains, cosine, sine)
        lo, gx, ga, gm, gg = backward(own, x, cot, full_gains, wa, wm, cosine, sine, *kept)
        out, gx = to_positions(lo[None]), to_positions(gx[None]).astype(F32)
        ga, gm = ga.astype(F32).reshape(d, 4, d), gm.astype(F32).reshape(tp, d, 3 * fw)
        pairs = ga[:, :, : 2 * HEAD * Z].reshape(d, 4, Z, 2 * HEAD)
        third = ga[:, :, 2 * HEAD * Z :].reshape(d, 4, Z, HEAD)
        ga = jnp.concatenate([pairs, third], axis=3).reshape(d, 4, d)
    else:
        full_gains = lax.all_gather(gains, ("dp", "tp"), axis=1, tiled=True)
        full_gains = jnp.pad(full_gains, ((0, 6), (0, 0)))
        x16 = to_sequences(tokens)
        wa = lax.all_gather(attn, "tp", axis=2, tiled=True).reshape(attn.shape[0], 4 * d)
        wa = lax.all_gather(wa, "dp", axis=0, tiled=True).reshape(1, 1, d, 4 * d)
        wm = lax.all_gather(lax.all_gather(mlp, "tp", axis=0), "dp", axis=1, tiled=True).reshape(tp, 1, 1, d, 3 * fw)
        cot16 = to_sequences(cotangent)
        los, gxs, ga, gm, gg = [], [], 0.0, 0.0, 0.0
        for i in range(n):
            lo, gx, a, m, g = one_sequence(own[i : i + 1], x16[i], cot16[i], full_gains, wa, wm, cosine, sine)
            los.append(lo)
            gxs.append(gx)
            ga, gm, gg = ga + a.astype(F32), gm + m.astype(F32), gg + g
        out = to_positions(jnp.stack(los))
        gx = to_positions(jnp.stack(gxs)).astype(F32)
        ga, gm = ga.reshape(d, 4, d), gm.reshape(tp, d, 3 * fw)
    s_mlp = lax.psum_scatter(lax.psum_scatter(gm, "dp", scatter_dimension=1, tiled=True), "tp", scatter_dimension=0)
    s_attn = lax.psum_scatter(ga.reshape(d, 4 * d), "dp", scatter_dimension=0, tiled=True)
    s_attn = lax.psum_scatter(s_attn.reshape(-1, 4, d), "tp", scatter_dimension=2, tiled=True)
    s_gains = lax.psum_scatter(gg, ("dp", "tp"), scatter_dimension=1, tiled=True)
    return (out, gx) + unpack_grads(s_attn, s_mlp, fw) + (s_gains,)


def solution(mesh):
    act = P("dp", "tp", None)
    cols, rows, gain = P(None, "dp", "tp"), P("tp", "dp"), P(None, ("dp", "tp"))
    return jax.shard_map(
        body,
        mesh=mesh,
        in_specs=(act, P("dp"), cols, rows, cols, rows, gain, act),
        out_specs=(act, act, cols, rows, cols, rows, gain),
        check_vma=False,
    )
```

```python
import functools

import numpy as np
import jax
import jax.numpy as jnp
from jax import lax
from jax.experimental import pallas as pl
from jax.experimental.pallas import tpu as pltpu
from jax.sharding import PartitionSpec as P

F32 = jnp.float32
BF16 = jnp.bfloat16
HEAD = 64
EPS = 1e-6
LOG2E = 1.4426950408889634
C2 = LOG2E * HEAD**-0.5
NEG = -1e30
BLK = 256


def dg(a, b, ca, cb):
    return lax.dot_general(a, b, (((ca,), (cb,)), ((), ())), preferred_element_type=F32)


def nn(a, b):
    return dg(a, b, 1, 0)


def nt(a, b):
    return dg(a, b, 1, 1)


def tn(a, b):
    return dg(a, b, 0, 0)


def rows_of(m):
    return pl.ds(pl.multiple_of(m * BLK, BLK), BLK)


def wa_cols(wa_ref, cols):
    part = wa_ref[:, :, :, cols]
    return part.reshape(-1, part.shape[-1])


def half_lane():
    return lax.broadcasted_iota(jnp.int32, (1, 128), 1) % HEAD < HEAD // 2


def head_lane(h):
    lane = lax.broadcasted_iota(jnp.int32, (1, 128), 1)
    return lane < HEAD if h == 0 else lane >= HEAD


def turned(v):
    return jnp.where(half_lane(), pltpu.roll(v, 96, 1), pltpu.roll(v, 32, 1))


def norm_rows(x, gain):
    r = lax.rsqrt(jnp.mean(x * x, axis=-1, keepdims=True) + EPS)
    return x * r, r


def norm_stage(t, x_ref, gains_ref, n1_ref):
    @pl.loop(0, t // BLK)
    def _(m):
        rs = rows_of(m)
        unit, _ = norm_rows(x_ref[rs, :].astype(F32), None)
        n1_ref[rs, :] = (unit * gains_ref[0:1, :]).astype(BF16)


def qkv_stage(t, d, n1_ref, wa_ref, cos_ref, sin_ref, q_ref, k_ref, v_ref):
    for c, out in enumerate((q_ref, k_ref, v_ref)):

        @pl.loop(0, d // 256)
        def _(j, c=c, out=out):
            cols = pl.ds(pl.multiple_of(c * d + j * 256, 256), 256)
            raw = nn(n1_ref[...], wa_cols(wa_ref, cols))
            for s in range(2):
                part = raw[:, s * 128 : (s + 1) * 128]
                if c < 2:
                    part = part * cos_ref[...] + turned(part) * sin_ref[...]
                out[:, pl.ds(pl.multiple_of(j * 256 + s * 128, 128), 128)] = part.astype(BF16)


def key_bias(t, length):
    pos = lax.broadcasted_iota(jnp.int32, (t, 1), 0)
    return jnp.where(pos < length, 0.0, NEG).astype(BF16)


def causal_block():
    key = lax.broadcasted_iota(jnp.int32, (BLK, BLK), 0)
    query = lax.broadcasted_iota(jnp.int32, (BLK, BLK), 1)
    return key <= query


def score_operands(h, qp, kp, bias):
    mine = head_lane(h)
    lane = lax.broadcasted_iota(jnp.int32, (1, 128), 1)
    spare = lane == (HEAD if h == 0 else 0)
    zero = jnp.zeros((), BF16)
    q_m = jnp.where(mine, qp, zero)
    k_m = jnp.where(mine, kp, zero)
    q_s = jnp.where(spare, jnp.ones((), BF16), q_m)
    k_s = jnp.where(spare, bias, k_m)
    return q_m, k_m, q_s, k_s


def mask_diag(s, i):
    if i == 0:
        return jnp.where(causal_block(), s, NEG)
    return jnp.concatenate([s[: i * BLK], jnp.where(causal_block(), s[i * BLK :], NEG)], axis=0)


def attend_stage(t, d, length, q_ref, k_ref, v_ref, ctxt_ref, lse_ref, first, last):
    bias = key_bias(t, length)

    @pl.loop(first, last)
    def _(p):
        cols = pl.ds(pl.multiple_of(p * 128, 128), 128)
        qp, kp, vp = q_ref[:, cols], k_ref[:, cols], v_ref[:, cols]
        for h in range(2):
            _, _, q_s, k_s = score_operands(h, qp, kp, bias)
            for i in range(t // BLK):
                n = (i + 1) * BLK
                s = mask_diag(nt(k_s[:n], q_s[i * BLK : n]), i)
                top = jnp.max(s, axis=0, keepdims=True)
                e = jnp.exp2((s - top) * C2)
                total = jnp.sum(e, axis=0, keepdims=True)
                o = tn(vp[:n], e.astype(BF16))[h * HEAD : (h + 1) * HEAD] / total
                ctxt_ref[pl.ds(pl.multiple_of(p * 128 + h * HEAD, HEAD), HEAD), i * BLK : n] = o.astype(BF16)
                lse_ref[pl.ds(p * 2 + h, 1), i * BLK : n] = top * C2 + jnp.log2(total)


def out_stage(t, d, length, x_ref, wa_ref, ctxt_ref, hid_ref):
    out = dg(ctxt_ref[...], wa_cols(wa_ref, slice(3 * d, 4 * d)), 0, 1)
    pos = lax.broadcasted_iota(jnp.int32, (t, 1), 0)
    hid_ref[...] = x_ref[...].astype(F32) + jnp.where(pos < length, out, 0.0)


def k1_alone(len_ref, x_ref, gains_ref, wa_ref, cos_ref, sin_ref, q_ref, k_ref, v_ref, ctxt_ref, lse_ref, hid_ref, n1_ref):
    t, d = x_ref.shape
    length = len_ref[0]
    norm_stage(t, x_ref, gains_ref, n1_ref)
    qkv_stage(t, d, n1_ref, wa_ref, cos_ref, sin_ref, q_ref, k_ref, v_ref)
    attend_stage(t, d, length, q_ref, k_ref, v_ref, ctxt_ref, lse_ref, 0, d // 128)
    out_stage(t, d, length, x_ref, wa_ref, ctxt_ref, hid_ref)


def token_mask(m, length):
    pos = m * BLK + lax.broadcasted_iota(jnp.int32, (BLK, 1), 0)
    return pos < length


def chunk_cols(wm, d, lo, hi):
    return wm[..., lo:hi].reshape(d, hi - lo)


def mlp_front(f, d, wm, n2_ref, dm_ref, wide):
    w = 256
    for j in range(f // w):
        lo, hi = j * w, (j + 1) * w
        gate = nn(n2_ref[...], chunk_cols(wm, d, lo, hi))
        up = nn(n2_ref[...], chunk_cols(wm, d, f + lo, f + hi))
        d_act = nn(dm_ref[...], chunk_cols(wm, d, 2 * f + lo, 2 * f + hi))
        s = 1.0 / (1.0 + jnp.exp2(gate * (-LOG2E)))
        sw = gate * s
        wide[:, 2 * f + lo : 2 * f + hi] = (sw * up).astype(BF16)
        wide[:, lo:hi] = (d_act * up * (s + sw * (1.0 - s))).astype(BF16)
        wide[:, f + lo : f + hi] = (d_act * sw).astype(BF16)


def mlp_back(f, d, wm, n2t_ref, dmt_ref, wide, mlp_ref, dn2_ref):
    w = 256
    mlp_ref[...] += nt(wide[:, 2 * f : 3 * f], chunk_cols(wm, d, 2 * f, 3 * f))
    dn2_ref[...] += nt(wide[:, : 2 * f], chunk_cols(wm, d, 0, 2 * f))
    for j in range(3 * f // w):
        cols = slice(j * w, (j + 1) * w)
        left = n2t_ref if j * w < 2 * f else dmt_ref
        wm[..., cols] = nn(left[...], wide[:, cols]).astype(BF16).reshape(wm.shape[:-1] + (w,))


def k2(len_ref, cot_ref, gains_ref, hid_ref, wm_ref, lo_ref, dh_ref, da_ref, gm_ref, gg_ref,
       n2_ref, dm_ref, n2t_ref, dmt_ref, wide, mlp_ref, dn2_ref):
    t, d = cot_ref.shape
    tp, f = wm_ref.shape[0], wm_ref.shape[-1] // 3
    length = len_ref[0]

    @pl.loop(0, t // BLK)
    def _(m):
        rs = rows_of(m)
        unit, _ = norm_rows(hid_ref[rs, :], None)
        n2 = (unit * gains_ref[1:2, :]).astype(BF16)
        n2_ref[rs, :] = n2
        n2t_ref[:, rs] = n2.T
        dm = jnp.where(token_mask(m, length), cot_ref[rs, :], jnp.zeros((), BF16))
        dm_ref[rs, :] = dm
        dmt_ref[:, rs] = dm.T

    mlp_ref[...] = jnp.zeros_like(mlp_ref)
    dn2_ref[...] = jnp.zeros_like(dn2_ref)

    @pl.loop(0, tp)
    def _(z):
        gm_ref[z] = wm_ref[z]
        mlp_front(f, d, gm_ref.at[z], n2_ref, dm_ref, wide)
        mlp_back(f, d, gm_ref.at[z], n2t_ref, dmt_ref, wide, mlp_ref, dn2_ref)

    gg_ref[...] = jnp.zeros_like(gg_ref)

    @pl.loop(0, t // BLK)
    def _(m):
        rs = rows_of(m)
        hid = hid_ref[rs, :]
        ok = token_mask(m, length)
        lo_ref[rs, :] = (hid + jnp.where(ok, mlp_ref[rs, :], 0.0)).astype(BF16)
        unit, r = norm_rows(hid, None)
        dn2 = dn2_ref[rs, :]
        gg_ref[...] += jnp.sum(dn2 * unit, axis=0, keepdims=True)
        e2 = dn2 * gains_ref[1:2, :]
        dh = cot_ref[rs, :].astype(F32) + r * (e2 - unit * jnp.mean(e2 * unit, axis=-1, keepdims=True))
        dh_ref[rs, :] = dh
        da_ref[rs, :] = jnp.where(ok, dh, 0.0).astype(BF16)


def attend_back(t, d, length, q_ref, k_ref, v_ref, dctx_ref, lse_ref, dlt_ref, cos_ref, sin_ref, dqkv_ref, dk_acc, dv_acc, first, last):
    bias = key_bias(t, length)

    @pl.loop(first, last)
    def _(p):
        cols = pl.ds(pl.multiple_of(p * 128, 128), 128)
        qp, kp, vp, gp = q_ref[:, cols], k_ref[:, cols], v_ref[:, cols], dctx_ref[:, cols]
        dk_acc[...] = jnp.zeros_like(dk_acc)
        dv_acc[...] = jnp.zeros_like(dv_acc)
        ops = [score_operands(h, qp, kp, bias) for h in range(2)]
        for i in range(t // BLK):
            n = (i + 1) * BLK
            qs = slice(i * BLK, n)
            dq = None
            for h in range(2):
                q_m, k_m, q_s, k_s = ops[h]
                g_m = jnp.where(head_lane(h), gp[qs], jnp.zeros((), BF16))
                s = mask_diag(nt(k_s[:n], q_s[qs]), i)
                pr = jnp.exp2(s * C2 - lse_ref[pl.ds(p * 2 + h, 1), qs])
                dp = nt(vp[:n], g_m)
                ds = (pr * (dp - dlt_ref[pl.ds(p * 2 + h, 1), qs])).astype(BF16)
                dv_acc[:n, :] += nn(pr.astype(BF16), g_m)
                dk_acc[:n, :] += nn(ds, q_m[qs])
                part = tn(ds, k_m[:n])
                dq = part if dq is None else dq + part
            dq = dq * (HEAD**-0.5)
            dqkv_ref[qs, cols] = (dq * cos_ref[qs, :] - turned(dq) * sin_ref[qs, :]).astype(BF16)
        dk = dk_acc[...] * (HEAD**-0.5)
        dqkv_ref[:, pl.ds(pl.multiple_of(d + p * 128, 128), 128)] = (dk * cos_ref[...] - turned(dk) * sin_ref[...]).astype(BF16)
        dqkv_ref[:, pl.ds(pl.multiple_of(2 * d + p * 128, 128), 128)] = dv_acc[...].astype(BF16)


def k3(len_ref, x_ref, gains_ref, wa_ref, cos_ref, sin_ref, q_ref, k_ref, v_ref, ctxt_ref, lse_ref, dh_ref, da_ref,
       gx_ref, ga_ref, gg_ref, n1_ref, n1t_ref, dat_ref, dctx_ref, dlt_ref, dqkv_ref, dk_acc, dv_acc, dn1_ref):
    t, d = x_ref.shape
    length = len_ref[0]

    dat_ref[...] = da_ref[...].T

    @pl.loop(0, d // 256)
    def _(j):
        rs = pl.ds(pl.multiple_of(j * 256, 256), 256)
        cols = pl.ds(pl.multiple_of(3 * d + j * 256, 256), 256)
        ga_ref[:, :, :, cols] = nt(dat_ref[...], ctxt_ref[rs, :]).astype(BF16).reshape(ga_ref.shape[:3] + (256,))
        dctx = nn(da_ref[...], wa_cols(wa_ref, cols)).astype(BF16)
        dctx_ref[:, rs] = dctx
        prod = dctx.T.astype(F32) * ctxt_ref[rs, :].astype(F32)
        for h in range(4):
            dlt_ref[pl.ds(j * 4 + h, 1), :] = jnp.sum(prod[h * HEAD : (h + 1) * HEAD], axis=0, keepdims=True)

    attend_back(t, d, length, q_ref, k_ref, v_ref, dctx_ref, lse_ref, dlt_ref, cos_ref, sin_ref, dqkv_ref, dk_acc, dv_acc, 0, d // 128)

    @pl.loop(0, t // BLK)
    def _(m):
        rs = rows_of(m)
        unit, _ = norm_rows(x_ref[rs, :].astype(F32), None)
        n1t_ref[:, rs] = (unit * gains_ref[0:1, :]).astype(BF16).T

    @pl.loop(0, 3 * d // 256)
    def _(j):
        cols = pl.ds(pl.multiple_of(j * 256, 256), 256)
        ga_ref[:, :, :, cols] = nn(n1t_ref[...], dqkv_ref[:, cols]).astype(BF16).reshape(ga_ref.shape[:3] + (256,))

    dn1_ref[...] = nt(dqkv_ref[...], wa_cols(wa_ref, slice(0, 3 * d)))

    gg_ref[...] = jnp.zeros_like(gg_ref)

    @pl.loop(0, t // BLK)
    def _(m):
        rs = rows_of(m)
        unit, r = norm_rows(x_ref[rs, :].astype(F32), None)
        dn1 = dn1_ref[rs, :]
        gg_ref[...] += jnp.sum(dn1 * unit, axis=0, keepdims=True)
        e1 = dn1 * gains_ref[0:1, :]
        gx_ref[rs, :] = (dh_ref[rs, :] + r * (e1 - unit * jnp.mean(e1 * unit, axis=-1, keepdims=True))).astype(BF16)


def rope_np(t):
    half = HEAD // 2
    freqs = np.float32(10000.0) ** (np.float32(-2.0) * np.arange(half, dtype=np.float32) / np.float32(HEAD))
    ang = np.arange(t, dtype=np.float32)[:, None] * freqs[None, :].astype(np.float32)
    c, s = np.cos(ang), np.sin(ang)
    return np.concatenate([c, c, c, c], 1).astype(np.float32), np.concatenate([-s, s, -s, s], 1).astype(np.float32)


MESH = pl.DeviceIdType.MESH
Z = 4


def flip(d, bit):
    return d + bit - 2 * bit * lax.rem(d // bit, 2)


class Net:
    def __init__(self, send, recv, local):
        self.d, self.z = lax.axis_index("dp"), lax.axis_index("tp")
        self.yx, self.c = self.d // 2, lax.rem(self.d, 2)
        self.x, self.y, self.core = ((flip(self.d, b), self.z) for b in (2, 4, 1))
        self.send, self.recv, self.local = send, recv, local
        self.copies, self.own = {}, {}

    def peer(self, r):
        return lax.rem(self.z + r, Z)

    def source(self, r):
        return lax.rem(self.z + Z - r, Z)

    def barrier(self):
        sem = pltpu.get_barrier_semaphore()
        for dev in (self.x, self.y, self.core) + tuple((self.d, self.peer(r)) for r in range(1, Z)):
            pl.semaphore_signal(sem, inc=1, device_id=dev, device_id_type=MESH)
        pl.semaphore_wait(sem, 6)

    def make(self, i, src, dst, dev):
        return pltpu.make_async_remote_copy(
            src_ref=src, dst_ref=dst, send_sem=self.send.at[i], recv_sem=self.recv.at[i], device_id=dev, device_id_type=MESH
        )

    def start(self, name, src, dst, dev):
        copy = self.make(len(self.copies), src, dst, dev)
        copy.start()
        self.copies[name] = copy

    def keep(self, name, src, dst):
        copy = pltpu.make_async_copy(src, dst, self.local.at[len(self.own)])
        copy.start()
        self.own[name] = copy

    def got(self, *names):
        for name in names:
            self.copies[name].wait_recv()

    def kept(self, name):
        self.own[name].wait()

    def finish(self):
        for copy in self.copies.values():
            copy.wait_send()


def spread(net, tag, own, slab, halves):
    net.start(tag + "x", own, slab(net.yx), net.x)
    net.start(tag + "y", own, slab(net.yx), net.y)


def relay(net, tag, slab, halves):
    kx, ky = flip(net.yx, 1), flip(net.yx, 2)
    net.got(tag + "x")
    net.start(tag + "l", slab(kx).at[:, halves[0]], slab(kx).at[:, halves[0]], net.y)
    net.got(tag + "y")
    net.start(tag + "r", slab(ky).at[:, halves[1]], slab(ky).at[:, halves[1]], net.x)


def all_sum(net, tag, own, boxes):
    for r in range(1, Z):
        net.start(f"{tag}z{r}", own, boxes.at[r - 1], (net.d, net.peer(r)))
    yield
    net.got(*(f"{tag}z{r}" for r in range(1, Z)))
    boxes[6] = own[...] + (boxes[0] + boxes[1] + boxes[2])
    net.start(tag + "x", boxes.at[6], boxes.at[3], net.x)
    yield
    net.got(tag + "x")
    boxes[7] = boxes[6] + boxes[3]
    net.start(tag + "y", boxes.at[7], boxes.at[4], net.y)
    yield
    net.got(tag + "y")
    boxes[8] = boxes[7] + boxes[4]
    net.start(tag + "c", boxes.at[8], boxes.at[5], net.core)
    yield
    net.got(tag + "c")
    boxes[9] = boxes[8] + boxes[5]
    yield


def lane_pairs(stage, hw):
    low = lax.broadcasted_iota(jnp.int32, (1, 128), 1) < HEAD
    parts = [[stage[z][:, c * 128 : (c + 1) * 128] for z in range(Z)] for c in range(4)]
    for j in range(Z // 2):
        for g in range(2):
            cols = slice(512 + g * 128, 640 + g * 128)
            a, b = stage[2 * j][:, cols].astype(F32), stage[2 * j + 1][:, cols].astype(F32)
            parts[2 * g].append(jnp.where(low, a, pltpu.roll(b, HEAD, 1)).astype(BF16))
            parts[2 * g + 1].append(jnp.where(low, pltpu.roll(a, HEAD, 1), b).astype(BF16))
    return parts


def k1(len_ref, tok_ref, cot_ref, was_ref, wms_ref, gs_ref, cos_ref, sin_ref,
       x_h, cotw_ref, wa_h, wm_ref, gains_ref, q_h, k_h, v_h, ctxt_h, lse_h, hid_h,
       x_ref, wa_ref, q_ref, k_ref, v_ref, ctxt_ref, lse_ref, hid_ref,
       n1_ref, stage_ref, boxes_ref, send, recv, local):
    t, d = x_ref.shape
    part = t // Z
    rows = wms_ref.shape[0]
    length = len_ref[0]
    net = Net(send, recv, local)
    z, yx, c = net.z, net.yx, net.c
    mine = pl.ds(pl.multiple_of(z * part, part), part)
    a_half = (slice(0, 2 * d), slice(2 * d, 4 * d))
    f3 = wms_ref.shape[1]
    m_half = (slice(0, f3 // 2), slice(f3 // 2, f3))
    a_slab = lambda k: wa_ref.at[k, c]
    m_slab = lambda w: lambda k: wm_ref.at[w, k, c]

    net.barrier()
    gains_steps = all_sum(net, "g", gs_ref, boxes_ref)
    next(gains_steps)
    for r in range(1, Z):
        net.start(f"az{r}", was_ref, stage_ref.at[z], (net.d, net.peer(r)))
    net.keep("a", was_ref, stage_ref.at[z])
    net.keep("m", wms_ref, wm_ref.at[z, yx, c])
    spread(net, "m0", wms_ref, m_slab(z), m_half)
    for r in range(1, Z):
        net.start(f"t{r}", tok_ref.at[net.peer(r)], x_ref.at[mine], (net.d, net.peer(r)))
    net.keep("t", tok_ref.at[z], x_ref.at[mine])
    next(gains_steps)

    net.got(*(f"az{r}" for r in range(1, Z)))
    net.kept("a")
    for i, heads in enumerate(lane_pairs(stage_ref, 4 * d // Z)):
        for j, value in enumerate(heads):
            wa_ref[yx, c, :, i * d + j * 128 : i * d + (j + 1) * 128] = value
    spread(net, "a", wa_ref.at[yx, c], a_slab, a_half)
    net.start("ac0", wa_ref.at[yx, c], wa_ref.at[yx, c], net.core)
    next(gains_steps)
    next(gains_steps)
    relay(net, "m0", m_slab(z), m_half)
    next(gains_steps)
    gains_ref[...] = boxes_ref[9]
    net.got(*(f"t{r}" for r in range(1, Z)))
    net.kept("t")
    for r in range(1, Z):
        net.start(f"mz{r}", wms_ref, wm_ref.at[z, yx, c], (net.d, net.peer(r)))
    norm_stage(t, x_ref, gains_ref, n1_ref)
    relay(net, "a", a_slab, a_half)
    net.start("ac1", wa_ref.at[flip(yx, 1), c], wa_ref.at[flip(yx, 1), c], net.core)
    net.start("ac2", wa_ref.at[flip(yx, 2), c], wa_ref.at[flip(yx, 2), c], net.core)
    net.got("al", "ar")
    kd = flip(flip(yx, 1), 2)
    net.start("ac3", wa_ref.at[kd, c], wa_ref.at[kd, c], net.core)
    net.got("m0l", "m0r")
    net.kept("m")
    net.start("m0c", wm_ref.at[z, :, c], wm_ref.at[z, :, c], net.core)
    net.got("ac0", "ac1", "ac2", "ac3")
    net.keep("x", x_ref, x_h)
    net.keep("wa", wa_ref, wa_h)
    qkv_stage(t, d, n1_ref, wa_ref, cos_ref, sin_ref, q_ref, k_ref, v_ref)
    attend = functools.partial(attend_stage, t, d, length, q_ref, k_ref, v_ref, ctxt_ref, lse_ref)
    for name, src, dst in (("q", q_ref, q_h), ("k", k_ref, k_h), ("v", v_ref, v_h)):
        net.keep(name, src, dst)
    attend(0, 3)
    for r in range(1, Z):
        w = net.source(r)
        net.got(f"mz{r}")
        spread(net, f"m{r}", wm_ref.at[w, yx, c], m_slab(w), m_half)
    for r in range(1, Z):
        net.start(f"c{r}", cot_ref.at[net.peer(r)], cotw_ref.at[mine], (net.d, net.peer(r)))
    net.keep("c", cot_ref.at[z], cotw_ref.at[mine])
    attend(3, d // 128)
    net.keep("ctxt", ctxt_ref, ctxt_h)
    net.keep("lse", lse_ref, lse_h)
    out_stage(t, d, length, x_ref, wa_ref, ctxt_ref, hid_ref)
    net.keep("hid", hid_ref, hid_h)
    for r in range(1, Z):
        relay(net, f"m{r}", m_slab(net.source(r)), m_half)
    for r in range(1, Z):
        w = net.source(r)
        net.got(f"m{r}l", f"m{r}r")
        net.start(f"m{r}c", wm_ref.at[w, :, c], wm_ref.at[w, :, c], net.core)
    net.got(*(f"m{r}c" for r in range(Z)), *(f"c{r}" for r in range(1, Z)))
    for name in ("c", "x", "wa", "q", "k", "v", "ctxt", "lse", "hid"):
        net.kept(name)
    net.finish()


class Reduce:
    def __init__(self, net, base, data, use, credit, rc, r1x, r1y, r2l, r2r):
        self.net, self.base, self.data, self.use, self.credit = net, base, data, use, credit
        self.rc, self.r1x, self.r1y, self.r2l, self.r2r = rc, r1x, r1y, r2l, r2r
        self.x, self.y = lax.rem(net.yx, 2), net.yx // 2
        half = data.shape[-1] // 2
        self.lo, self.hi = slice(0, half), slice(half, 2 * half)

    def slot(self, i):
        return self.rc.at[lax.rem(self.use(i), 2), :, :, :, 0 : self.data.shape[-1]]

    def copies0(self, g, i):
        return [self.net.make(self.base + i, self.data.at[g, :, :, 1 - self.net.c], self.slot(i), self.net.core)]

    def copies1(self, g, i):
        net, c = self.net, self.net.c
        return [
            net.make(self.base + 4 + i, self.data.at[g, :, 1 - self.x, c, :, self.lo], self.r1x.at[i], net.x),
            net.make(self.base + 8 + i, self.data.at[g, 1 - self.y, :, c, :, self.hi], self.r1y.at[i], net.y),
        ]

    def copies2(self, g, i):
        net, c = self.net, self.net.c
        return [
            net.make(self.base + 12 + i, self.data.at[g, 1 - self.y, self.x, c, :, self.lo], self.r2l.at[i], net.y),
            net.make(self.base + 16 + i, self.data.at[g, self.y, 1 - self.x, c, :, self.hi], self.r2r.at[i], net.x),
        ]

    def add(self, at, value):
        self.data[at] = (self.data[at].astype(F32) + value.astype(F32)).astype(BF16)

    def p0(self, g, i):
        @pl.when(self.use(i) >= 2)
        def _():
            pl.semaphore_wait(self.credit, 1)

        for copy in self.copies0(g, i):
            copy.start()

    def p1(self, g, i):
        for copy in self.copies0(g, i):
            copy.wait_recv()
        for y in range(2):
            for x in range(2):
                self.add((g, y, x, self.net.c), self.slot(i)[y, x])

        @pl.when(self.use(i) < 6)
        def _():
            pl.semaphore_signal(self.credit, inc=1, device_id=self.net.core, device_id_type=MESH)

        for copy in self.copies1(g, i):
            copy.start()

    def p2(self, g, i):
        for copy in self.copies1(g, i):
            copy.wait_recv()
        for k in range(2):
            self.add((g, k, self.x, self.net.c, slice(None), self.lo), self.r1x[i, k])
            self.add((g, self.y, k, self.net.c, slice(None), self.hi), self.r1y[i, k])
        for copy in self.copies2(g, i):
            copy.start()

    def p3(self, g, i):
        for copy in self.copies2(g, i):
            copy.wait_recv()
        self.add((g, self.y, self.x, self.net.c, slice(None), self.lo), self.r2l[i])
        self.add((g, self.y, self.x, self.net.c, slice(None), self.hi), self.r2r[i])

    def own(self, g):
        return self.data.at[g, self.y, self.x, self.net.c]

    def sent(self, g, i):
        for copy in self.copies0(g, i) + self.copies1(g, i) + self.copies2(g, i):
            copy.wait_send()


def packed_heads(own):
    low = lax.broadcasted_iota(jnp.int32, (1, 128), 1) < HEAD
    for z in range(Z):
        s, u = z % 2, z // 2
        first = [own(u)[:, c * 256 + s * 128 : c * 256 + s * 128 + 128] for c in range(3)]
        first.append(own(3)[:, z * 128 : z * 128 + 128])
        third = [own(2)[:, c * 256 + u * 128 : c * 256 + u * 128 + 128].astype(F32) for c in range(3)]
        third.append(own(3)[:, 512 + u * 128 : 512 + u * 128 + 128].astype(F32))
        for a, b in ((third[0], third[1]), (third[2], third[3])):
            both = jnp.where(low, a, pltpu.roll(b, HEAD, 1)) if s == 0 else jnp.where(low, pltpu.roll(a, HEAD, 1), b)
            first.append(both.astype(BF16))
        yield z, first


def kb(len_ref, gains_ref, x_h, cot_h, cos_h, sin_h, wa_h, wm_h, q_h, k_h, v_h, ctxt_h, lse_h, hid_h,
       lo_out, gx_out, grads_out, gg_ref,
       x_ref, cot_ref, cos_ref, sin_ref, wa_ref, gm_ref, ctxt_ref, lse_ref, hid_ref,
       b1, b2, t1, t2, wide, f1, f2, dlt_ref, gsum_ref, boxes_ref,
       mc, mx, my, ml, mr, mz, ga_ref, ax, ay, al, ar, az, pack_ref,
       send, recv, local, credit):
    t, d = x_ref.shape
    part = t // Z
    f = gm_ref.shape[-1] // 3
    length = len_ref[0]
    net = Net(send, recv, local)
    z = net.z
    net.barrier()
    net.keep("hid", hid_h, hid_ref)
    net.keep("cot", cot_h, cot_ref)

    def chunk(i):
        return lax.rem(z + 1 + i, Z)

    def chunk_load(i):
        return pltpu.make_async_copy(wm_h.at[chunk(i)], gm_ref.at[chunk(i)], local.at[16 + i])

    for i in range(Z):
        chunk_load(i).start()
    late = dict(wa=(wa_h, wa_ref), ctxt=(ctxt_h, ctxt_ref), x=(x_h, x_ref),
                lse=(lse_h, lse_ref), cos=(cos_h, cos_ref), sin=(sin_h, sin_ref))
    for name, (src, dst) in late.items():
        net.keep(name, src, dst)
    mred = Reduce(net, 32, gm_ref, lambda i: i, credit, mc, mx, my, ml, mr)
    ared = Reduce(net, 52, ga_ref, lambda i: 4 + lax.rem(i + 1, 4), credit, mc, ax, ay, al, ar)

    def mz_copy(i):
        return net.make(72 + i, mred.own(chunk(i)), mz.at[i], (net.d, chunk(i)))

    net.kept("hid")
    net.kept("cot")

    n2_ref, dm_ref, n2t_ref, dmt_ref = b1, b2, t1, t2

    @pl.loop(0, t // BLK)
    def _(m):
        rs = rows_of(m)
        unit, _ = norm_rows(hid_ref[rs, :], None)
        n2 = (unit * gains_ref[1:2, :]).astype(BF16)
        n2_ref[rs, :] = n2
        n2t_ref[:, rs] = n2.T
        dm = jnp.where(token_mask(m, length), cot_ref[rs, :], jnp.zeros((), BF16))
        dm_ref[rs, :] = dm
        dmt_ref[:, rs] = dm.T

    f1[...] = jnp.zeros_like(f1)
    f2[...] = jnp.zeros_like(f2)

    @pl.loop(0, Z)
    def _(i):
        w = chunk(i)
        chunk_load(i).wait()
        gm = gm_ref.at[w]
        mlp_front(f, d, gm, n2_ref, dm_ref, wide)

        @pl.when(i >= 3)
        def _():
            mred.p3(chunk(i - 3), i - 3)
            mz_copy(i - 3).start()

        @pl.when(i >= 2)
        def _():
            mred.p2(chunk(i - 2), i - 2)

        @pl.when(i >= 1)
        def _():
            mred.p1(chunk(i - 1), i - 1)

        mlp_back(f, d, gm, n2t_ref, dmt_ref, wide, f1, f2)
        mred.p0(w, i)

    q_ref, k_ref, v_ref = (wide.at[:, c * d : (c + 1) * d] for c in range(3))
    for name, src, dst in (("q", q_h, q_ref), ("k", k_h, k_ref), ("v", v_h, v_ref)):
        net.keep(name, src, dst)
    gsum_ref[...] = jnp.zeros_like(gsum_ref)
    dh_ref, da_ref, lo_ref = hid_ref, b1, b2
    for j in range(Z):
        m = chunk(j)
        rs = rows_of(m)
        hid = hid_ref[rs, :]
        ok = token_mask(m, length)
        lo_ref[rs, :] = (hid + jnp.where(ok, f1[rs, :], 0.0)).astype(BF16)
        if j < Z - 1:
            net.start(f"lo{j}", lo_ref.at[rs], lo_out.at[z], (net.d, m))
        else:
            net.keep("lo", lo_ref.at[rs], lo_out.at[z])
        unit, r = norm_rows(hid, None)
        dn2 = f2[rs, :]
        gsum_ref[1:2, :] += jnp.sum(dn2 * unit, axis=0, keepdims=True)
        e2 = dn2 * gains_ref[1:2, :]
        dh = cot_ref[rs, :].astype(F32) + r * (e2 - unit * jnp.mean(e2 * unit, axis=-1, keepdims=True))
        dh_ref[rs, :] = dh
        da_ref[rs, :] = jnp.where(ok, dh, 0.0).astype(BF16)

    mred.p3(chunk(1), 1)
    mz_copy(1).start()
    mred.p2(chunk(2), 2)
    mred.p1(chunk(3), 3)
    for name in late:
        net.kept(name)
    dat_ref, n1t_ref, dctx_ref = t1, t2, cot_ref
    dat_ref[...] = da_ref[...].T
    shape = ga_ref.shape[1:5]

    @pl.loop(0, d // 256)
    def _(j):
        rs = pl.ds(pl.multiple_of(j * 256, 256), 256)
        cols = pl.ds(pl.multiple_of(3 * d + j * 256, 256), 256)
        ga_ref[3, :, :, :, :, rs] = nt(dat_ref[...], ctxt_ref[rs, :]).astype(BF16).reshape(shape + (256,))
        dctx = nn(da_ref[...], wa_cols(wa_ref, cols)).astype(BF16)
        dctx_ref[:, rs] = dctx
        prod = dctx.T.astype(F32) * ctxt_ref[rs, :].astype(F32)
        for h in range(4):
            dlt_ref[pl.ds(j * 4 + h, 1), :] = jnp.sum(prod[h * HEAD : (h + 1) * HEAD], axis=0, keepdims=True)

    ared.p0(3, 3)

    @pl.loop(0, t // BLK)
    def _(m):
        rs = rows_of(m)
        unit, _ = norm_rows(x_ref[rs, :].astype(F32), None)
        n1t_ref[:, rs] = (unit * gains_ref[0:1, :]).astype(BF16).T

    mred.p3(chunk(2), 2)
    mz_copy(2).start()
    mred.p2(chunk(3), 3)
    ared.p1(3, 3)
    for name in ("q", "k", "v"):
        net.kept(name)
    dk_acc, dv_acc = f2.at[:, 0:128], f2.at[:, 128:256]

    @pl.loop(0, 3)
    def _(g):
        attend_back(t, d, length, q_ref, k_ref, v_ref, dctx_ref, lse_ref, dlt_ref, cos_ref, sin_ref, wide, dk_acc, dv_acc, 2 * g, 2 * g + 2)
        for c in range(3):
            cols = pl.ds(pl.multiple_of(c * d + g * 256, 256), 256)
            ga_ref[g, :, :, :, :, c * 256 : (c + 1) * 256] = nn(n1t_ref[...], wide[:, cols]).astype(BF16).reshape(shape + (256,))
        ared.p0(g, g)

        @pl.when(g == 0)
        def _():
            mred.p3(chunk(3), 3)
            ared.p2(3, 3)

        @pl.when(g == 1)
        def _():
            ared.p3(3, 3)
            ared.p1(0, 0)

        @pl.when(g == 2)
        def _():
            ared.p2(0, 0)
            ared.p1(1, 1)

    gx_ref = b1
    for j in range(Z):
        m = chunk(j)
        rs = rows_of(m)
        dn1 = nt(wide[rs, :], wa_cols(wa_ref, slice(0, 3 * d)))
        unit, r = norm_rows(x_ref[rs, :].astype(F32), None)
        gsum_ref[0:1, :] += jnp.sum(dn1 * unit, axis=0, keepdims=True)
        e1 = dn1 * gains_ref[0:1, :]
        gx_ref[rs, :] = (dh_ref[rs, :] + r * (e1 - unit * jnp.mean(e1 * unit, axis=-1, keepdims=True))).astype(BF16)
        if j < Z - 1:
            net.start(f"gx{j}", gx_ref.at[rs], gx_out.at[z], (net.d, m))
        else:
            net.keep("gx", gx_ref.at[rs], gx_out.at[z])
    steps = all_sum(net, "g", gsum_ref, boxes_ref)
    next(steps)
    ared.p1(2, 2)
    ared.p2(1, 1)
    ared.p3(0, 0)
    next(steps)
    ared.p2(2, 2)
    ared.p3(1, 1)
    next(steps)
    ared.p3(2, 2)
    for w, values in packed_heads(lambda g: ared.own(g)[...]):
        for j, value in enumerate(values):
            pack_ref[w, :, j * 128 : (j + 1) * 128] = value
    for r in range(1, Z):
        net.start(f"az{r}", pack_ref.at[net.peer(r)], az.at[r - 1], (net.d, net.peer(r)))
    next(steps)
    next(steps)
    gg_ref[...] = boxes_ref[9]
    total = mred.own(z)[...].astype(F32)
    for i in range(Z - 1):
        mz_copy(i).wait_recv()
        total = total + mz[i].astype(F32)
    rows, half = total.shape[0], total.shape[1] // 2
    f1[0:rows, :] = total[:, :half]
    f1[rows : 2 * rows, :] = total[:, half:]
    net.got(*(f"az{r}" for r in range(1, Z)))
    total = pack_ref[z].astype(F32)
    for i in range(Z - 1):
        total = total + az[i].astype(F32)
    f1[2 * rows : 3 * rows, :] = total
    net.keep("grads", f1.at[0 : 3 * rows], grads_out)
    net.got(*(f"{n}{j}" for n in ("lo", "gx") for j in range(Z - 1)))
    net.kept("lo")
    net.kept("gx")
    net.kept("grads")
    for i in range(Z):
        mred.sent(chunk(i), i)
        ared.sent(i, i)
        if i < Z - 1:
            mz_copy(i).wait_send()
    net.finish()


VM = pl.BlockSpec(memory_space=pltpu.VMEM)
SM = pl.BlockSpec(memory_space=pltpu.SMEM)


def call(kernel, ins, outs, scratch):
    return pl.pallas_call(
        kernel,
        out_shape=[jax.ShapeDtypeStruct(s, dt) for s, dt in outs],
        in_specs=[SM] + [VM] * (len(ins) - 1),
        out_specs=[VM] * len(outs),
        scratch_shapes=[pltpu.VMEM(s, dt) for s, dt in scratch],
        compiler_params=pltpu.CompilerParams(vmem_limit_bytes=60 * 2**20),
    )(*ins)


def backward(length, x, cot, gains, wa, wm, cosine, sine, q, k, v, ctxt, lse, hid):
    t, d = x.shape
    f = wm.shape[-1] // 3
    heads = lse.shape[0]
    td, dt = ((t, d), BF16), ((d, t), BF16)
    lo, dh, da, gm, gg2 = call(
        k2,
        (length, cot, gains, hid, wm),
        (td, ((t, d), F32), td, (wm.shape, BF16), ((1, d), F32)),
        (td, td, dt, dt, ((t, 3 * f), BF16), ((t, d), F32), ((t, d), F32)),
    )
    gx, ga, gg1 = call(
        k3,
        (length, x, gains, wa, cosine, sine, q, k, v, ctxt, lse, dh, da),
        (td, (wa.shape, BF16), ((1, d), F32)),
        (td, dt, dt, td, ((heads, t), F32), ((t, 3 * d), BF16), ((t, 128), F32), ((t, 128), F32), ((t, d), F32)),
    )
    return lo, gx, ga, gm, jnp.concatenate([gg1, gg2])


def one_sequence(length, x, cot, gains, wa, wm, cosine, sine):
    t, d = x.shape
    heads = -(-d // HEAD // 8) * 8
    td, dt = ((t, d), BF16), ((d, t), BF16)
    kept = call(k1_alone, (length, x, gains, wa, cosine, sine), (td, td, td, dt, ((heads, t), F32), ((t, d), F32)), (td,))
    return backward(length, x, cot, gains, wa, wm, cosine, sine, *kept)


def pack_weights(w_qkv, w_out, w_gate_up, w_down):
    attn = jnp.stack([w_qkv[0], w_qkv[1], w_qkv[2], w_out.T], axis=1)
    mlp = jnp.concatenate([w_gate_up[0], w_gate_up[1], w_down.T], axis=1)
    return attn, mlp


def unpack_grads(g_attn, g_mlp, fw):
    g_qkv = jnp.transpose(g_attn[:, :3], (1, 0, 2))
    g_gate_up = jnp.stack([g_mlp[:, i * fw : (i + 1) * fw] for i in range(2)])
    return g_qkv, g_attn[:, 3].T, g_gate_up, g_mlp[:, 2 * fw :].T


def to_sequences(local):
    return lax.all_to_all(local, "tp", split_axis=0, concat_axis=1, tiled=True)


def to_positions(whole):
    return lax.all_to_all(whole, "tp", split_axis=1, concat_axis=0, tiled=True)


def fused_forward(length, tokens, cotangent, attn, mlp, gains, cosine, sine):
    batch, part, d = tokens.shape
    t, rows, hw = part * Z, attn.shape[0], attn.shape[2]
    heads = -(-d // HEAD // 8) * 8
    pairs = 2 * HEAD
    was = jnp.concatenate(
        [attn[:, :, :pairs].reshape(rows, 4 * pairs), attn[:, :, pairs:].reshape(rows, 4 * HEAD)], axis=1
    )
    spot = (lax.axis_index("dp") * Z + lax.axis_index("tp")) * gains.shape[1]
    gs = lax.dynamic_update_slice(jnp.zeros((8, d), F32), gains, (0, spot))
    f3 = mlp.shape[1]
    td, dt = ((t, d), BF16), ((d, t), BF16)
    outs = (
        td, td, ((4, 2, rows, 4 * d), BF16), ((Z, 4, 2, rows, f3), BF16), ((8, d), F32),
        td, td, td, dt, ((heads, t), F32), ((t, d), F32),
    )
    hbm = pl.BlockSpec(memory_space=pl.ANY)
    out_specs = [hbm] * 4 + [VM] + [hbm] * 6
    return pl.pallas_call(
        k1,
        out_shape=[jax.ShapeDtypeStruct(s, dt_) for s, dt_ in outs],
        in_specs=[SM, hbm, hbm, VM, hbm, VM, VM, VM],
        out_specs=out_specs,
        scratch_shapes=[
            pltpu.VMEM((t, d), BF16),
            pltpu.VMEM((4, 2, rows, 4 * d), BF16),
            pltpu.VMEM((t, d), BF16),
            pltpu.VMEM((t, d), BF16),
            pltpu.VMEM((t, d), BF16),
            pltpu.VMEM((d, t), BF16),
            pltpu.VMEM((heads, t), F32),
            pltpu.VMEM((t, d), F32),
            pltpu.VMEM((t, d), BF16),
            pltpu.VMEM((Z, rows, d), BF16),
            pltpu.VMEM((10, 8, d), F32),
            pltpu.SemaphoreType.DMA((64,)),
            pltpu.SemaphoreType.DMA((64,)),
            pltpu.SemaphoreType.DMA((16,)),
        ],
        compiler_params=pltpu.CompilerParams(collective_id=0, has_side_effects=True, vmem_limit_bytes=60 * 2**20),
    )(length, tokens, cotangent, was, mlp, gs, cosine, sine)


def fused_backward(length, gains, x, cot, wa, wm, q, k, v, ctxt, lse, hid, cosine, sine):
    t, d = x.shape
    rows, f3 = wm.shape[-2:]
    wm = wm.reshape(Z, 2, 2, 2, rows, f3)
    hbm = pl.BlockSpec(memory_space=pl.ANY)
    ins = (length, gains, x, cot, cosine, sine, wa, wm, q, k, v, ctxt, lse, hid)
    moved = ((Z, t // Z, d), BF16)
    outs = (moved, moved, ((3 * rows, d), F32), ((8, d), F32))
    td, dt, big = ((t, d), BF16), ((d, t), BF16), ((t, d), F32)

    def boxes(cols):
        pair = ((4, 2, rows, cols // 2), BF16)
        one = ((4, rows, cols // 2), BF16)
        return [pair, pair, one, one, ((Z - 1, rows, cols), BF16)]

    scratch = [td, td] + [(cosine.shape, F32)] * 2 + [(wa.shape, BF16), (wm.shape, BF16), dt, (lse.shape, F32), big]
    scratch += [td, td, dt, dt, ((t, 3 * d), BF16), big, big, (lse.shape, F32), ((8, d), F32), ((10, 8, d), F32)]
    scratch += [((2, 2, 2, rows, f3), BF16)] + boxes(f3) + [((4, 2, 2, 2, rows, d), BF16)] + boxes(d) + [((Z, rows, d), BF16)]
    return pl.pallas_call(
        kb,
        out_shape=[jax.ShapeDtypeStruct(s, dt_) for s, dt_ in outs],
        in_specs=[SM, VM] + [hbm] * 12,
        out_specs=[hbm, hbm, hbm, VM],
        scratch_shapes=[pltpu.VMEM(s, dt_) for s, dt_ in scratch]
        + [pltpu.SemaphoreType.DMA((80,)), pltpu.SemaphoreType.DMA((80,)), pltpu.SemaphoreType.DMA((24,)), pltpu.SemaphoreType.REGULAR],
        compiler_params=pltpu.CompilerParams(collective_id=1, has_side_effects=True, vmem_limit_bytes=60 * 2**20),
    )(*ins)


def fits(mesh_dp, tokens, w_qkv, w_gate_up):
    tp = lax.axis_size("tp")
    rows, hw = w_qkv.shape[1:]
    return (
        mesh_dp == 8 and tp == Z and tokens.shape[0] == Z and hw == 3 * HEAD and rows % 16 == 0
        and w_gate_up.shape[2] % 256 == 0 and tokens.shape[1] % BLK == 0
    )


def body(tokens, lengths, w_qkv, w_out, w_gate_up, w_down, gains, cotangent):
    tp, dp = lax.axis_size("tp"), lax.axis_size("dp")
    batch, part, d = tokens.shape
    n, t = batch // tp, part * tp
    fw = w_gate_up.shape[2]
    cosine, sine = map(jnp.asarray, rope_np(t))
    attn, mlp = pack_weights(w_qkv, w_out, w_gate_up, w_down)
    own = lax.dynamic_slice_in_dim(lengths, lax.axis_index("tp") * n, n)
    if fits(dp, tokens, w_qkv, w_gate_up):
        x, cot, wa, wm, full_gains, *kept = fused_forward(own, tokens, cotangent, attn, mlp, gains, cosine, sine)
        out, gx, grads, gg = fused_backward(own, full_gains, x, cot, wa, wm, *kept, cosine, sine)
        pairs, rows = 2 * HEAD, attn.shape[0]
        s_mlp = jnp.concatenate([grads[:rows], grads[rows : 2 * rows]], axis=1)
        s_attn = grads[2 * rows :]
        first, third = s_attn[:, : 4 * pairs], s_attn[:, 4 * pairs :]
        s_attn = jnp.concatenate([first.reshape(-1, 4, pairs), third.reshape(-1, 4, HEAD)], axis=2)
        spot = (lax.axis_index("dp") * tp + lax.axis_index("tp")) * gains.shape[1]
        s_gains = lax.dynamic_slice(gg, (0, spot), gains.shape)
        gx = gx.astype(F32)
    else:
        full_gains = lax.all_gather(gains, ("dp", "tp"), axis=1, tiled=True)
        full_gains = jnp.pad(full_gains, ((0, 6), (0, 0)))
        x16 = to_sequences(tokens)
        wa = lax.all_gather(attn, "tp", axis=2, tiled=True).reshape(attn.shape[0], 4 * d)
        wa = lax.all_gather(wa, "dp", axis=0, tiled=True).reshape(1, 1, d, 4 * d)
        wm = lax.all_gather(lax.all_gather(mlp, "tp", axis=0), "dp", axis=1, tiled=True).reshape(tp, 1, 1, d, 3 * fw)
        cot16 = to_sequences(cotangent)
        los, gxs, ga, gm, gg = [], [], 0.0, 0.0, 0.0
        for i in range(n):
            lo, gx, a, m, g = one_sequence(own[i : i + 1], x16[i], cot16[i], full_gains, wa, wm, cosine, sine)
            los.append(lo)
            gxs.append(gx)
            ga, gm, gg = ga + a.astype(F32), gm + m.astype(F32), gg + g
        out = to_positions(jnp.stack(los))
        gx = to_positions(jnp.stack(gxs)).astype(F32)
        ga, gm = ga.reshape(d, 4, d), gm.reshape(tp, d, 3 * fw)
        s_mlp = lax.psum_scatter(lax.psum_scatter(gm, "dp", scatter_dimension=1, tiled=True), "tp", scatter_dimension=0)
        s_attn = lax.psum_scatter(ga.reshape(d, 4 * d), "dp", scatter_dimension=0, tiled=True)
        s_attn = lax.psum_scatter(s_attn.reshape(-1, 4, d), "tp", scatter_dimension=2, tiled=True)
        s_gains = lax.psum_scatter(gg, ("dp", "tp"), scatter_dimension=1, tiled=True)
    return (out, gx) + unpack_grads(s_attn, s_mlp, fw) + (s_gains,)


def solution(mesh):
    act = P("dp", "tp", None)
    cols, rows, gain = P(None, "dp", "tp"), P("tp", "dp"), P(None, ("dp", "tp"))
    return jax.shard_map(
        body,
        mesh=mesh,
        in_specs=(act, P("dp"), cols, rows, cols, rows, gain, act),
        out_specs=(act, act, cols, rows, cols, rows, gain),
        check_vma=False,
    )
```

```python
import functools

import numpy as np
import jax
import jax.numpy as jnp
from jax import lax
from jax.experimental import pallas as pl
from jax.experimental.pallas import tpu as pltpu
from jax.sharding import PartitionSpec as P

F32 = jnp.float32
BF16 = jnp.bfloat16
HEAD = 64
EPS = 1e-6
LOG2E = 1.4426950408889634
C2 = LOG2E * HEAD**-0.5
NEG = -1e30
BLK = 256


def dg(a, b, ca, cb):
    return lax.dot_general(a, b, (((ca,), (cb,)), ((), ())), preferred_element_type=F32)


def nn(a, b):
    return dg(a, b, 1, 0)


def nt(a, b):
    return dg(a, b, 1, 1)


def tn(a, b):
    return dg(a, b, 0, 0)


def rows_of(m):
    return pl.ds(pl.multiple_of(m * BLK, BLK), BLK)


def wa_cols(wa_ref, cols):
    part = wa_ref[:, :, :, cols]
    return part.reshape(-1, part.shape[-1])


def half_lane():
    return lax.broadcasted_iota(jnp.int32, (1, 128), 1) % HEAD < HEAD // 2


def head_lane(h):
    lane = lax.broadcasted_iota(jnp.int32, (1, 128), 1)
    return lane < HEAD if h == 0 else lane >= HEAD


def turned(v):
    return jnp.where(half_lane(), pltpu.roll(v, 96, 1), pltpu.roll(v, 32, 1))


def norm_rows(x, gain):
    r = lax.rsqrt(jnp.mean(x * x, axis=-1, keepdims=True) + EPS)
    return x * r, r


def norm_stage(t, x_ref, gains_ref, n1_ref):
    @pl.loop(0, t // BLK)
    def _(m):
        rs = rows_of(m)
        unit, _ = norm_rows(x_ref[rs, :].astype(F32), None)
        n1_ref[rs, :] = (unit * gains_ref[0:1, :]).astype(BF16)


def qkv_stage(t, d, n1_ref, wa_ref, cos_ref, sin_ref, outs):
    for c, out in enumerate(outs):
        if out is None:
            continue

        @pl.loop(0, d // 256)
        def _(j, c=c, out=out):
            cols = pl.ds(pl.multiple_of(c * d + j * 256, 256), 256)
            raw = nn(n1_ref[...], wa_cols(wa_ref, cols))
            for s in range(2):
                part = raw[:, s * 128 : (s + 1) * 128]
                if c < 2:
                    part = part * cos_ref[...] + turned(part) * sin_ref[...]
                out[:, pl.ds(pl.multiple_of(j * 256 + s * 128, 128), 128)] = part.astype(BF16)


def key_bias(t, length):
    pos = lax.broadcasted_iota(jnp.int32, (t, 1), 0)
    return jnp.where(pos < length, 0.0, NEG).astype(BF16)


def causal_block():
    key = lax.broadcasted_iota(jnp.int32, (BLK, BLK), 0)
    query = lax.broadcasted_iota(jnp.int32, (BLK, BLK), 1)
    return key <= query


def score_operands(h, qp, kp, bias):
    mine = head_lane(h)
    lane = lax.broadcasted_iota(jnp.int32, (1, 128), 1)
    spare = lane == (HEAD if h == 0 else 0)
    zero = jnp.zeros((), BF16)
    q_m = jnp.where(mine, qp, zero)
    k_m = jnp.where(mine, kp, zero)
    q_s = jnp.where(spare, jnp.ones((), BF16), q_m)
    k_s = jnp.where(spare, bias, k_m)
    return q_m, k_m, q_s, k_s


def mask_diag(s, i):
    if i == 0:
        return jnp.where(causal_block(), s, NEG)
    return jnp.concatenate([s[: i * BLK], jnp.where(causal_block(), s[i * BLK :], NEG)], axis=0)


def attend_stage(t, d, length, q_ref, k_ref, v_ref, ctxt_ref, lse_ref, first, last):
    bias = key_bias(t, length)

    @pl.loop(first, last)
    def _(p):
        cols = pl.ds(pl.multiple_of(p * 128, 128), 128)
        qp, kp, vp = q_ref[:, cols], k_ref[:, cols], v_ref[:, cols]
        for h in range(2):
            _, _, q_s, k_s = score_operands(h, qp, kp, bias)
            for i in range(t // BLK):
                n = (i + 1) * BLK
                s = mask_diag(nt(k_s[:n], q_s[i * BLK : n]), i)
                top = jnp.max(s, axis=0, keepdims=True)
                e = jnp.exp2((s - top) * C2)
                total = jnp.sum(e, axis=0, keepdims=True)
                o = tn(vp[:n], e.astype(BF16))[h * HEAD : (h + 1) * HEAD] / total
                ctxt_ref[pl.ds(pl.multiple_of(p * 128 + h * HEAD, HEAD), HEAD), i * BLK : n] = o.astype(BF16)
                lse_ref[pl.ds(p * 2 + h, 1), i * BLK : n] = top * C2 + jnp.log2(total)


def out_stage(t, d, length, x_ref, wa_ref, ctxt_ref, hid_ref):
    out = dg(ctxt_ref[...], wa_cols(wa_ref, slice(3 * d, 4 * d)), 0, 1)
    pos = lax.broadcasted_iota(jnp.int32, (t, 1), 0)
    hid_ref[...] = x_ref[...].astype(F32) + jnp.where(pos < length, out, 0.0)


def k1_alone(len_ref, x_ref, gains_ref, wa_ref, cos_ref, sin_ref, q_ref, k_ref, v_ref, ctxt_ref, lse_ref, hid_ref, n1_ref):
    t, d = x_ref.shape
    length = len_ref[0]
    norm_stage(t, x_ref, gains_ref, n1_ref)
    qkv_stage(t, d, n1_ref, wa_ref, cos_ref, sin_ref, (q_ref, k_ref, v_ref))
    attend_stage(t, d, length, q_ref, k_ref, v_ref, ctxt_ref, lse_ref, 0, d // 128)
    out_stage(t, d, length, x_ref, wa_ref, ctxt_ref, hid_ref)


def token_mask(m, length):
    pos = m * BLK + lax.broadcasted_iota(jnp.int32, (BLK, 1), 0)
    return pos < length


def chunk_cols(wm, d, lo, hi):
    return wm[..., lo:hi].reshape(d, hi - lo)


def mlp_front(f, d, wm, n2_ref, dm_ref, wide):
    w = 256
    for j in range(f // w):
        lo, hi = j * w, (j + 1) * w
        gate = nn(n2_ref[...], chunk_cols(wm, d, lo, hi))
        up = nn(n2_ref[...], chunk_cols(wm, d, f + lo, f + hi))
        d_act = nn(dm_ref[...], chunk_cols(wm, d, 2 * f + lo, 2 * f + hi))
        s = 1.0 / (1.0 + jnp.exp2(gate * (-LOG2E)))
        sw = gate * s
        wide[:, 2 * f + lo : 2 * f + hi] = (sw * up).astype(BF16)
        wide[:, lo:hi] = (d_act * up * (s + sw * (1.0 - s))).astype(BF16)
        wide[:, f + lo : f + hi] = (d_act * sw).astype(BF16)


def mlp_out(f, d, wm, n2_ref, wide, mlp_ref):
    w = 256
    for j in range(f // w):
        lo, hi = j * w, (j + 1) * w
        gate = nn(n2_ref[...], chunk_cols(wm, d, lo, hi))
        up = nn(n2_ref[...], chunk_cols(wm, d, f + lo, f + hi))
        wide[:, lo:hi] = (gate * up / (1.0 + jnp.exp2(gate * (-LOG2E)))).astype(BF16)
    mlp_ref[...] += nt(wide[:, :f], chunk_cols(wm, d, 2 * f, 3 * f))


def mlp_back(f, d, wm, n2t_ref, dmt_ref, wide, dn2_ref):
    w = 256
    dn2_ref[...] += nt(wide[:, : 2 * f], chunk_cols(wm, d, 0, 2 * f))
    for j in range(3 * f // w):
        cols = slice(j * w, (j + 1) * w)
        left = n2t_ref if j * w < 2 * f else dmt_ref
        wm[..., cols] = nn(left[...], wide[:, cols]).astype(BF16).reshape(wm.shape[:-1] + (w,))


def k2(len_ref, cot_ref, gains_ref, hid_ref, wm_ref, lo_ref, dh_ref, da_ref, gm_ref, gg_ref,
       n2_ref, dm_ref, n2t_ref, dmt_ref, wide, mlp_ref, dn2_ref):
    t, d = cot_ref.shape
    tp, f = wm_ref.shape[0], wm_ref.shape[-1] // 3
    length = len_ref[0]

    @pl.loop(0, t // BLK)
    def _(m):
        rs = rows_of(m)
        unit, _ = norm_rows(hid_ref[rs, :], None)
        n2 = (unit * gains_ref[1:2, :]).astype(BF16)
        n2_ref[rs, :] = n2
        n2t_ref[:, rs] = n2.T
        dm = jnp.where(token_mask(m, length), cot_ref[rs, :], jnp.zeros((), BF16))
        dm_ref[rs, :] = dm
        dmt_ref[:, rs] = dm.T

    mlp_ref[...] = jnp.zeros_like(mlp_ref)
    dn2_ref[...] = jnp.zeros_like(dn2_ref)

    @pl.loop(0, tp)
    def _(z):
        gm_ref[z] = wm_ref[z]
        mlp_out(f, d, gm_ref.at[z], n2_ref, wide, mlp_ref)
        mlp_front(f, d, gm_ref.at[z], n2_ref, dm_ref, wide)
        mlp_back(f, d, gm_ref.at[z], n2t_ref, dmt_ref, wide, dn2_ref)

    gg_ref[...] = jnp.zeros_like(gg_ref)

    @pl.loop(0, t // BLK)
    def _(m):
        rs = rows_of(m)
        hid = hid_ref[rs, :]
        ok = token_mask(m, length)
        lo_ref[rs, :] = (hid + jnp.where(ok, mlp_ref[rs, :], 0.0)).astype(BF16)
        unit, r = norm_rows(hid, None)
        dn2 = dn2_ref[rs, :]
        gg_ref[...] += jnp.sum(dn2 * unit, axis=0, keepdims=True)
        e2 = dn2 * gains_ref[1:2, :]
        dh = cot_ref[rs, :].astype(F32) + r * (e2 - unit * jnp.mean(e2 * unit, axis=-1, keepdims=True))
        dh_ref[rs, :] = dh
        da_ref[rs, :] = jnp.where(ok, dh, 0.0).astype(BF16)


def attend_back(t, d, length, q_ref, k_ref, v_ref, dctx_ref, lse_ref, dlt_ref, cos_ref, sin_ref, dqkv_ref, dk_acc, dv_acc, first, last):
    bias = key_bias(t, length)

    @pl.loop(first, last)
    def _(p):
        cols = pl.ds(pl.multiple_of(p * 128, 128), 128)
        qp, kp, vp, gp = q_ref[:, cols], k_ref[:, cols], v_ref[:, cols], dctx_ref[:, cols]
        dk_acc[...] = jnp.zeros_like(dk_acc)
        dv_acc[...] = jnp.zeros_like(dv_acc)
        ops = [score_operands(h, qp, kp, bias) for h in range(2)]
        for i in range(t // BLK):
            n = (i + 1) * BLK
            qs = slice(i * BLK, n)
            dq = None
            for h in range(2):
                q_m, k_m, q_s, k_s = ops[h]
                g_m = jnp.where(head_lane(h), gp[qs], jnp.zeros((), BF16))
                s = mask_diag(nt(k_s[:n], q_s[qs]), i)
                pr = jnp.exp2(s * C2 - lse_ref[pl.ds(p * 2 + h, 1), qs])
                dp = nt(vp[:n], g_m)
                ds = (pr * (dp - dlt_ref[pl.ds(p * 2 + h, 1), qs])).astype(BF16)
                dv_acc[:n, :] += nn(pr.astype(BF16), g_m)
                dk_acc[:n, :] += nn(ds, q_m[qs])
                part = tn(ds, k_m[:n])
                dq = part if dq is None else dq + part
            dq = dq * (HEAD**-0.5)
            dqkv_ref[qs, cols] = (dq * cos_ref[qs, :] - turned(dq) * sin_ref[qs, :]).astype(BF16)
        dk = dk_acc[...] * (HEAD**-0.5)
        dqkv_ref[:, pl.ds(pl.multiple_of(d + p * 128, 128), 128)] = (dk * cos_ref[...] - turned(dk) * sin_ref[...]).astype(BF16)
        dqkv_ref[:, pl.ds(pl.multiple_of(2 * d + p * 128, 128), 128)] = dv_acc[...].astype(BF16)


def k3(len_ref, x_ref, gains_ref, wa_ref, cos_ref, sin_ref, q_ref, k_ref, v_ref, ctxt_ref, lse_ref, dh_ref, da_ref,
       gx_ref, ga_ref, gg_ref, n1_ref, n1t_ref, dat_ref, dctx_ref, dlt_ref, dqkv_ref, dk_acc, dv_acc, dn1_ref):
    t, d = x_ref.shape
    length = len_ref[0]

    dat_ref[...] = da_ref[...].T

    @pl.loop(0, d // 256)
    def _(j):
        rs = pl.ds(pl.multiple_of(j * 256, 256), 256)
        cols = pl.ds(pl.multiple_of(3 * d + j * 256, 256), 256)
        ga_ref[:, :, :, cols] = nt(dat_ref[...], ctxt_ref[rs, :]).astype(BF16).reshape(ga_ref.shape[:3] + (256,))
        dctx = nn(da_ref[...], wa_cols(wa_ref, cols)).astype(BF16)
        dctx_ref[:, rs] = dctx
        prod = dctx.T.astype(F32) * ctxt_ref[rs, :].astype(F32)
        for h in range(4):
            dlt_ref[pl.ds(j * 4 + h, 1), :] = jnp.sum(prod[h * HEAD : (h + 1) * HEAD], axis=0, keepdims=True)

    attend_back(t, d, length, q_ref, k_ref, v_ref, dctx_ref, lse_ref, dlt_ref, cos_ref, sin_ref, dqkv_ref, dk_acc, dv_acc, 0, d // 128)

    @pl.loop(0, t // BLK)
    def _(m):
        rs = rows_of(m)
        unit, _ = norm_rows(x_ref[rs, :].astype(F32), None)
        n1t_ref[:, rs] = (unit * gains_ref[0:1, :]).astype(BF16).T

    @pl.loop(0, 3 * d // 256)
    def _(j):
        cols = pl.ds(pl.multiple_of(j * 256, 256), 256)
        ga_ref[:, :, :, cols] = nn(n1t_ref[...], dqkv_ref[:, cols]).astype(BF16).reshape(ga_ref.shape[:3] + (256,))

    dn1_ref[...] = nt(dqkv_ref[...], wa_cols(wa_ref, slice(0, 3 * d)))

    gg_ref[...] = jnp.zeros_like(gg_ref)

    @pl.loop(0, t // BLK)
    def _(m):
        rs = rows_of(m)
        unit, r = norm_rows(x_ref[rs, :].astype(F32), None)
        dn1 = dn1_ref[rs, :]
        gg_ref[...] += jnp.sum(dn1 * unit, axis=0, keepdims=True)
        e1 = dn1 * gains_ref[0:1, :]
        gx_ref[rs, :] = (dh_ref[rs, :] + r * (e1 - unit * jnp.mean(e1 * unit, axis=-1, keepdims=True))).astype(BF16)


def rope_np(t):
    half = HEAD // 2
    freqs = np.float32(10000.0) ** (np.float32(-2.0) * np.arange(half, dtype=np.float32) / np.float32(HEAD))
    ang = np.arange(t, dtype=np.float32)[:, None] * freqs[None, :].astype(np.float32)
    c, s = np.cos(ang), np.sin(ang)
    return np.concatenate([c, c, c, c], 1).astype(np.float32), np.concatenate([-s, s, -s, s], 1).astype(np.float32)


MESH = pl.DeviceIdType.MESH
Z = 4


def flip(d, bit):
    return d + bit - 2 * bit * lax.rem(d // bit, 2)


class Net:
    def __init__(self, send, recv, local):
        self.d, self.z = lax.axis_index("dp"), lax.axis_index("tp")
        self.yx, self.c = self.d // 2, lax.rem(self.d, 2)
        self.x, self.y, self.core = ((flip(self.d, b), self.z) for b in (2, 4, 1))
        self.send, self.recv, self.local = send, recv, local
        self.copies, self.own, self.gone = {}, {}, set()

    def peer(self, r):
        return lax.rem(self.z + r, Z)

    def source(self, r):
        return lax.rem(self.z + Z - r, Z)

    def barrier(self):
        sem = pltpu.get_barrier_semaphore()
        for dev in (self.x, self.y, self.core) + tuple((self.d, self.peer(r)) for r in range(1, Z)):
            pl.semaphore_signal(sem, inc=1, device_id=dev, device_id_type=MESH)
        pl.semaphore_wait(sem, 6)

    def make(self, i, src, dst, dev):
        return pltpu.make_async_remote_copy(
            src_ref=src, dst_ref=dst, send_sem=self.send.at[i], recv_sem=self.recv.at[i], device_id=dev, device_id_type=MESH
        )

    def plan(self, name, src, dst, dev):
        self.copies[name] = self.make(len(self.copies), src, dst, dev)

    def go(self, *names):
        for name in names:
            self.copies[name].start()

    def start(self, name, src, dst, dev):
        self.plan(name, src, dst, dev)
        self.go(name)

    def keep(self, name, src, dst):
        copy = pltpu.make_async_copy(src, dst, self.local.at[len(self.own)])
        copy.start()
        self.own[name] = copy

    def got(self, *names):
        for name in names:
            self.copies[name].wait_recv()

    def kept(self, name):
        self.own[name].wait()

    def left(self, name):
        self.copies[name].wait_send()
        self.gone.add(name)

    def finish(self):
        for name, copy in self.copies.items():
            if name not in self.gone:
                copy.wait_send()


def plan_gather(net, tag, own, slab, halves):
    kx, ky = flip(net.yx, 1), flip(net.yx, 2)
    net.plan(tag + "x", own, slab(net.yx), net.x)
    net.plan(tag + "y", own, slab(net.yx), net.y)
    net.plan(tag + "l", slab(kx).at[:, halves[0]], slab(kx).at[:, halves[0]], net.y)
    net.plan(tag + "r", slab(ky).at[:, halves[1]], slab(ky).at[:, halves[1]], net.x)


def spread(net, tag):
    net.go(tag + "x", tag + "y")


def relay(net, tag):
    net.got(tag + "x")
    net.go(tag + "l")
    net.got(tag + "y")
    net.go(tag + "r")


def all_sum(net, tag, own, boxes, last=False):
    def over_tp(src, out):
        for r in range(1, Z):
            net.start(f"{tag}z{r}", src, boxes.at[r - 1], (net.d, net.peer(r)))
        yield
        net.got(*(f"{tag}z{r}" for r in range(1, Z)))
        boxes[out] = src[...] + (boxes[0] + boxes[1] + boxes[2])

    def over_dp(src, outs):
        for i, (name, dev) in enumerate((("x", net.x), ("y", net.y), ("c", net.core))):
            net.start(tag + name, src, boxes.at[3 + i], dev)
            yield
            net.got(tag + name)
            boxes[outs[i]] = src[...] + boxes[3 + i]
            src = boxes.at[outs[i]]

    if last:
        yield from over_dp(own, (6, 7, 8))
        yield from over_tp(boxes.at[8], 9)
    else:
        yield from over_tp(own, 6)
        yield from over_dp(boxes.at[6], (7, 8, 9))
    yield


def lane_pairs(stage, hw):
    low = lax.broadcasted_iota(jnp.int32, (1, 128), 1) < HEAD
    parts = [[stage[z][:, c * 128 : (c + 1) * 128] for z in range(Z)] for c in range(4)]
    for j in range(Z // 2):
        for g in range(2):
            cols = slice(512 + g * 128, 640 + g * 128)
            a, b = stage[2 * j][:, cols].astype(F32), stage[2 * j + 1][:, cols].astype(F32)
            parts[2 * g].append(jnp.where(low, a, pltpu.roll(b, HEAD, 1)).astype(BF16))
            parts[2 * g + 1].append(jnp.where(low, pltpu.roll(a, HEAD, 1), b).astype(BF16))
    return parts


class Reduce:
    def __init__(self, net, base, data, use, credit, rc, r1x, r1y, r2l, r2r):
        self.net, self.base, self.data, self.use, self.credit = net, base, data, use, credit
        self.rc, self.r1x, self.r1y, self.r2l, self.r2r = rc, r1x, r1y, r2l, r2r
        self.x, self.y = lax.rem(net.yx, 2), net.yx // 2
        half = data.shape[-1] // 2
        self.lo, self.hi = slice(0, half), slice(half, 2 * half)

    def slot(self, i):
        return self.rc.at[lax.rem(self.use(i), 2), :, :, :, 0 : self.data.shape[-1]]

    def copies0(self, g, i):
        return [self.net.make(self.base + i, self.data.at[g, :, :, 1 - self.net.c], self.slot(i), self.net.core)]

    def copies1(self, g, i):
        net, c = self.net, self.net.c
        return [
            net.make(self.base + 4 + i, self.data.at[g, :, 1 - self.x, c, :, self.lo], self.r1x.at[i], net.x),
            net.make(self.base + 8 + i, self.data.at[g, 1 - self.y, :, c, :, self.hi], self.r1y.at[i], net.y),
        ]

    def copies2(self, g, i):
        net, c = self.net, self.net.c
        return [
            net.make(self.base + 12 + i, self.data.at[g, 1 - self.y, self.x, c, :, self.lo], self.r2l.at[i], net.y),
            net.make(self.base + 16 + i, self.data.at[g, self.y, 1 - self.x, c, :, self.hi], self.r2r.at[i], net.x),
        ]

    def add(self, at, value):
        self.data[at] = (self.data[at].astype(F32) + value.astype(F32)).astype(BF16)

    def p0(self, g, i):
        @pl.when(self.use(i) >= 2)
        def _():
            pl.semaphore_wait(self.credit, 1)

        for copy in self.copies0(g, i):
            copy.start()

    def p1(self, g, i):
        for copy in self.copies0(g, i):
            copy.wait_recv()
        for y in range(2):
            for x in range(2):
                self.add((g, y, x, self.net.c), self.slot(i)[y, x])

        @pl.when(self.use(i) < 6)
        def _():
            pl.semaphore_signal(self.credit, inc=1, device_id=self.net.core, device_id_type=MESH)

        for copy in self.copies1(g, i):
            copy.start()

    def p2(self, g, i):
        for copy in self.copies1(g, i):
            copy.wait_recv()
        for k in range(2):
            self.add((g, k, self.x, self.net.c, slice(None), self.lo), self.r1x[i, k])
            self.add((g, self.y, k, self.net.c, slice(None), self.hi), self.r1y[i, k])
        for copy in self.copies2(g, i):
            copy.start()

    def p3(self, g, i):
        for copy in self.copies2(g, i):
            copy.wait_recv()
        self.add((g, self.y, self.x, self.net.c, slice(None), self.lo), self.r2l[i])
        self.add((g, self.y, self.x, self.net.c, slice(None), self.hi), self.r2r[i])

    def own(self, g):
        return self.data.at[g, self.y, self.x, self.net.c]

    def sent(self, g, i):
        for copy in self.copies0(g, i) + self.copies1(g, i) + self.copies2(g, i):
            copy.wait_send()


def packed_thirds(own):
    low = lax.broadcasted_iota(jnp.int32, (1, 128), 1) < HEAD
    for z in range(Z):
        s, u = z % 2, z // 2
        third = [own(2)[:, c * 256 + u * 128 : c * 256 + u * 128 + 128].astype(F32) for c in range(3)]
        third.append(own(3)[:, 512 + u * 128 : 512 + u * 128 + 128].astype(F32))
        for j in range(2):
            a, b = third[2 * j], third[2 * j + 1]
            both = jnp.where(low, a, pltpu.roll(b, HEAD, 1)) if s == 0 else jnp.where(low, pltpu.roll(a, HEAD, 1), b)
            yield z, j, both.astype(BF16)


def layer_kernel(len_ref, gs_ref, was_h, tok_h, cot_h, wms_h, cos_h, sin_h,
                 lo_out, gx_out, grads_out, gg_ref, q_h, k_h,
                 x_ref, cot_ref, cos_ref, sin_ref, wa_ref, gm_ref, ctxt_ref, lse_ref, hid_ref,
                 b1, b2, lo_ref, t1, t2, wide, f1, dlt_ref, gains_ref, gsum_ref, boxes_ref, boxes2_ref, pack_ref,
                 mc, mx, my, ml, mr, mz, ga_ref, ax, ay, al, ar, az,
                 send, recv, local, credit):
    t, d = x_ref.shape
    part = t // Z
    f = gm_ref.shape[-1] // 3
    length = len_ref[0]
    net = Net(send, recv, local)
    z, yx, c = net.z, net.yx, net.c
    px, py = lax.rem(yx, 2), yx // 2
    mine = pl.ds(pl.multiple_of(z * part, part), part)
    kd = flip(flip(yx, 1), 2)
    order = ((1, 0, 2, 3), (0, 1, 2, 3), (3, 2, 1, 0), (2, 3, 1, 0))

    def chunk(i):
        if not isinstance(i, int):
            return sum((i == k).astype(jnp.int32) * chunk(k) for k in range(Z))
        return sum((z == k).astype(jnp.int32) * order[k][i] for k in range(Z))

    a_half = (slice(0, 2 * d), slice(2 * d, 4 * d))
    m_half = (slice(0, 3 * f // 2), slice(3 * f // 2, 3 * f))
    a_slab = lambda k: wa_ref.at[k, c]
    m_slab = lambda i: lambda k: gm_ref.at[chunk(i), k // 2, lax.rem(k, 2), c]
    mine_slab = lambda i: m_slab(i)(yx)

    def line(k, right):
        shard = z - (k - 1) if right else z + (k - 1)
        place = gm_ref.at[shard, py, px, c]
        return net.make(76 + 2 * k + right, wms_h if k == 1 else place, place, (net.d, z + 1 if right else z - 1))

    def came(k, right):
        place = gm_ref.at[z - k if right else z + k, py, px, c]
        return net.make(76 + 2 * k + right, place, place, (net.d, z - 1 if right else z + 1))

    def line_go(k):
        pl.when((z >= k - 1) & (z <= Z - 2))(lambda: line(k, 1).start())
        pl.when((z <= Z - k) & (z >= 1))(lambda: line(k, 0).start())

    def line_wait(k):
        pl.when(z >= k)(lambda: came(k, 1).wait_recv())
        pl.when(z <= Z - 1 - k)(lambda: came(k, 0).wait_recv())

    def line_left():
        for k in range(1, Z):
            pl.when((z >= k - 1) & (z <= Z - 2))(lambda k=k: line(k, 1).wait_send())
            pl.when((z <= Z - k) & (z >= 1))(lambda k=k: line(k, 0).wait_send())

    def chunk_out(i):
        net.got(f"m{i}l", f"m{i}r")
        net.go(f"m{i}c")

    plan_gather(net, "a", wa_ref.at[yx, c], a_slab, a_half)
    for i in range(Z):
        plan_gather(net, f"m{i}", wms_h if i == 1 else mine_slab(i), m_slab(i), m_half)
        rows = gm_ref.at[chunk(i), :, :, c]
        net.plan(f"m{i}c", rows, rows, net.core)

    net.barrier()
    gains_steps = all_sum(net, "g", gs_ref, boxes_ref)
    next(gains_steps)
    for r in range(1, Z):
        net.start(f"az{r}", was_h, pack_ref.at[z], (net.d, net.peer(r)))
    net.keep("a", was_h, pack_ref.at[z])
    net.keep("m", wms_h, gm_ref.at[z, py, px, c])
    net.keep("t", tok_h.at[z], x_ref.at[mine])
    net.keep("c", cot_h.at[z], cot_ref.at[mine])
    net.keep("cos", cos_h, cos_ref)
    net.keep("sin", sin_h, sin_ref)
    for _ in range(4):
        next(gains_steps)
    gains_ref[...] = boxes_ref[9]
    net.got("az1", "az2", "az3")
    line_go(1)
    for r in range(1, Z):
        net.start(f"t{r}", tok_h.at[net.peer(r)], x_ref.at[mine], (net.d, net.peer(r)))
    net.kept("a")
    for i, heads in enumerate(lane_pairs(pack_ref, 4 * d // Z)):
        for j, value in enumerate(heads):
            wa_ref[yx, c, :, i * d + j * 128 : i * d + (j + 1) * 128] = value
    spread(net, "a")
    net.start("ac0", wa_ref.at[yx, c], wa_ref.at[yx, c], net.core)
    relay(net, "a")
    spread(net, "m1")
    net.start("ac1", a_slab(flip(yx, 1)), a_slab(flip(yx, 1)), net.core)
    net.start("ac2", a_slab(flip(yx, 2)), a_slab(flip(yx, 2)), net.core)
    net.got("al", "ar")
    net.start("ac3", a_slab(kd), a_slab(kd), net.core)
    net.kept("m")
    line_wait(1)
    net.got("t1", "t2", "t3")
    net.kept("t")
    line_go(2)
    spread(net, "m0")
    n1_ref = b1
    norm_stage(t, x_ref, gains_ref, n1_ref)
    net.kept("cos")
    net.kept("sin")
    net.got("ac0", "ac1", "ac2", "ac3")

    q_ref, k_ref, v_ref = (wide.at[:, i * d : (i + 1) * d] for i in range(3))
    qkv_stage(t, d, n1_ref, wa_ref, cos_ref, sin_ref, (q_ref, k_ref, v_ref))
    for name, src, dst in (("q", q_ref, q_h), ("k", k_ref, k_h)):
        net.keep(name, src, dst)
    line_wait(2)
    line_go(3)
    for r in range(1, Z):
        net.start(f"c{r}", cot_h.at[net.peer(r)], cot_ref.at[mine], (net.d, net.peer(r)))
    spread(net, "m2")
    relay(net, "m1")
    attend = functools.partial(attend_stage, t, d, length, q_ref, k_ref, v_ref, ctxt_ref, lse_ref)
    attend(0, 3)
    line_wait(3)
    spread(net, "m3")
    relay(net, "m0")
    chunk_out(1)
    attend(3, d // 128)
    chunk_out(0)
    relay(net, "m2")
    out_stage(t, d, length, x_ref, wa_ref, ctxt_ref, hid_ref)
    chunk_out(2)

    mred = Reduce(net, 86, gm_ref, lambda i: i, credit, mc, mx, my, ml, mr)
    ared = Reduce(net, 106, ga_ref, lambda i: 4 + lax.rem(i + 1, 4), credit, mc, ax, ay, al, ar)

    def mz_copy(w, r):
        return net.make(126 + r, mred.own(w), mz.at[r - 1], (net.d, w))

    def mz_out(i):
        w = chunk(i)
        mz_copy(w, lax.rem(w + Z - z, Z)).start()

    n2_ref, dm_ref, n2t_ref, dmt_ref = b1, b2, t1, t2

    @pl.loop(0, t // BLK)
    def _(m):
        rs = rows_of(m)
        unit, _ = norm_rows(hid_ref[rs, :], None)
        n2 = (unit * gains_ref[1:2, :]).astype(BF16)
        n2_ref[rs, :] = n2
        n2t_ref[:, rs] = n2.T

    def chunk_left(i):
        for tag in ("x", "y", "l", "r", "c"):
            net.left(f"m{i}{tag}")

    arrived = tuple((lambda i=i: net.got(f"m{i}c"),) for i in range(Z))
    last_chunk = ((lambda: relay(net, "m3"),), (lambda: chunk_out(3),), (), ())
    middle = (
        (),
        (lambda: mred.p1(chunk(0), 0),),
        (lambda: mred.p2(chunk(0), 0), lambda: mred.p1(chunk(1), 1)),
        (lambda: mred.p2(chunk(1), 1), lambda: mred.p1(chunk(2), 2)),
    )
    after = ((), (), (lambda: mred.p3(chunk(0), 0), lambda: mz_out(0)), ())

    def at(i, steps):
        for k in range(Z):
            if steps[k]:

                @pl.when(i == k)
                def _():
                    for step in steps[k]:
                        step()

    f1[...] = jnp.zeros_like(f1)
    net.kept("q")
    net.kept("k")

    @pl.loop(0, Z)
    def _(i):
        at(i, arrived)
        mlp_out(f, d, gm_ref.at[chunk(i)], n2_ref, wide, f1)
        at(i, last_chunk)

    for j in (1, 2, 3, 0):
        m = net.peer(j)
        rs = rows_of(m)
        lo_ref[rs, :] = (hid_ref[rs, :] + jnp.where(token_mask(m, length), f1[rs, :], 0.0)).astype(BF16)
        if j:
            net.start(f"lo{j}", lo_ref.at[rs], lo_out.at[z], (net.d, m))
        else:
            net.keep("lo", lo_ref.at[rs], lo_out.at[z])
    line_left()
    net.got("c1", "c2", "c3")
    net.kept("c")

    @pl.loop(0, t // BLK)
    def _(m):
        rs = rows_of(m)
        dm = jnp.where(token_mask(m, length), cot_ref[rs, :], jnp.zeros((), BF16))
        dm_ref[rs, :] = dm
        dmt_ref[:, rs] = dm.T

    f1[...] = jnp.zeros_like(f1)

    @pl.loop(0, Z)
    def _(i):
        gm = gm_ref.at[chunk(i)]
        mlp_front(f, d, gm, n2_ref, dm_ref, wide)
        at(i, middle)
        at(i, tuple((functools.partial(chunk_left, k),) for k in range(Z)))
        mlp_back(f, d, gm, n2t_ref, dmt_ref, wide, f1)
        mred.p0(chunk(i), i)
        at(i, after)

    for name, src, dst in (("q2", q_h, q_ref), ("k2", k_h, k_ref)):
        net.keep(name, src, dst)
    gsum_ref[...] = jnp.zeros_like(gsum_ref)
    dh_ref, da_ref = hid_ref, b1

    @pl.loop(0, t // BLK)
    def _(m):
        rs = rows_of(m)
        hid = hid_ref[rs, :]
        ok = token_mask(m, length)
        unit, r = norm_rows(hid, None)
        dn2 = f1[rs, :]
        gsum_ref[1:2, :] += jnp.sum(dn2 * unit, axis=0, keepdims=True)
        e2 = dn2 * gains_ref[1:2, :]
        dh = cot_ref[rs, :].astype(F32) + r * (e2 - unit * jnp.mean(e2 * unit, axis=-1, keepdims=True))
        dh_ref[rs, :] = dh
        da_ref[rs, :] = jnp.where(ok, dh, 0.0).astype(BF16)

    mred.p2(chunk(2), 2)
    mred.p3(chunk(1), 1)
    mred.p1(chunk(3), 3)

    dat_ref, n1t_ref, dctx_ref = t1, t2, cot_ref
    dat_ref[...] = da_ref[...].T
    shape = ga_ref.shape[1:5]

    @pl.loop(0, d // 256)
    def _(j):
        rs = pl.ds(pl.multiple_of(j * 256, 256), 256)
        cols = pl.ds(pl.multiple_of(3 * d + j * 256, 256), 256)
        ga_ref[3, :, :, :, :, rs] = nt(dat_ref[...], ctxt_ref[rs, :]).astype(BF16).reshape(shape + (256,))
        dctx = nn(da_ref[...], wa_cols(wa_ref, cols)).astype(BF16)
        dctx_ref[:, rs] = dctx
        prod = dctx.T.astype(F32) * ctxt_ref[rs, :].astype(F32)
        for h in range(4):
            dlt_ref[pl.ds(j * 4 + h, 1), :] = jnp.sum(prod[h * HEAD : (h + 1) * HEAD], axis=0, keepdims=True)

    ared.p0(3, 3)

    @pl.loop(0, t // BLK)
    def _(m):
        rs = rows_of(m)
        unit, _ = norm_rows(x_ref[rs, :].astype(F32), None)
        n1t_ref[:, rs] = (unit * gains_ref[0:1, :]).astype(BF16).T

    mred.p3(chunk(2), 2)
    mz_out(2)
    mred.p2(chunk(3), 3)
    ared.p1(3, 3)
    net.kept("q2")
    net.kept("k2")
    dk_acc, dv_acc = f1.at[:, 0:128], f1.at[:, 128:256]
    lanes = dict(o=slice(512 - 128, 512), q=slice(0, 384), t=slice(512, 768))

    def to_owner(base, w, tag):
        r = lax.rem(w + Z - z, Z)

        @pl.when(r != 0)
        def _():
            net.make(base + r - 1, pack_ref.at[w, :, lanes[tag]], az.at[r - 1, :, lanes[tag]], (net.d, w)).start()

    def pack_out():
        for w in range(Z):
            pack_ref[w, :, lanes["o"]] = ared.own(3)[:, w * 128 : w * 128 + 128]
            to_owner(132, w, "o")

    def pack_pairs(g):
        for s in range(2):
            w = 2 * g + s
            for k in range(3):
                pack_ref[w, :, k * 128 : (k + 1) * 128] = ared.own(g)[:, k * 256 + s * 128 : k * 256 + s * 128 + 128]
            to_owner(135, w, "q")

    def pack_thirds():
        for w, j, value in packed_thirds(ared.own):
            pack_ref[w, :, 512 + j * 128 : 640 + j * 128] = value
        for w in range(Z):
            to_owner(138, w, "t")

    first = (
        (lambda: mred.p3(chunk(3), 3), lambda: mz_out(3), lambda: ared.p2(3, 3)),
        (lambda: ared.p1(0, 0),),
        (lambda: ared.p3(0, 0), lambda: pack_pairs(0), lambda: ared.p1(1, 1)),
    )
    second = (
        (lambda: ared.p3(3, 3), pack_out),
        (lambda: ared.p2(0, 0),),
        (lambda: ared.p2(1, 1),),
    )

    @pl.loop(0, 3)
    def _(g):
        @pl.loop(0, 2)
        def _(s):
            p = 2 * g + s
            attend_back(t, d, length, q_ref, k_ref, v_ref, dctx_ref, lse_ref, dlt_ref, cos_ref, sin_ref, wide, dk_acc, dv_acc, p, p + 1)
            for k in range(3):
                for steps, which in ((first, 0), (second, 1)):

                    @pl.when((g == k) & (s == which))
                    def _():
                        for step in steps[k]:
                            step()

        for k in range(3):
            cols = pl.ds(pl.multiple_of(k * d + g * 256, 256), 256)
            ga_ref[g, :, :, :, :, k * 256 : (k + 1) * 256] = nn(n1t_ref[...], wide[:, cols]).astype(BF16).reshape(shape + (256,))
        ared.p0(g, g)

    gx_ref = b1
    for j in (1, 2, 3, 0):
        m = net.peer(j)
        rs = rows_of(m)
        dn1 = nt(wide[rs, :], wa_cols(wa_ref, slice(0, 3 * d)))
        unit, r = norm_rows(x_ref[rs, :].astype(F32), None)
        gsum_ref[0:1, :] += jnp.sum(dn1 * unit, axis=0, keepdims=True)
        e1 = dn1 * gains_ref[0:1, :]
        gx_ref[rs, :] = (dh_ref[rs, :] + r * (e1 - unit * jnp.mean(e1 * unit, axis=-1, keepdims=True))).astype(BF16)
        if j:
            net.start(f"gx{j}", gx_ref.at[rs], gx_out.at[z], (net.d, m))
        else:
            net.keep("gx", gx_ref.at[rs], gx_out.at[z])
        if j == 1:
            ared.p1(2, 2)
        elif j == 2:
            ared.p3(1, 1)
            pack_pairs(1)
    steps = all_sum(net, "s", gsum_ref, boxes2_ref, last=True)
    next(steps)
    ared.p2(2, 2)
    next(steps)
    next(steps)
    ared.p3(2, 2)
    pack_thirds()
    next(steps)
    total = mred.own(z)[...].astype(F32)
    for r in range(1, Z):
        mz_copy(net.peer(r), r).wait_recv()
        total = total + mz[r - 1].astype(F32)
    rows, half = total.shape[0], total.shape[1] // 2
    f1[0:rows, :] = total[:, :half]
    f1[rows : 2 * rows, :] = total[:, half:]

    parts = [
        net.make(base + r - 1, pack_ref.at[net.peer(r), :, lanes[tag]], az.at[r - 1, :, lanes[tag]], (net.d, net.peer(r)))
        for base, tag in ((132, "o"), (135, "q"), (138, "t"))
        for r in range(1, Z)
    ]
    for copy in parts:
        copy.wait_recv()
    total = pack_ref[z].astype(F32)
    for i in range(Z - 1):
        total = total + az[i].astype(F32)
    f1[2 * rows : 3 * rows, :] = total
    net.keep("grads", f1.at[0 : 3 * rows], grads_out)
    next(steps)
    gg_ref[...] = boxes2_ref[9]
    net.got(*(f"{n}{j}" for n in ("lo", "gx") for j in range(1, Z)))
    for name in ("lo", "gx", "grads"):
        net.kept(name)
    for i in range(Z):
        mred.sent(chunk(i), i)
        ared.sent(i, i)
    for copy in parts:
        copy.wait_send()
    for r in range(1, Z):
        mz_copy(net.peer(r), r).wait_send()
    net.finish()


VM = pl.BlockSpec(memory_space=pltpu.VMEM)
SM = pl.BlockSpec(memory_space=pltpu.SMEM)


def call(kernel, ins, outs, scratch):
    return pl.pallas_call(
        kernel,
        out_shape=[jax.ShapeDtypeStruct(s, dt) for s, dt in outs],
        in_specs=[SM] + [VM] * (len(ins) - 1),
        out_specs=[VM] * len(outs),
        scratch_shapes=[pltpu.VMEM(s, dt) for s, dt in scratch],
        compiler_params=pltpu.CompilerParams(vmem_limit_bytes=60 * 2**20),
    )(*ins)


def backward(length, x, cot, gains, wa, wm, cosine, sine, q, k, v, ctxt, lse, hid):
    t, d = x.shape
    f = wm.shape[-1] // 3
    heads = lse.shape[0]
    td, dt = ((t, d), BF16), ((d, t), BF16)
    lo, dh, da, gm, gg2 = call(
        k2,
        (length, cot, gains, hid, wm),
        (td, ((t, d), F32), td, (wm.shape, BF16), ((1, d), F32)),
        (td, td, dt, dt, ((t, 3 * f), BF16), ((t, d), F32), ((t, d), F32)),
    )
    gx, ga, gg1 = call(
        k3,
        (length, x, gains, wa, cosine, sine, q, k, v, ctxt, lse, dh, da),
        (td, (wa.shape, BF16), ((1, d), F32)),
        (td, dt, dt, td, ((heads, t), F32), ((t, 3 * d), BF16), ((t, 128), F32), ((t, 128), F32), ((t, d), F32)),
    )
    return lo, gx, ga, gm, jnp.concatenate([gg1, gg2])


def one_sequence(length, x, cot, gains, wa, wm, cosine, sine):
    t, d = x.shape
    heads = -(-d // HEAD // 8) * 8
    td, dt = ((t, d), BF16), ((d, t), BF16)
    kept = call(k1_alone, (length, x, gains, wa, cosine, sine), (td, td, td, dt, ((heads, t), F32), ((t, d), F32)), (td,))
    return backward(length, x, cot, gains, wa, wm, cosine, sine, *kept)


def pack_weights(w_qkv, w_out, w_gate_up, w_down):
    attn = jnp.stack([w_qkv[0], w_qkv[1], w_qkv[2], w_out.T], axis=1)
    mlp = jnp.concatenate([w_gate_up[0], w_gate_up[1], w_down.T], axis=1)
    return attn, mlp


def unpack_grads(g_attn, g_mlp, fw):
    g_qkv = jnp.transpose(g_attn[:, :3], (1, 0, 2))
    g_gate_up = jnp.stack([g_mlp[:, i * fw : (i + 1) * fw] for i in range(2)])
    return g_qkv, g_attn[:, 3].T, g_gate_up, g_mlp[:, 2 * fw :].T


def to_sequences(local):
    return lax.all_to_all(local, "tp", split_axis=0, concat_axis=1, tiled=True)


def to_positions(whole):
    return lax.all_to_all(whole, "tp", split_axis=1, concat_axis=0, tiled=True)


def fused_layer(length, tokens, cotangent, attn, mlp, gains, cosine, sine):
    batch, part, d = tokens.shape
    t, rows, f3 = part * Z, attn.shape[0], mlp.shape[1]
    heads = -(-d // HEAD // 8) * 8
    pairs = 2 * HEAD
    was = jnp.concatenate(
        [attn[:, :, :pairs].reshape(rows, 4 * pairs), attn[:, :, pairs:].reshape(rows, 4 * HEAD)], axis=1
    )
    spot = (lax.axis_index("dp") * Z + lax.axis_index("tp")) * gains.shape[1]
    gs = lax.dynamic_update_slice(jnp.zeros((8, d), F32), gains, (0, spot))
    hbm = pl.BlockSpec(memory_space=pl.ANY)
    moved = ((Z, part, d), BF16)
    td, dt, big, small = ((t, d), BF16), ((d, t), BF16), ((t, d), F32), ((8, d), F32)
    outs = (moved, moved, ((3 * rows, d), F32), small, td, td)

    def boxes(cols, last=Z - 1):
        pair = ((4, 2, rows, cols // 2), BF16)
        one = ((4, rows, cols // 2), BF16)
        return [pair, pair, one, one, ((last, rows, cols), BF16)]

    wm = ((Z, 2, 2, 2, rows, f3), BF16)
    stage = ((Z, rows, d), BF16)
    lse = ((heads, t), F32)
    scratch = [td, td] + [(cosine.shape, F32)] * 2 + [((4, 2, rows, 4 * d), BF16), wm, dt, lse, big]
    scratch += [td, td, td, dt, dt, ((t, 3 * d), BF16), big, lse, small, small, ((10, 8, d), F32), ((10, 8, d), F32), stage]
    scratch += [((2, 2, 2, rows, f3), BF16)] + boxes(f3) + [((4, 2, 2, 2, rows, d), BF16)] + boxes(d)
    return pl.pallas_call(
        layer_kernel,
        out_shape=[jax.ShapeDtypeStruct(s, dt_) for s, dt_ in outs],
        in_specs=[SM, VM] + [hbm] * 6,
        out_specs=[hbm, hbm, hbm, VM, hbm, hbm],
        scratch_shapes=[pltpu.VMEM(s, dt_) for s, dt_ in scratch]
        + [pltpu.SemaphoreType.DMA((144,)), pltpu.SemaphoreType.DMA((144,)), pltpu.SemaphoreType.DMA((16,)), pltpu.SemaphoreType.REGULAR],
        compiler_params=pltpu.CompilerParams(collective_id=0, has_side_effects=True, vmem_limit_bytes=62 * 2**20),
    )(length, gs, was, tokens, cotangent, mlp, cosine, sine)[:4]


def fits(mesh_dp, tokens, w_qkv, w_gate_up):
    tp = lax.axis_size("tp")
    rows, hw = w_qkv.shape[1:]
    return (
        mesh_dp == 8 and tp == Z and tokens.shape[0] == Z and hw == 3 * HEAD and rows % 16 == 0
        and w_gate_up.shape[2] % 256 == 0 and 3 * w_gate_up.shape[2] <= 2 * tokens.shape[2] and tokens.shape[1] % BLK == 0
    )


def body(tokens, lengths, w_qkv, w_out, w_gate_up, w_down, gains, cotangent):
    tp, dp = lax.axis_size("tp"), lax.axis_size("dp")
    batch, part, d = tokens.shape
    n, t = batch // tp, part * tp
    fw = w_gate_up.shape[2]
    cosine, sine = map(jnp.asarray, rope_np(t))
    attn, mlp = pack_weights(w_qkv, w_out, w_gate_up, w_down)
    own = lax.dynamic_slice_in_dim(lengths, lax.axis_index("tp") * n, n)
    if fits(dp, tokens, w_qkv, w_gate_up):
        out, gx, grads, gg = fused_layer(own, tokens, cotangent, attn, mlp, gains, cosine, sine)
        pairs, rows = 2 * HEAD, attn.shape[0]
        s_mlp = jnp.concatenate([grads[:rows], grads[rows : 2 * rows]], axis=1)
        s_attn = grads[2 * rows :]
        first, third = s_attn[:, : 4 * pairs], s_attn[:, 4 * pairs :]
        s_attn = jnp.concatenate([first.reshape(-1, 4, pairs), third.reshape(-1, 4, HEAD)], axis=2)
        spot = (lax.axis_index("dp") * tp + lax.axis_index("tp")) * gains.shape[1]
        s_gains = lax.dynamic_slice(gg, (0, spot), gains.shape)
        gx = gx.astype(F32)
    else:
        full_gains = lax.all_gather(gains, ("dp", "tp"), axis=1, tiled=True)
        full_gains = jnp.pad(full_gains, ((0, 6), (0, 0)))
        x16 = to_sequences(tokens)
        wa = lax.all_gather(attn, "tp", axis=2, tiled=True).reshape(attn.shape[0], 4 * d)
        wa = lax.all_gather(wa, "dp", axis=0, tiled=True).reshape(1, 1, d, 4 * d)
        wm = lax.all_gather(lax.all_gather(mlp, "tp", axis=0), "dp", axis=1, tiled=True).reshape(tp, 1, 1, d, 3 * fw)
        cot16 = to_sequences(cotangent)
        los, gxs, ga, gm, gg = [], [], 0.0, 0.0, 0.0
        for i in range(n):
            lo, gx, a, m, g = one_sequence(own[i : i + 1], x16[i], cot16[i], full_gains, wa, wm, cosine, sine)
            los.append(lo)
            gxs.append(gx)
            ga, gm, gg = ga + a.astype(F32), gm + m.astype(F32), gg + g
        out = to_positions(jnp.stack(los))
        gx = to_positions(jnp.stack(gxs)).astype(F32)
        ga, gm = ga.reshape(d, 4, d), gm.reshape(tp, d, 3 * fw)
        s_mlp = lax.psum_scatter(lax.psum_scatter(gm, "dp", scatter_dimension=1, tiled=True), "tp", scatter_dimension=0)
        s_attn = lax.psum_scatter(ga.reshape(d, 4 * d), "dp", scatter_dimension=0, tiled=True)
        s_attn = lax.psum_scatter(s_attn.reshape(-1, 4, d), "tp", scatter_dimension=2, tiled=True)
        s_gains = lax.psum_scatter(gg, ("dp", "tp"), scatter_dimension=1, tiled=True)
    return (out, gx) + unpack_grads(s_attn, s_mlp, fw) + (s_gains,)


def solution(mesh):
    act = P("dp", "tp", None)
    cols, rows, gain = P(None, "dp", "tp"), P("tp", "dp"), P(None, ("dp", "tp"))
    return jax.shard_map(
        body,
        mesh=mesh,
        in_specs=(act, P("dp"), cols, rows, cols, rows, gain, act),
        out_specs=(act, act, cols, rows, cols, rows, gain),
        check_vma=False,
    )
```

```python
import functools

import numpy as np
import jax
import jax.numpy as jnp
from jax import lax
from jax.experimental import pallas as pl
from jax.experimental.pallas import tpu as pltpu
from jax.sharding import PartitionSpec as P

F32 = jnp.float32
BF16 = jnp.bfloat16
HEAD = 64
EPS = 1e-6
LOG2E = 1.4426950408889634
C2 = LOG2E * HEAD**-0.5
NEG = -1e30
BLK = 256


def dg(a, b, ca, cb):
    return lax.dot_general(a, b, (((ca,), (cb,)), ((), ())), preferred_element_type=F32)


def nn(a, b):
    return dg(a, b, 1, 0)


def nt(a, b):
    return dg(a, b, 1, 1)


def tn(a, b):
    return dg(a, b, 0, 0)


def rows_of(m):
    return pl.ds(pl.multiple_of(m * BLK, BLK), BLK)


def wa_cols(wa_ref, cols):
    part = wa_ref[:, :, :, cols]
    return part.reshape(-1, part.shape[-1])


def half_lane():
    return lax.broadcasted_iota(jnp.int32, (1, 128), 1) % HEAD < HEAD // 2


def head_lane(h):
    lane = lax.broadcasted_iota(jnp.int32, (1, 128), 1)
    return lane < HEAD if h == 0 else lane >= HEAD


def turned(v):
    return jnp.where(half_lane(), pltpu.roll(v, 96, 1), pltpu.roll(v, 32, 1))


def norm_rows(x, gain):
    r = lax.rsqrt(jnp.mean(x * x, axis=-1, keepdims=True) + EPS)
    return x * r, r


def norm_stage(t, x_ref, gains_ref, n1_ref):
    @pl.loop(0, t // BLK)
    def _(m):
        rs = rows_of(m)
        unit, _ = norm_rows(x_ref[rs, :].astype(F32), None)
        n1_ref[rs, :] = (unit * gains_ref[0:1, :]).astype(BF16)


def qkv_stage(t, d, n1_ref, wa_ref, cos_ref, sin_ref, outs):
    for c, out in enumerate(outs):
        if out is None:
            continue

        @pl.loop(0, d // 256)
        def _(j, c=c, out=out):
            cols = pl.ds(pl.multiple_of(c * d + j * 256, 256), 256)
            raw = nn(n1_ref[...], wa_cols(wa_ref, cols))
            for s in range(2):
                part = raw[:, s * 128 : (s + 1) * 128]
                if c < 2:
                    part = part * cos_ref[...] + turned(part) * sin_ref[...]
                out[:, pl.ds(pl.multiple_of(j * 256 + s * 128, 128), 128)] = part.astype(BF16)


def key_bias(t, length):
    pos = lax.broadcasted_iota(jnp.int32, (t, 1), 0)
    return jnp.where(pos < length, 0.0, NEG).astype(BF16)


def causal_block():
    key = lax.broadcasted_iota(jnp.int32, (BLK, BLK), 0)
    query = lax.broadcasted_iota(jnp.int32, (BLK, BLK), 1)
    return key <= query


def score_operands(h, qp, kp, bias):
    mine = head_lane(h)
    lane = lax.broadcasted_iota(jnp.int32, (1, 128), 1)
    spare = lane == (HEAD if h == 0 else 0)
    zero = jnp.zeros((), BF16)
    q_m = jnp.where(mine, qp, zero)
    k_m = jnp.where(mine, kp, zero)
    q_s = jnp.where(spare, jnp.ones((), BF16), q_m)
    k_s = jnp.where(spare, bias, k_m)
    return q_m, k_m, q_s, k_s


def mask_diag(s, i):
    if i == 0:
        return jnp.where(causal_block(), s, NEG)
    return jnp.concatenate([s[: i * BLK], jnp.where(causal_block(), s[i * BLK :], NEG)], axis=0)


def attend_stage(t, d, length, q_ref, k_ref, v_ref, ctxt_ref, lse_ref, first, last):
    bias = key_bias(t, length)

    @pl.loop(first, last)
    def _(p):
        cols = pl.ds(pl.multiple_of(p * 128, 128), 128)
        qp, kp, vp = q_ref[:, cols], k_ref[:, cols], v_ref[:, cols]
        for h in range(2):
            _, _, q_s, k_s = score_operands(h, qp, kp, bias)
            for i in range(t // BLK):
                n = (i + 1) * BLK
                s = mask_diag(nt(k_s[:n], q_s[i * BLK : n]), i)
                top = jnp.max(s, axis=0, keepdims=True)
                e = jnp.exp2((s - top) * C2)
                total = jnp.sum(e, axis=0, keepdims=True)
                o = tn(vp[:n], e.astype(BF16))[h * HEAD : (h + 1) * HEAD] / total
                ctxt_ref[pl.ds(pl.multiple_of(p * 128 + h * HEAD, HEAD), HEAD), i * BLK : n] = o.astype(BF16)
                lse_ref[pl.ds(p * 2 + h, 1), i * BLK : n] = top * C2 + jnp.log2(total)


def out_stage(t, d, length, x_ref, wa_ref, ctxt_ref, hid_ref):
    out = dg(ctxt_ref[...], wa_cols(wa_ref, slice(3 * d, 4 * d)), 0, 1)
    pos = lax.broadcasted_iota(jnp.int32, (t, 1), 0)
    hid_ref[...] = x_ref[...].astype(F32) + jnp.where(pos < length, out, 0.0)


def k1_alone(len_ref, x_ref, gains_ref, wa_ref, cos_ref, sin_ref, q_ref, k_ref, v_ref, ctxt_ref, lse_ref, hid_ref, n1_ref):
    t, d = x_ref.shape
    length = len_ref[0]
    norm_stage(t, x_ref, gains_ref, n1_ref)
    qkv_stage(t, d, n1_ref, wa_ref, cos_ref, sin_ref, (q_ref, k_ref, v_ref))
    attend_stage(t, d, length, q_ref, k_ref, v_ref, ctxt_ref, lse_ref, 0, d // 128)
    out_stage(t, d, length, x_ref, wa_ref, ctxt_ref, hid_ref)


def token_mask(m, length):
    pos = m * BLK + lax.broadcasted_iota(jnp.int32, (BLK, 1), 0)
    return pos < length


def chunk_cols(wm, d, lo, hi):
    return wm[..., lo:hi].reshape(d, hi - lo)


def mlp_front(f, d, wm, n2_ref, dm_ref, wide):
    w = 256
    for j in range(f // w):
        lo, hi = j * w, (j + 1) * w
        gate = nn(n2_ref[...], chunk_cols(wm, d, lo, hi))
        up = nn(n2_ref[...], chunk_cols(wm, d, f + lo, f + hi))
        d_act = nn(dm_ref[...], chunk_cols(wm, d, 2 * f + lo, 2 * f + hi))
        s = 1.0 / (1.0 + jnp.exp2(gate * (-LOG2E)))
        sw = gate * s
        wide[:, 2 * f + lo : 2 * f + hi] = (sw * up).astype(BF16)
        wide[:, lo:hi] = (d_act * up * (s + sw * (1.0 - s))).astype(BF16)
        wide[:, f + lo : f + hi] = (d_act * sw).astype(BF16)


def mlp_out(f, d, wm, n2_ref, wide, mlp_ref):
    w = 256
    for j in range(f // w):
        lo, hi = j * w, (j + 1) * w
        gate = nn(n2_ref[...], chunk_cols(wm, d, lo, hi))
        up = nn(n2_ref[...], chunk_cols(wm, d, f + lo, f + hi))
        wide[:, lo:hi] = (gate * up / (1.0 + jnp.exp2(gate * (-LOG2E)))).astype(BF16)
    mlp_ref[...] += nt(wide[:, :f], chunk_cols(wm, d, 2 * f, 3 * f))


def mlp_back(f, d, wm, n2t_ref, dmt_ref, wide, dn2_ref):
    w = 256
    dn2_ref[...] += nt(wide[:, : 2 * f], chunk_cols(wm, d, 0, 2 * f))
    for j in range(3 * f // w):
        cols = slice(j * w, (j + 1) * w)
        left = n2t_ref if j * w < 2 * f else dmt_ref
        wm[..., cols] = nn(left[...], wide[:, cols]).astype(BF16).reshape(wm.shape[:-1] + (w,))


def k2(len_ref, cot_ref, gains_ref, hid_ref, wm_ref, lo_ref, dh_ref, da_ref, gm_ref, gg_ref,
       n2_ref, dm_ref, n2t_ref, dmt_ref, wide, mlp_ref, dn2_ref):
    t, d = cot_ref.shape
    tp, f = wm_ref.shape[0], wm_ref.shape[-1] // 3
    length = len_ref[0]

    @pl.loop(0, t // BLK)
    def _(m):
        rs = rows_of(m)
        unit, _ = norm_rows(hid_ref[rs, :], None)
        n2 = (unit * gains_ref[1:2, :]).astype(BF16)
        n2_ref[rs, :] = n2
        n2t_ref[:, rs] = n2.T
        dm = jnp.where(token_mask(m, length), cot_ref[rs, :], jnp.zeros((), BF16))
        dm_ref[rs, :] = dm
        dmt_ref[:, rs] = dm.T

    mlp_ref[...] = jnp.zeros_like(mlp_ref)
    dn2_ref[...] = jnp.zeros_like(dn2_ref)

    @pl.loop(0, tp)
    def _(z):
        gm_ref[z] = wm_ref[z]
        mlp_out(f, d, gm_ref.at[z], n2_ref, wide, mlp_ref)
        mlp_front(f, d, gm_ref.at[z], n2_ref, dm_ref, wide)
        mlp_back(f, d, gm_ref.at[z], n2t_ref, dmt_ref, wide, dn2_ref)

    gg_ref[...] = jnp.zeros_like(gg_ref)

    @pl.loop(0, t // BLK)
    def _(m):
        rs = rows_of(m)
        hid = hid_ref[rs, :]
        ok = token_mask(m, length)
        lo_ref[rs, :] = (hid + jnp.where(ok, mlp_ref[rs, :], 0.0)).astype(BF16)
        unit, r = norm_rows(hid, None)
        dn2 = dn2_ref[rs, :]
        gg_ref[...] += jnp.sum(dn2 * unit, axis=0, keepdims=True)
        e2 = dn2 * gains_ref[1:2, :]
        dh = cot_ref[rs, :].astype(F32) + r * (e2 - unit * jnp.mean(e2 * unit, axis=-1, keepdims=True))
        dh_ref[rs, :] = dh
        da_ref[rs, :] = jnp.where(ok, dh, 0.0).astype(BF16)


def attend_back(t, d, length, q_ref, k_ref, v_ref, dctx_ref, lse_ref, dlt_ref, cos_ref, sin_ref, dqkv_ref, dk_acc, dv_acc, first, last):
    bias = key_bias(t, length)

    @pl.loop(first, last)
    def _(p):
        cols = pl.ds(pl.multiple_of(p * 128, 128), 128)
        qp, kp, vp, gp = q_ref[:, cols], k_ref[:, cols], v_ref[:, cols], dctx_ref[:, cols]
        dk_acc[...] = jnp.zeros_like(dk_acc)
        dv_acc[...] = jnp.zeros_like(dv_acc)
        ops = [score_operands(h, qp, kp, bias) for h in range(2)]
        for i in range(t // BLK):
            n = (i + 1) * BLK
            qs = slice(i * BLK, n)
            dq = None
            for h in range(2):
                q_m, k_m, q_s, k_s = ops[h]
                g_m = jnp.where(head_lane(h), gp[qs], jnp.zeros((), BF16))
                s = mask_diag(nt(k_s[:n], q_s[qs]), i)
                pr = jnp.exp2(s * C2 - lse_ref[pl.ds(p * 2 + h, 1), qs])
                dp = nt(vp[:n], g_m)
                ds = (pr * (dp - dlt_ref[pl.ds(p * 2 + h, 1), qs])).astype(BF16)
                dv_acc[:n, :] += nn(pr.astype(BF16), g_m)
                dk_acc[:n, :] += nn(ds, q_m[qs])
                part = tn(ds, k_m[:n])
                dq = part if dq is None else dq + part
            dq = dq * (HEAD**-0.5)
            dqkv_ref[qs, cols] = (dq * cos_ref[qs, :] - turned(dq) * sin_ref[qs, :]).astype(BF16)
        dk = dk_acc[...] * (HEAD**-0.5)
        dqkv_ref[:, pl.ds(pl.multiple_of(d + p * 128, 128), 128)] = (dk * cos_ref[...] - turned(dk) * sin_ref[...]).astype(BF16)
        dqkv_ref[:, pl.ds(pl.multiple_of(2 * d + p * 128, 128), 128)] = dv_acc[...].astype(BF16)


def k3(len_ref, x_ref, gains_ref, wa_ref, cos_ref, sin_ref, q_ref, k_ref, v_ref, ctxt_ref, lse_ref, dh_ref, da_ref,
       gx_ref, ga_ref, gg_ref, n1_ref, n1t_ref, dat_ref, dctx_ref, dlt_ref, dqkv_ref, dk_acc, dv_acc, dn1_ref):
    t, d = x_ref.shape
    length = len_ref[0]

    dat_ref[...] = da_ref[...].T

    @pl.loop(0, d // 256)
    def _(j):
        rs = pl.ds(pl.multiple_of(j * 256, 256), 256)
        cols = pl.ds(pl.multiple_of(3 * d + j * 256, 256), 256)
        ga_ref[:, :, :, cols] = nt(dat_ref[...], ctxt_ref[rs, :]).astype(BF16).reshape(ga_ref.shape[:3] + (256,))
        dctx = nn(da_ref[...], wa_cols(wa_ref, cols)).astype(BF16)
        dctx_ref[:, rs] = dctx
        prod = dctx.T.astype(F32) * ctxt_ref[rs, :].astype(F32)
        for h in range(4):
            dlt_ref[pl.ds(j * 4 + h, 1), :] = jnp.sum(prod[h * HEAD : (h + 1) * HEAD], axis=0, keepdims=True)

    attend_back(t, d, length, q_ref, k_ref, v_ref, dctx_ref, lse_ref, dlt_ref, cos_ref, sin_ref, dqkv_ref, dk_acc, dv_acc, 0, d // 128)

    @pl.loop(0, t // BLK)
    def _(m):
        rs = rows_of(m)
        unit, _ = norm_rows(x_ref[rs, :].astype(F32), None)
        n1t_ref[:, rs] = (unit * gains_ref[0:1, :]).astype(BF16).T

    @pl.loop(0, 3 * d // 256)
    def _(j):
        cols = pl.ds(pl.multiple_of(j * 256, 256), 256)
        ga_ref[:, :, :, cols] = nn(n1t_ref[...], dqkv_ref[:, cols]).astype(BF16).reshape(ga_ref.shape[:3] + (256,))

    dn1_ref[...] = nt(dqkv_ref[...], wa_cols(wa_ref, slice(0, 3 * d)))

    gg_ref[...] = jnp.zeros_like(gg_ref)

    @pl.loop(0, t // BLK)
    def _(m):
        rs = rows_of(m)
        unit, r = norm_rows(x_ref[rs, :].astype(F32), None)
        dn1 = dn1_ref[rs, :]
        gg_ref[...] += jnp.sum(dn1 * unit, axis=0, keepdims=True)
        e1 = dn1 * gains_ref[0:1, :]
        gx_ref[rs, :] = (dh_ref[rs, :] + r * (e1 - unit * jnp.mean(e1 * unit, axis=-1, keepdims=True))).astype(BF16)


def rope_np(t):
    half = HEAD // 2
    freqs = np.float32(10000.0) ** (np.float32(-2.0) * np.arange(half, dtype=np.float32) / np.float32(HEAD))
    ang = np.arange(t, dtype=np.float32)[:, None] * freqs[None, :].astype(np.float32)
    c, s = np.cos(ang), np.sin(ang)
    return np.concatenate([c, c, c, c], 1).astype(np.float32), np.concatenate([-s, s, -s, s], 1).astype(np.float32)


MESH = pl.DeviceIdType.MESH
Z = 4


def flip(d, bit):
    return d + bit - 2 * bit * lax.rem(d // bit, 2)


class Net:
    def __init__(self, send, recv, local):
        self.d, self.z = lax.axis_index("dp"), lax.axis_index("tp")
        self.yx, self.c = self.d // 2, lax.rem(self.d, 2)
        self.x, self.y, self.core = ((flip(self.d, b), self.z) for b in (2, 4, 1))
        self.send, self.recv, self.local = send, recv, local
        self.copies, self.own, self.gone = {}, {}, set()

    def peer(self, r):
        return lax.rem(self.z + r, Z)

    def source(self, r):
        return lax.rem(self.z + Z - r, Z)

    def barrier(self):
        sem = pltpu.get_barrier_semaphore()
        for dev in (self.x, self.y, self.core) + tuple((self.d, self.peer(r)) for r in range(1, Z)):
            pl.semaphore_signal(sem, inc=1, device_id=dev, device_id_type=MESH)
        pl.semaphore_wait(sem, 6)

    def make(self, i, src, dst, dev):
        return pltpu.make_async_remote_copy(
            src_ref=src, dst_ref=dst, send_sem=self.send.at[i], recv_sem=self.recv.at[i], device_id=dev, device_id_type=MESH
        )

    def plan(self, name, src, dst, dev):
        self.copies[name] = self.make(len(self.copies), src, dst, dev)

    def go(self, *names):
        for name in names:
            self.copies[name].start()

    def start(self, name, src, dst, dev):
        self.plan(name, src, dst, dev)
        self.go(name)

    def keep(self, name, src, dst):
        copy = pltpu.make_async_copy(src, dst, self.local.at[len(self.own)])
        copy.start()
        self.own[name] = copy

    def got(self, *names):
        for name in names:
            self.copies[name].wait_recv()

    def kept(self, name):
        self.own[name].wait()

    def left(self, name):
        self.copies[name].wait_send()
        self.gone.add(name)

    def finish(self):
        for name, copy in self.copies.items():
            if name not in self.gone:
                copy.wait_send()


def plan_gather(net, tag, own, slab, halves):
    kx, ky = flip(net.yx, 1), flip(net.yx, 2)
    net.plan(tag + "x", own, slab(net.yx), net.x)
    net.plan(tag + "y", own, slab(net.yx), net.y)
    net.plan(tag + "l", slab(kx).at[:, halves[0]], slab(kx).at[:, halves[0]], net.y)
    net.plan(tag + "r", slab(ky).at[:, halves[1]], slab(ky).at[:, halves[1]], net.x)


def spread(net, tag):
    net.go(tag + "x", tag + "y")


def relay(net, tag):
    net.got(tag + "x")
    net.go(tag + "l")
    net.got(tag + "y")
    net.go(tag + "r")


def all_sum(net, tag, own, boxes, last=False):
    def over_tp(src, out):
        for r in range(1, Z):
            net.start(f"{tag}z{r}", src, boxes.at[r - 1], (net.d, net.peer(r)))
        yield
        net.got(*(f"{tag}z{r}" for r in range(1, Z)))
        boxes[out] = src[...] + (boxes[0] + boxes[1] + boxes[2])

    def over_dp(src, outs):
        for i, (name, dev) in enumerate((("x", net.x), ("y", net.y), ("c", net.core))):
            net.start(tag + name, src, boxes.at[3 + i], dev)
            yield
            net.got(tag + name)
            boxes[outs[i]] = src[...] + boxes[3 + i]
            src = boxes.at[outs[i]]

    if last:
        yield from over_dp(own, (6, 7, 8))
        yield from over_tp(boxes.at[8], 9)
    else:
        yield from over_tp(own, 6)
        yield from over_dp(boxes.at[6], (7, 8, 9))
    yield


def lane_pairs(stage, hw):
    low = lax.broadcasted_iota(jnp.int32, (1, 128), 1) < HEAD
    parts = [[stage[z][:, c * 128 : (c + 1) * 128] for z in range(Z)] for c in range(4)]
    for j in range(Z // 2):
        for g in range(2):
            cols = slice(512 + g * 128, 640 + g * 128)
            a, b = stage[2 * j][:, cols].astype(F32), stage[2 * j + 1][:, cols].astype(F32)
            parts[2 * g].append(jnp.where(low, a, pltpu.roll(b, HEAD, 1)).astype(BF16))
            parts[2 * g + 1].append(jnp.where(low, pltpu.roll(a, HEAD, 1), b).astype(BF16))
    return parts


class Reduce:
    def __init__(self, net, base, data, use, credit, rc, r1x, r1y, r2l, r2r):
        self.net, self.base, self.data, self.use, self.credit = net, base, data, use, credit
        self.rc, self.r1x, self.r1y, self.r2l, self.r2r = rc, r1x, r1y, r2l, r2r
        self.x, self.y = lax.rem(net.yx, 2), net.yx // 2
        half = data.shape[-1] // 2
        self.lo, self.hi = slice(0, half), slice(half, 2 * half)

    def slot(self, i):
        return self.rc.at[lax.rem(self.use(i), 2), :, :, :, 0 : self.data.shape[-1]]

    def copies0(self, g, i):
        return [self.net.make(self.base + i, self.data.at[g, :, :, 1 - self.net.c], self.slot(i), self.net.core)]

    def copies1(self, g, i):
        net, c = self.net, self.net.c
        return [
            net.make(self.base + 4 + i, self.data.at[g, :, 1 - self.x, c, :, self.lo], self.r1x.at[i], net.x),
            net.make(self.base + 8 + i, self.data.at[g, 1 - self.y, :, c, :, self.hi], self.r1y.at[i], net.y),
        ]

    def copies2(self, g, i):
        net, c = self.net, self.net.c
        return [
            net.make(self.base + 12 + i, self.data.at[g, 1 - self.y, self.x, c, :, self.lo], self.r2l.at[i], net.y),
            net.make(self.base + 16 + i, self.data.at[g, self.y, 1 - self.x, c, :, self.hi], self.r2r.at[i], net.x),
        ]

    def add(self, at, value):
        self.data[at] = (self.data[at].astype(F32) + value.astype(F32)).astype(BF16)

    def p0(self, g, i):
        @pl.when(self.use(i) >= 2)
        def _():
            pl.semaphore_wait(self.credit, 1)

        for copy in self.copies0(g, i):
            copy.start()

    def p1(self, g, i):
        for copy in self.copies0(g, i):
            copy.wait_recv()
        for y in range(2):
            for x in range(2):
                self.add((g, y, x, self.net.c), self.slot(i)[y, x])

        @pl.when(self.use(i) < 6)
        def _():
            pl.semaphore_signal(self.credit, inc=1, device_id=self.net.core, device_id_type=MESH)

        for copy in self.copies1(g, i):
            copy.start()

    def p2(self, g, i):
        for copy in self.copies1(g, i):
            copy.wait_recv()
        for k in range(2):
            self.add((g, k, self.x, self.net.c, slice(None), self.lo), self.r1x[i, k])
            self.add((g, self.y, k, self.net.c, slice(None), self.hi), self.r1y[i, k])
        for copy in self.copies2(g, i):
            copy.start()

    def p3(self, g, i):
        for copy in self.copies2(g, i):
            copy.wait_recv()
        self.add((g, self.y, self.x, self.net.c, slice(None), self.lo), self.r2l[i])
        self.add((g, self.y, self.x, self.net.c, slice(None), self.hi), self.r2r[i])

    def own(self, g):
        return self.data.at[g, self.y, self.x, self.net.c]

    def sent(self, g, i):
        for copy in self.copies0(g, i) + self.copies1(g, i) + self.copies2(g, i):
            copy.wait_send()


def packed_thirds(own):
    low = lax.broadcasted_iota(jnp.int32, (1, 128), 1) < HEAD
    for z in range(Z):
        s, u = z % 2, z // 2
        third = [own(2)[:, c * 256 + u * 128 : c * 256 + u * 128 + 128].astype(F32) for c in range(3)]
        third.append(own(3)[:, 512 + u * 128 : 512 + u * 128 + 128].astype(F32))
        for j in range(2):
            a, b = third[2 * j], third[2 * j + 1]
            both = jnp.where(low, a, pltpu.roll(b, HEAD, 1)) if s == 0 else jnp.where(low, pltpu.roll(a, HEAD, 1), b)
            yield z, j, both.astype(BF16)


def layer_kernel(len_ref, gs_ref, was_h, tok_h, cot_h, wms_h, cos_h, sin_h,
                 lo_out, gx_out, grads_out, gg_ref, q_h, k_h, hid_h,
                 x_ref, cot_ref, cos_ref, sin_ref, wa_ref, gm_ref, ctxt_ref, lse_ref, hid_ref,
                 b1, b2, lo_ref, t1, t2, wide, f1, dlt_ref, gains_ref, gsum_ref, boxes_ref, boxes2_ref, pack_ref,
                 mc, mx, my, ml, mr, mz, ga_ref, ax, ay, al, ar, az,
                 send, recv, local, credit):
    t, d = x_ref.shape
    part = t // Z
    f = gm_ref.shape[-1] // 3
    net = Net(send, recv, local)
    z, yx, c = net.z, net.yx, net.c
    length = len_ref[z]
    spot = (net.d * Z + z) * gs_ref.shape[1]
    px, py = lax.rem(yx, 2), yx // 2
    mine = pl.ds(pl.multiple_of(z * part, part), part)
    kd = flip(flip(yx, 1), 2)
    order = ((1, 0, 2, 3), (0, 1, 2, 3), (3, 2, 1, 0), (2, 3, 1, 0))

    def chunk(i):
        if not isinstance(i, int):
            return sum((i == k).astype(jnp.int32) * chunk(k) for k in range(Z))
        return sum((z == k).astype(jnp.int32) * order[k][i] for k in range(Z))

    a_half = (slice(0, 2 * d), slice(2 * d, 4 * d))
    m_half = (slice(0, 3 * f // 2), slice(3 * f // 2, 3 * f))
    a_slab = lambda k: wa_ref.at[k, c]
    m_slab = lambda i: lambda k: gm_ref.at[chunk(i), k // 2, lax.rem(k, 2), c]
    mine_slab = lambda i: m_slab(i)(yx)

    def line(k, right):
        shard = z - (k - 1) if right else z + (k - 1)
        place = gm_ref.at[shard, py, px, c]
        return net.make(76 + 2 * k + right, wms_h if k == 1 else place, place, (net.d, z + 1 if right else z - 1))

    def came(k, right):
        place = gm_ref.at[z - k if right else z + k, py, px, c]
        return net.make(76 + 2 * k + right, place, place, (net.d, z - 1 if right else z + 1))

    def line_go(k):
        pl.when((z >= k - 1) & (z <= Z - 2))(lambda: line(k, 1).start())
        pl.when((z <= Z - k) & (z >= 1))(lambda: line(k, 0).start())

    def line_wait(k):
        pl.when(z >= k)(lambda: came(k, 1).wait_recv())
        pl.when(z <= Z - 1 - k)(lambda: came(k, 0).wait_recv())

    def line_left(k):
        pl.when((z >= k - 1) & (z <= Z - 2))(lambda: line(k, 1).wait_send())
        pl.when((z <= Z - k) & (z >= 1))(lambda: line(k, 0).wait_send())

    def chunk_out(i):
        net.got(f"m{i}l", f"m{i}r")
        net.go(f"m{i}c")

    plan_gather(net, "a", wa_ref.at[yx, c], a_slab, a_half)
    for i in range(Z):
        plan_gather(net, f"m{i}", wms_h if i == 1 else mine_slab(i), m_slab(i), m_half)
        rows = gm_ref.at[chunk(i), :, :, c]
        net.plan(f"m{i}c", rows, rows, net.core)

    gsum_ref[...] = jnp.zeros_like(gsum_ref)
    gsum_ref[0:2, 0 : gs_ref.shape[1]] = gs_ref[...]
    gains_ref[...] = pltpu.roll(gsum_ref[...], spot, 1)
    net.barrier()
    gains_steps = all_sum(net, "g", gains_ref, boxes_ref)
    next(gains_steps)
    for r in range(1, Z):
        net.start(f"az{r}", was_h, pack_ref.at[z], (net.d, net.peer(r)))
    net.keep("a", was_h, pack_ref.at[z])
    net.keep("m", wms_h, gm_ref.at[z, py, px, c])
    net.keep("t", tok_h.at[z], x_ref.at[mine])
    net.keep("c", cot_h.at[z], cot_ref.at[mine])
    net.keep("cos", cos_h, cos_ref)
    net.keep("sin", sin_h, sin_ref)
    next(gains_steps)
    net.got("az1", "az2", "az3")
    line_go(1)
    for r in range(1, Z):
        net.start(f"t{r}", tok_h.at[net.peer(r)], x_ref.at[mine], (net.d, net.peer(r)))
    net.kept("a")
    for i, heads in enumerate(lane_pairs(pack_ref, 4 * d // Z)):
        for j, value in enumerate(heads):
            wa_ref[yx, c, :, i * d + j * 128 : i * d + (j + 1) * 128] = value
    spread(net, "a")
    net.start("ac0", wa_ref.at[yx, c], wa_ref.at[yx, c], net.core)
    for _ in range(3):
        next(gains_steps)
    for r in range(1, Z):
        net.left(f"gz{r}")
    gains_ref[...] = boxes_ref[9]
    relay(net, "a")
    spread(net, "m1")
    net.start("ac1", a_slab(flip(yx, 1)), a_slab(flip(yx, 1)), net.core)
    net.start("ac2", a_slab(flip(yx, 2)), a_slab(flip(yx, 2)), net.core)
    net.got("al", "ar")
    net.start("ac3", a_slab(kd), a_slab(kd), net.core)
    net.kept("m")
    line_wait(1)
    net.got("t1", "t2", "t3")
    net.kept("t")
    line_go(2)
    spread(net, "m0")
    n1_ref = b1
    norm_stage(t, x_ref, gains_ref, n1_ref)
    net.kept("cos")
    net.kept("sin")
    net.got("ac0", "ac1", "ac2", "ac3")

    q_ref, k_ref, v_ref = (wide.at[:, i * d : (i + 1) * d] for i in range(3))
    qkv_stage(t, d, n1_ref, wa_ref, cos_ref, sin_ref, (q_ref, k_ref, v_ref))
    for name, src, dst in (("q", q_ref, q_h), ("k", k_ref, k_h)):
        net.keep(name, src, dst)
    for r in range(1, Z):
        net.start(f"c{r}", cot_h.at[net.peer(r)], cot_ref.at[mine], (net.d, net.peer(r)))
    relay(net, "m1")
    attend = functools.partial(attend_stage, t, d, length, q_ref, k_ref, v_ref, ctxt_ref, lse_ref)
    attend(0, 3)
    line_wait(2)
    line_go(3)
    spread(net, "m2")
    relay(net, "m0")
    chunk_out(1)
    attend(3, d // 128)
    chunk_out(0)
    out_stage(t, d, length, x_ref, wa_ref, ctxt_ref, hid_ref)

    mred = Reduce(net, 86, gm_ref, lambda i: i, credit, mc, mx, my, ml, mr)
    ared = Reduce(net, 106, ga_ref, lambda i: 4 + lax.rem(i + 1, 4), credit, mc, ax, ay, al, ar)

    def mz_copy(w, r):
        return net.make(126 + r, mred.own(w), mz.at[r - 1], (net.d, w))

    def mz_out(i):
        w = chunk(i)
        mz_copy(w, lax.rem(w + Z - z, Z)).start()

    net.keep("hid", hid_ref, hid_h)
    hid_back = pltpu.make_async_copy(hid_h, hid_ref, local.at[15])
    n2_ref, dm_ref, n2t_ref, dmt_ref = b1, b2, t1, t2

    @pl.loop(0, t // BLK)
    def _(m):
        rs = rows_of(m)
        unit, _ = norm_rows(hid_ref[rs, :], None)
        n2 = jnp.where(token_mask(m, length), unit * gains_ref[1:2, :], 0.0).astype(BF16)
        n2_ref[rs, :] = n2
        n2t_ref[:, rs] = n2.T

    def chunk_left(i):
        for tag in ("x", "y", "l", "r", "c"):
            net.left(f"m{i}{tag}")

    def last_shard():
        line_wait(3)
        spread(net, "m3")

    arrived = (
        (lambda: net.got("m1c"),),
        (lambda: relay(net, "m3"), lambda: net.got("m2c")),
        (lambda: net.got("m3c"),),
        (),
    )
    middle = (
        (lambda: line_left(1), lambda: line_left(2), lambda: chunk_out(2)),
        (lambda: line_left(3), lambda: chunk_out(3), lambda: mred.p1(chunk(0), 0)),
        (lambda: mred.p2(chunk(0), 0), lambda: mred.p1(chunk(1), 1)),
        (lambda: mred.p3(chunk(0), 0), lambda: mz_out(0), lambda: mred.p2(chunk(1), 1), lambda: mred.p1(chunk(2), 2)),
    )

    def at(i, steps):
        for k in range(Z):
            if steps[k]:

                @pl.when(i == k)
                def _():
                    for step in steps[k]:
                        step()

    f1[...] = jnp.zeros_like(f1)
    net.kept("hid")
    net.kept("q")
    net.kept("k")
    relay(net, "m2")
    net.got("m0c")
    mlp_out(f, d, gm_ref.at[chunk(0)], n2_ref, wide, hid_ref)
    peer_rows = [rows_of(net.peer(j)) for j in range(Z)]
    for j in range(1, Z):
        net.plan(f"lo{j}", lo_ref.at[peer_rows[j]], lo_out.at[z], (net.d, net.peer(j)))

    @pl.loop(0, Z)
    def _(i):
        at(i, arrived)
        ahead = gm_ref.at[chunk(i + 1)]
        pl.when(i < Z - 1)(lambda: mlp_out(f, d, ahead, n2_ref, wide, hid_ref))

        @pl.when(i == 0)
        def _():
            last_shard()
            net.got("c1", "c2", "c3")
            net.kept("c")

            for m in range(t // BLK):
                rs = slice(m * BLK, (m + 1) * BLK)
                dm = jnp.where(token_mask(m, length), cot_ref[rs, :], jnp.zeros((), BF16))
                dm_ref[rs, :] = dm
                dmt_ref[:, rs] = dm.T

        @pl.when(i == Z - 2)
        def _():
            for j in (2, 1, 3, 0):
                rs = peer_rows[j]
                lo_ref[rs, :] = hid_ref[rs, :].astype(BF16)
                if j:
                    net.go(f"lo{j}")
            hid_back.start()

        gm = gm_ref.at[chunk(i)]
        mlp_front(f, d, gm, n2_ref, dm_ref, wide)
        at(i, middle)
        at(i, tuple((functools.partial(chunk_left, k),) for k in range(Z)))
        mlp_back(f, d, gm, n2t_ref, dmt_ref, wide, f1)
        mred.p0(chunk(i), i)

    net.keep("lo", lo_ref.at[peer_rows[0]], lo_out.at[z])
    for name, src, dst in (("q2", q_h, q_ref), ("k2", k_h, k_ref)):
        net.keep(name, src, dst)
    gsum_ref[...] = jnp.zeros_like(gsum_ref)
    dh_ref, da_ref = hid_ref, b1
    hid_back.wait()

    @pl.loop(0, t // BLK)
    def _(m):
        rs = rows_of(m)
        hid = hid_ref[rs, :]
        ok = token_mask(m, length)
        unit, r = norm_rows(hid, None)
        dn2 = f1[rs, :]
        gsum_ref[1:2, :] += jnp.sum(dn2 * unit, axis=0, keepdims=True)
        e2 = dn2 * gains_ref[1:2, :]
        dh = cot_ref[rs, :].astype(F32) + r * (e2 - unit * jnp.mean(e2 * unit, axis=-1, keepdims=True))
        dh_ref[rs, :] = dh
        da_ref[rs, :] = jnp.where(ok, dh, 0.0).astype(BF16)

    mred.p1(chunk(3), 3)

    dat_ref, n1t_ref, dctx_ref = t1, t2, cot_ref
    dat_ref[...] = da_ref[...].T
    shape = ga_ref.shape[1:5]

    @pl.loop(0, d // 256)
    def _(j):
        rs = pl.ds(pl.multiple_of(j * 256, 256), 256)
        cols = pl.ds(pl.multiple_of(3 * d + j * 256, 256), 256)
        ga_ref[3, :, :, :, :, rs] = nt(dat_ref[...], ctxt_ref[rs, :]).astype(BF16).reshape(shape + (256,))
        dctx = nn(da_ref[...], wa_cols(wa_ref, cols)).astype(BF16)
        dctx_ref[:, rs] = dctx
        prod = dctx.T.astype(F32) * ctxt_ref[rs, :].astype(F32)
        for h in range(4):
            dlt_ref[pl.ds(j * 4 + h, 1), :] = jnp.sum(prod[h * HEAD : (h + 1) * HEAD], axis=0, keepdims=True)

    mred.p2(chunk(2), 2)
    mred.p3(chunk(1), 1)
    ared.p0(3, 3)

    @pl.loop(0, t // BLK)
    def _(m):
        rs = rows_of(m)
        unit, _ = norm_rows(x_ref[rs, :].astype(F32), None)
        n1t_ref[:, rs] = (unit * gains_ref[0:1, :]).astype(BF16).T

    net.kept("q2")
    net.kept("k2")
    dk_acc, dv_acc = f1.at[:, 0:128], f1.at[:, 128:256]
    lanes = dict(o=slice(512 - 128, 512), q=slice(0, 384), t=slice(512, 768))

    def to_owner(base, w, tag):
        r = lax.rem(w + Z - z, Z)

        @pl.when(r != 0)
        def _():
            net.make(base + r - 1, pack_ref.at[w, :, lanes[tag]], az.at[r - 1, :, lanes[tag]], (net.d, w)).start()

    def pack_out():
        for w in range(Z):
            pack_ref[w, :, lanes["o"]] = ared.own(3)[:, w * 128 : w * 128 + 128]
            to_owner(132, w, "o")

    def pack_pairs(g):
        for s in range(2):
            w = 2 * g + s
            for k in range(3):
                pack_ref[w, :, k * 128 : (k + 1) * 128] = ared.own(g)[:, k * 256 + s * 128 : k * 256 + s * 128 + 128]
            to_owner(135, w, "q")

    def pack_thirds():
        for w, j, value in packed_thirds(ared.own):
            pack_ref[w, :, 512 + j * 128 : 640 + j * 128] = value
        for w in range(Z):
            to_owner(138, w, "t")

    def heads_out(g):
        for k in range(3):
            cols = pl.ds(pl.multiple_of(k * d + g * 256, 256), 256)
            ga_ref[g, :, :, :, :, k * 256 : (k + 1) * 256] = nn(n1t_ref[...], wide[:, cols]).astype(BF16).reshape(shape + (256,))
        ared.p0(g, g)

    first = (
        (lambda: ared.p1(3, 3), lambda: mred.p2(chunk(3), 3)),
        (lambda: mred.p3(chunk(3), 3), lambda: mz_out(3), lambda: ared.p1(0, 0)),
        (lambda: ared.p3(0, 0), lambda: pack_pairs(0), lambda: ared.p1(1, 1)),
    )
    second = (
        (lambda: mred.p3(chunk(2), 2), lambda: mz_out(2), lambda: ared.p2(3, 3)),
        (lambda: ared.p3(3, 3), pack_out, lambda: ared.p2(0, 0)),
        (lambda: ared.p2(1, 1),),
    )

    @pl.loop(0, 3)
    def _(g):
        @pl.loop(0, 2)
        def _(s):
            p = 2 * g + s
            attend_back(t, d, length, q_ref, k_ref, v_ref, dctx_ref, lse_ref, dlt_ref, cos_ref, sin_ref, wide, dk_acc, dv_acc, p, p + 1)
            for k in range(3):
                for steps, which in ((first, 0), (second, 1)):

                    @pl.when((g == k) & (s == which))
                    def _():
                        for step in steps[k]:
                            step()

        pl.when(g < 2)(lambda: heads_out(g))

    gx_ref = b1
    for j in (2, 1, 3, 0):
        m = net.peer(j)
        rs = rows_of(m)
        dn1 = nt(wide[rs, :], wa_cols(wa_ref, slice(0, 3 * d)))
        unit, r = norm_rows(x_ref[rs, :].astype(F32), None)
        gsum_ref[0:1, :] += jnp.sum(dn1 * unit, axis=0, keepdims=True)
        e1 = dn1 * gains_ref[0:1, :]
        gx_ref[rs, :] = (dh_ref[rs, :] + r * (e1 - unit * jnp.mean(e1 * unit, axis=-1, keepdims=True))).astype(BF16)
        if j:
            net.start(f"gx{j}", gx_ref.at[rs], gx_out.at[z], (net.d, m))
        else:
            net.keep("gx", gx_ref.at[rs], gx_out.at[z])
        if j == 1:
            ared.p3(1, 1)
            pack_pairs(1)
    heads_out(2)
    steps = all_sum(net, "s", gsum_ref, boxes2_ref, last=True)
    next(steps)
    ared.p1(2, 2)
    next(steps)
    ared.p2(2, 2)
    next(steps)
    ared.p3(2, 2)
    pack_thirds()
    next(steps)
    total = mred.own(z)[...].astype(F32)
    for r in range(1, Z):
        mz_copy(net.peer(r), r).wait_recv()
        total = total + mz[r - 1].astype(F32)
    rows, half = total.shape[0], total.shape[1] // 2
    f1[0:rows, :] = total[:, :half]
    f1[rows : 2 * rows, :] = total[:, half:]

    parts = [
        net.make(base + r - 1, pack_ref.at[net.peer(r), :, lanes[tag]], az.at[r - 1, :, lanes[tag]], (net.d, net.peer(r)))
        for base, tag in ((132, "o"), (135, "q"), (138, "t"))
        for r in range(1, Z)
    ]
    for copy in parts:
        copy.wait_recv()
    total = pack_ref[z].astype(F32)
    for i in range(Z - 1):
        total = total + az[i].astype(F32)
    f1[2 * rows : 3 * rows, :] = total
    net.keep("grads", f1.at[0 : 3 * rows], grads_out)
    next(steps)
    gg_ref[...] = pltpu.roll(boxes2_ref[9], d - spot, 1)[0:2, 0 : gs_ref.shape[1]]
    net.got(*(f"{n}{j}" for n in ("lo", "gx") for j in range(1, Z)))
    for name in ("lo", "gx", "grads"):
        net.kept(name)
    for i in range(Z):
        mred.sent(chunk(i), i)
        ared.sent(i, i)
    for copy in parts:
        copy.wait_send()
    for r in range(1, Z):
        mz_copy(net.peer(r), r).wait_send()
    net.finish()


VM = pl.BlockSpec(memory_space=pltpu.VMEM)
SM = pl.BlockSpec(memory_space=pltpu.SMEM)


def call(kernel, ins, outs, scratch):
    return pl.pallas_call(
        kernel,
        out_shape=[jax.ShapeDtypeStruct(s, dt) for s, dt in outs],
        in_specs=[SM] + [VM] * (len(ins) - 1),
        out_specs=[VM] * len(outs),
        scratch_shapes=[pltpu.VMEM(s, dt) for s, dt in scratch],
        compiler_params=pltpu.CompilerParams(vmem_limit_bytes=60 * 2**20),
    )(*ins)


def backward(length, x, cot, gains, wa, wm, cosine, sine, q, k, v, ctxt, lse, hid):
    t, d = x.shape
    f = wm.shape[-1] // 3
    heads = lse.shape[0]
    td, dt = ((t, d), BF16), ((d, t), BF16)
    lo, dh, da, gm, gg2 = call(
        k2,
        (length, cot, gains, hid, wm),
        (td, ((t, d), F32), td, (wm.shape, BF16), ((1, d), F32)),
        (td, td, dt, dt, ((t, 3 * f), BF16), ((t, d), F32), ((t, d), F32)),
    )
    gx, ga, gg1 = call(
        k3,
        (length, x, gains, wa, cosine, sine, q, k, v, ctxt, lse, dh, da),
        (td, (wa.shape, BF16), ((1, d), F32)),
        (td, dt, dt, td, ((heads, t), F32), ((t, 3 * d), BF16), ((t, 128), F32), ((t, 128), F32), ((t, d), F32)),
    )
    return lo, gx, ga, gm, jnp.concatenate([gg1, gg2])


def one_sequence(length, x, cot, gains, wa, wm, cosine, sine):
    t, d = x.shape
    heads = -(-d // HEAD // 8) * 8
    td, dt = ((t, d), BF16), ((d, t), BF16)
    kept = call(k1_alone, (length, x, gains, wa, cosine, sine), (td, td, td, dt, ((heads, t), F32), ((t, d), F32)), (td,))
    return backward(length, x, cot, gains, wa, wm, cosine, sine, *kept)


def pack_weights(w_qkv, w_out, w_gate_up, w_down):
    attn = jnp.stack([w_qkv[0], w_qkv[1], w_qkv[2], w_out.T], axis=1)
    mlp = jnp.concatenate([w_gate_up[0], w_gate_up[1], w_down.T], axis=1)
    return attn, mlp


def unpack_grads(g_attn, g_mlp, fw):
    g_qkv = jnp.transpose(g_attn[:, :3], (1, 0, 2))
    g_gate_up = jnp.stack([g_mlp[:, i * fw : (i + 1) * fw] for i in range(2)])
    return g_qkv, g_attn[:, 3].T, g_gate_up, g_mlp[:, 2 * fw :].T


def to_sequences(local):
    return lax.all_to_all(local, "tp", split_axis=0, concat_axis=1, tiled=True)


def to_positions(whole):
    return lax.all_to_all(whole, "tp", split_axis=1, concat_axis=0, tiled=True)


def fused_layer(lengths, tokens, cotangent, attn, mlp, gains, cosine, sine):
    batch, part, d = tokens.shape
    t, rows, f3 = part * Z, attn.shape[0], mlp.shape[1]
    heads = -(-d // HEAD // 8) * 8
    pairs = 2 * HEAD
    was = jnp.concatenate(
        [attn[:, :, :pairs].reshape(rows, 4 * pairs), attn[:, :, pairs:].reshape(rows, 4 * HEAD)], axis=1
    )
    hbm = pl.BlockSpec(memory_space=pl.ANY)
    moved = ((Z, part, d), BF16)
    td, dt, big, small = ((t, d), BF16), ((d, t), BF16), ((t, d), F32), ((8, d), F32)
    outs = (moved, moved, ((3 * rows, d), F32), (gains.shape, F32), td, td, big)

    def boxes(cols, last=Z - 1):
        pair = ((4, 2, rows, cols // 2), BF16)
        one = ((4, rows, cols // 2), BF16)
        return [pair, pair, one, one, ((last, rows, cols), BF16)]

    wm = ((Z, 2, 2, 2, rows, f3), BF16)
    stage = ((Z, rows, d), BF16)
    lse = ((heads, t), F32)
    scratch = [td, td] + [(cosine.shape, F32)] * 2 + [((4, 2, rows, 4 * d), BF16), wm, dt, lse, big]
    scratch += [td, td, td, dt, dt, ((t, 3 * d), BF16), big, lse, small, small, ((10, 8, d), F32), ((10, 8, d), F32), stage]
    scratch += [((2, 2, 2, rows, f3), BF16)] + boxes(f3) + [((4, 2, 2, 2, rows, d), BF16)] + boxes(d)
    return pl.pallas_call(
        layer_kernel,
        out_shape=[jax.ShapeDtypeStruct(s, dt_) for s, dt_ in outs],
        in_specs=[SM, VM] + [hbm] * 6,
        out_specs=[hbm, hbm, hbm, VM, hbm, hbm, hbm],
        scratch_shapes=[pltpu.VMEM(s, dt_) for s, dt_ in scratch]
        + [pltpu.SemaphoreType.DMA((144,)), pltpu.SemaphoreType.DMA((144,)), pltpu.SemaphoreType.DMA((16,)), pltpu.SemaphoreType.REGULAR],
        compiler_params=pltpu.CompilerParams(collective_id=0, has_side_effects=True, vmem_limit_bytes=62 * 2**20),
    )(lengths, gains, was, tokens, cotangent, mlp, cosine, sine)[:4]


def fits(mesh_dp, tokens, w_qkv, w_gate_up):
    tp = lax.axis_size("tp")
    rows, hw = w_qkv.shape[1:]
    return (
        mesh_dp == 8 and tp == Z and tokens.shape[0] == Z and hw == 3 * HEAD and rows % 16 == 0
        and w_gate_up.shape[2] % 256 == 0 and 3 * w_gate_up.shape[2] <= 2 * tokens.shape[2] and tokens.shape[1] % BLK == 0
    )


def body(tokens, lengths, w_qkv, w_out, w_gate_up, w_down, gains, cotangent):
    tp, dp = lax.axis_size("tp"), lax.axis_size("dp")
    batch, part, d = tokens.shape
    n, t = batch // tp, part * tp
    fw = w_gate_up.shape[2]
    cosine, sine = map(jnp.asarray, rope_np(t))
    attn, mlp = pack_weights(w_qkv, w_out, w_gate_up, w_down)
    own = lax.dynamic_slice_in_dim(lengths, lax.axis_index("tp") * n, n)
    if fits(dp, tokens, w_qkv, w_gate_up):
        out, gx, grads, s_gains = fused_layer(lengths, tokens, cotangent, attn, mlp, gains, cosine, sine)
        pairs, rows = 2 * HEAD, attn.shape[0]
        s_mlp = jnp.concatenate([grads[:rows], grads[rows : 2 * rows]], axis=1)
        s_attn = grads[2 * rows :]
        first, third = s_attn[:, : 4 * pairs], s_attn[:, 4 * pairs :]
        s_attn = jnp.concatenate([first.reshape(-1, 4, pairs), third.reshape(-1, 4, HEAD)], axis=2)
        gx = gx.astype(F32)
    else:
        full_gains = lax.all_gather(gains, ("dp", "tp"), axis=1, tiled=True)
        full_gains = jnp.pad(full_gains, ((0, 6), (0, 0)))
        x16 = to_sequences(tokens)
        wa = lax.all_gather(attn, "tp", axis=2, tiled=True).reshape(attn.shape[0], 4 * d)
        wa = lax.all_gather(wa, "dp", axis=0, tiled=True).reshape(1, 1, d, 4 * d)
        wm = lax.all_gather(lax.all_gather(mlp, "tp", axis=0), "dp", axis=1, tiled=True).reshape(tp, 1, 1, d, 3 * fw)
        cot16 = to_sequences(cotangent)
        los, gxs, ga, gm, gg = [], [], 0.0, 0.0, 0.0
        for i in range(n):
            lo, gx, a, m, g = one_sequence(own[i : i + 1], x16[i], cot16[i], full_gains, wa, wm, cosine, sine)
            los.append(lo)
            gxs.append(gx)
            ga, gm, gg = ga + a.astype(F32), gm + m.astype(F32), gg + g
        out = to_positions(jnp.stack(los))
        gx = to_positions(jnp.stack(gxs)).astype(F32)
        ga, gm = ga.reshape(d, 4, d), gm.reshape(tp, d, 3 * fw)
        s_mlp = lax.psum_scatter(lax.psum_scatter(gm, "dp", scatter_dimension=1, tiled=True), "tp", scatter_dimension=0)
        s_attn = lax.psum_scatter(ga.reshape(d, 4 * d), "dp", scatter_dimension=0, tiled=True)
        s_attn = lax.psum_scatter(s_attn.reshape(-1, 4, d), "tp", scatter_dimension=2, tiled=True)
        s_gains = lax.psum_scatter(gg, ("dp", "tp"), scatter_dimension=1, tiled=True)
    return (out, gx) + unpack_grads(s_attn, s_mlp, fw) + (s_gains,)


def solution(mesh):
    act = P("dp", "tp", None)
    cols, rows, gain = P(None, "dp", "tp"), P("tp", "dp"), P(None, ("dp", "tp"))
    return jax.shard_map(
        body,
        mesh=mesh,
        in_specs=(act, P("dp"), cols, rows, cols, rows, gain, act),
        out_specs=(act, act, cols, rows, cols, rows, gain),
        check_vma=False,
    )
```

```python
import functools

import numpy as np
import jax
import jax.numpy as jnp
from jax import lax
from jax.experimental import pallas as pl
from jax.experimental.pallas import tpu as pltpu
from jax.sharding import PartitionSpec as P

F32 = jnp.float32
BF16 = jnp.bfloat16
HEAD = 64
EPS = 1e-6
LOG2E = 1.4426950408889634
C2 = LOG2E * HEAD**-0.5
NEG = -1e30
BLK = 256


def dg(a, b, ca, cb):
    return lax.dot_general(a, b, (((ca,), (cb,)), ((), ())), preferred_element_type=F32)


def nn(a, b):
    return dg(a, b, 1, 0)


def nt(a, b):
    return dg(a, b, 1, 1)


def tn(a, b):
    return dg(a, b, 0, 0)


def rows_of(m):
    return pl.ds(pl.multiple_of(m * BLK, BLK), BLK)


def wa_cols(wa_ref, cols):
    part = wa_ref[:, :, :, cols]
    return part.reshape(-1, part.shape[-1])


def half_lane():
    return lax.broadcasted_iota(jnp.int32, (1, 128), 1) % HEAD < HEAD // 2


def head_lane(h):
    lane = lax.broadcasted_iota(jnp.int32, (1, 128), 1)
    return lane < HEAD if h == 0 else lane >= HEAD


def turned(v):
    return jnp.where(half_lane(), pltpu.roll(v, 96, 1), pltpu.roll(v, 32, 1))


def norm_rows(x, gain):
    r = lax.rsqrt(jnp.mean(x * x, axis=-1, keepdims=True) + EPS)
    return x * r, r


def norm_stage(t, x_ref, gains_ref, n1_ref):
    @pl.loop(0, t // BLK)
    def _(m):
        rs = rows_of(m)
        unit, _ = norm_rows(x_ref[rs, :].astype(F32), None)
        n1_ref[rs, :] = (unit * gains_ref[0:1, :]).astype(BF16)


def qkv_stage(t, d, n1_ref, wa_ref, cos_ref, sin_ref, outs):
    for c, out in enumerate(outs):
        if out is None:
            continue

        @pl.loop(0, d // 256)
        def _(j, c=c, out=out):
            cols = pl.ds(pl.multiple_of(c * d + j * 256, 256), 256)
            raw = nn(n1_ref[...], wa_cols(wa_ref, cols))
            for s in range(2):
                part = raw[:, s * 128 : (s + 1) * 128]
                if c < 2:
                    part = part * cos_ref[...] + turned(part) * sin_ref[...]
                out[:, pl.ds(pl.multiple_of(j * 256 + s * 128, 128), 128)] = part.astype(BF16)


def key_bias(t, length):
    pos = lax.broadcasted_iota(jnp.int32, (t, 1), 0)
    return jnp.where(pos < length, 0.0, NEG).astype(BF16)


def causal_block():
    key = lax.broadcasted_iota(jnp.int32, (BLK, BLK), 0)
    query = lax.broadcasted_iota(jnp.int32, (BLK, BLK), 1)
    return key <= query


def score_operands(h, qp, kp, bias):
    mine = head_lane(h)
    lane = lax.broadcasted_iota(jnp.int32, (1, 128), 1)
    spare = lane == (HEAD if h == 0 else 0)
    zero = jnp.zeros((), BF16)
    q_m = jnp.where(mine, qp, zero)
    k_m = jnp.where(mine, kp, zero)
    q_s = jnp.where(spare, jnp.ones((), BF16), q_m)
    k_s = jnp.where(spare, bias, k_m)
    return q_m, k_m, q_s, k_s


def mask_diag(s, i):
    if i == 0:
        return jnp.where(causal_block(), s, NEG)
    return jnp.concatenate([s[: i * BLK], jnp.where(causal_block(), s[i * BLK :], NEG)], axis=0)


def attend_stage(t, d, length, q_ref, k_ref, v_ref, ctxt_ref, lse_ref, first, last):
    bias = key_bias(t, length)

    @pl.loop(first, last)
    def _(p):
        cols = pl.ds(pl.multiple_of(p * 128, 128), 128)
        qp, kp, vp = q_ref[:, cols], k_ref[:, cols], v_ref[:, cols]
        for h in range(2):
            _, _, q_s, k_s = score_operands(h, qp, kp, bias)
            for i in range(t // BLK):
                n = (i + 1) * BLK
                s = mask_diag(nt(k_s[:n], q_s[i * BLK : n]), i)
                top = jnp.max(s, axis=0, keepdims=True)
                e = jnp.exp2((s - top) * C2)
                total = jnp.sum(e, axis=0, keepdims=True)
                o = tn(vp[:n], e.astype(BF16))[h * HEAD : (h + 1) * HEAD] / total
                ctxt_ref[pl.ds(pl.multiple_of(p * 128 + h * HEAD, HEAD), HEAD), i * BLK : n] = o.astype(BF16)
                lse_ref[pl.ds(p * 2 + h, 1), i * BLK : n] = top * C2 + jnp.log2(total)


def out_stage(t, d, length, x_ref, wa_ref, ctxt_ref, hid_ref):
    out = dg(ctxt_ref[...], wa_cols(wa_ref, slice(3 * d, 4 * d)), 0, 1)
    pos = lax.broadcasted_iota(jnp.int32, (t, 1), 0)
    hid_ref[...] = x_ref[...].astype(F32) + jnp.where(pos < length, out, 0.0)


def k1_alone(len_ref, x_ref, gains_ref, wa_ref, cos_ref, sin_ref, q_ref, k_ref, v_ref, ctxt_ref, lse_ref, hid_ref, n1_ref):
    t, d = x_ref.shape
    length = len_ref[0]
    norm_stage(t, x_ref, gains_ref, n1_ref)
    qkv_stage(t, d, n1_ref, wa_ref, cos_ref, sin_ref, (q_ref, k_ref, v_ref))
    attend_stage(t, d, length, q_ref, k_ref, v_ref, ctxt_ref, lse_ref, 0, d // 128)
    out_stage(t, d, length, x_ref, wa_ref, ctxt_ref, hid_ref)


def token_mask(m, length):
    pos = m * BLK + lax.broadcasted_iota(jnp.int32, (BLK, 1), 0)
    return pos < length


def chunk_cols(wm, d, lo, hi):
    return wm[..., lo:hi].reshape(d, hi - lo)


def mlp_front(f, d, wm, n2_ref, dm_ref, wide):
    w = 256
    for j in range(f // w):
        lo, hi = j * w, (j + 1) * w
        gate = nn(n2_ref[...], chunk_cols(wm, d, lo, hi))
        up = nn(n2_ref[...], chunk_cols(wm, d, f + lo, f + hi))
        d_act = nn(dm_ref[...], chunk_cols(wm, d, 2 * f + lo, 2 * f + hi))
        s = 1.0 / (1.0 + jnp.exp2(gate * (-LOG2E)))
        sw = gate * s
        wide[:, 2 * f + lo : 2 * f + hi] = (sw * up).astype(BF16)
        wide[:, lo:hi] = (d_act * up * (s + sw * (1.0 - s))).astype(BF16)
        wide[:, f + lo : f + hi] = (d_act * sw).astype(BF16)


def mlp_out(f, d, wm, n2_ref, wide, mlp_ref):
    w = 256
    for j in range(f // w):
        lo, hi = j * w, (j + 1) * w
        gate = nn(n2_ref[...], chunk_cols(wm, d, lo, hi))
        up = nn(n2_ref[...], chunk_cols(wm, d, f + lo, f + hi))
        wide[:, lo:hi] = (gate * up / (1.0 + jnp.exp2(gate * (-LOG2E)))).astype(BF16)
    mlp_ref[...] += nt(wide[:, :f], chunk_cols(wm, d, 2 * f, 3 * f))


def mlp_back(f, d, wm, n2t_ref, dmt_ref, wide, dn2_ref):
    w = 256
    dn2_ref[...] += nt(wide[:, : 2 * f], chunk_cols(wm, d, 0, 2 * f))
    for j in range(3 * f // w):
        cols = slice(j * w, (j + 1) * w)
        left = n2t_ref if j * w < 2 * f else dmt_ref
        wm[..., cols] = nn(left[...], wide[:, cols]).astype(BF16).reshape(wm.shape[:-1] + (w,))


def k2(len_ref, cot_ref, gains_ref, hid_ref, wm_ref, lo_ref, dh_ref, da_ref, gm_ref, gg_ref,
       n2_ref, dm_ref, n2t_ref, dmt_ref, wide, mlp_ref, dn2_ref):
    t, d = cot_ref.shape
    tp, f = wm_ref.shape[0], wm_ref.shape[-1] // 3
    length = len_ref[0]

    @pl.loop(0, t // BLK)
    def _(m):
        rs = rows_of(m)
        unit, _ = norm_rows(hid_ref[rs, :], None)
        n2 = (unit * gains_ref[1:2, :]).astype(BF16)
        n2_ref[rs, :] = n2
        n2t_ref[:, rs] = n2.T
        dm = jnp.where(token_mask(m, length), cot_ref[rs, :], jnp.zeros((), BF16))
        dm_ref[rs, :] = dm
        dmt_ref[:, rs] = dm.T

    mlp_ref[...] = jnp.zeros_like(mlp_ref)
    dn2_ref[...] = jnp.zeros_like(dn2_ref)

    @pl.loop(0, tp)
    def _(z):
        gm_ref[z] = wm_ref[z]
        mlp_out(f, d, gm_ref.at[z], n2_ref, wide, mlp_ref)
        mlp_front(f, d, gm_ref.at[z], n2_ref, dm_ref, wide)
        mlp_back(f, d, gm_ref.at[z], n2t_ref, dmt_ref, wide, dn2_ref)

    gg_ref[...] = jnp.zeros_like(gg_ref)

    @pl.loop(0, t // BLK)
    def _(m):
        rs = rows_of(m)
        hid = hid_ref[rs, :]
        ok = token_mask(m, length)
        lo_ref[rs, :] = (hid + jnp.where(ok, mlp_ref[rs, :], 0.0)).astype(BF16)
        unit, r = norm_rows(hid, None)
        dn2 = dn2_ref[rs, :]
        gg_ref[...] += jnp.sum(dn2 * unit, axis=0, keepdims=True)
        e2 = dn2 * gains_ref[1:2, :]
        dh = cot_ref[rs, :].astype(F32) + r * (e2 - unit * jnp.mean(e2 * unit, axis=-1, keepdims=True))
        dh_ref[rs, :] = dh
        da_ref[rs, :] = jnp.where(ok, dh, 0.0).astype(BF16)


def attend_back(t, d, length, q_ref, k_ref, v_ref, dctx_ref, lse_ref, dlt_ref, cos_ref, sin_ref, dqkv_ref, dk_acc, dv_acc, first, last):
    bias = key_bias(t, length)

    @pl.loop(first, last)
    def _(p):
        cols = pl.ds(pl.multiple_of(p * 128, 128), 128)
        qp, kp, vp, gp = q_ref[:, cols], k_ref[:, cols], v_ref[:, cols], dctx_ref[:, cols]
        dk_acc[...] = jnp.zeros_like(dk_acc)
        dv_acc[...] = jnp.zeros_like(dv_acc)
        ops = [score_operands(h, qp, kp, bias) for h in range(2)]
        for i in range(t // BLK):
            n = (i + 1) * BLK
            qs = slice(i * BLK, n)
            dq = None
            for h in range(2):
                q_m, k_m, q_s, k_s = ops[h]
                g_m = jnp.where(head_lane(h), gp[qs], jnp.zeros((), BF16))
                s = mask_diag(nt(k_s[:n], q_s[qs]), i)
                pr = jnp.exp2(s * C2 - lse_ref[pl.ds(p * 2 + h, 1), qs])
                dp = nt(vp[:n], g_m)
                ds = (pr * (dp - dlt_ref[pl.ds(p * 2 + h, 1), qs])).astype(BF16)
                dv_acc[:n, :] += nn(pr.astype(BF16), g_m)
                dk_acc[:n, :] += nn(ds, q_m[qs])
                part = tn(ds, k_m[:n])
                dq = part if dq is None else dq + part
            dq = dq * (HEAD**-0.5)
            dqkv_ref[qs, cols] = (dq * cos_ref[qs, :] - turned(dq) * sin_ref[qs, :]).astype(BF16)
        dk = dk_acc[...] * (HEAD**-0.5)
        dqkv_ref[:, pl.ds(pl.multiple_of(d + p * 128, 128), 128)] = (dk * cos_ref[...] - turned(dk) * sin_ref[...]).astype(BF16)
        dqkv_ref[:, pl.ds(pl.multiple_of(2 * d + p * 128, 128), 128)] = dv_acc[...].astype(BF16)


def k3(len_ref, x_ref, gains_ref, wa_ref, cos_ref, sin_ref, q_ref, k_ref, v_ref, ctxt_ref, lse_ref, dh_ref, da_ref,
       gx_ref, ga_ref, gg_ref, n1_ref, n1t_ref, dat_ref, dctx_ref, dlt_ref, dqkv_ref, dk_acc, dv_acc, dn1_ref):
    t, d = x_ref.shape
    length = len_ref[0]

    dat_ref[...] = da_ref[...].T

    @pl.loop(0, d // 256)
    def _(j):
        rs = pl.ds(pl.multiple_of(j * 256, 256), 256)
        cols = pl.ds(pl.multiple_of(3 * d + j * 256, 256), 256)
        ga_ref[:, :, :, cols] = nt(dat_ref[...], ctxt_ref[rs, :]).astype(BF16).reshape(ga_ref.shape[:3] + (256,))
        dctx = nn(da_ref[...], wa_cols(wa_ref, cols)).astype(BF16)
        dctx_ref[:, rs] = dctx
        prod = dctx.T.astype(F32) * ctxt_ref[rs, :].astype(F32)
        for h in range(4):
            dlt_ref[pl.ds(j * 4 + h, 1), :] = jnp.sum(prod[h * HEAD : (h + 1) * HEAD], axis=0, keepdims=True)

    attend_back(t, d, length, q_ref, k_ref, v_ref, dctx_ref, lse_ref, dlt_ref, cos_ref, sin_ref, dqkv_ref, dk_acc, dv_acc, 0, d // 128)

    @pl.loop(0, t // BLK)
    def _(m):
        rs = rows_of(m)
        unit, _ = norm_rows(x_ref[rs, :].astype(F32), None)
        n1t_ref[:, rs] = (unit * gains_ref[0:1, :]).astype(BF16).T

    @pl.loop(0, 3 * d // 256)
    def _(j):
        cols = pl.ds(pl.multiple_of(j * 256, 256), 256)
        ga_ref[:, :, :, cols] = nn(n1t_ref[...], dqkv_ref[:, cols]).astype(BF16).reshape(ga_ref.shape[:3] + (256,))

    dn1_ref[...] = nt(dqkv_ref[...], wa_cols(wa_ref, slice(0, 3 * d)))

    gg_ref[...] = jnp.zeros_like(gg_ref)

    @pl.loop(0, t // BLK)
    def _(m):
        rs = rows_of(m)
        unit, r = norm_rows(x_ref[rs, :].astype(F32), None)
        dn1 = dn1_ref[rs, :]
        gg_ref[...] += jnp.sum(dn1 * unit, axis=0, keepdims=True)
        e1 = dn1 * gains_ref[0:1, :]
        gx_ref[rs, :] = (dh_ref[rs, :] + r * (e1 - unit * jnp.mean(e1 * unit, axis=-1, keepdims=True))).astype(BF16)


def rope_np(t):
    half = HEAD // 2
    freqs = np.float32(10000.0) ** (np.float32(-2.0) * np.arange(half, dtype=np.float32) / np.float32(HEAD))
    ang = np.arange(t, dtype=np.float32)[:, None] * freqs[None, :].astype(np.float32)
    c, s = np.cos(ang), np.sin(ang)
    return np.concatenate([c, c, c, c], 1).astype(np.float32), np.concatenate([-s, s, -s, s], 1).astype(np.float32)


MESH = pl.DeviceIdType.MESH
Z = 4
PAIRS = (0, 2, 1, 3)


def flip(d, bit):
    return d + bit - 2 * bit * lax.rem(d // bit, 2)


class Net:
    def __init__(self, send, recv, local):
        self.d, self.z = lax.axis_index("dp"), lax.axis_index("tp")
        self.yx, self.c = self.d // 2, lax.rem(self.d, 2)
        self.x, self.y, self.core = ((flip(self.d, b), self.z) for b in (2, 4, 1))
        self.send, self.recv, self.local = send, recv, local
        self.copies, self.own, self.gone = {}, {}, set()

    def peer(self, r):
        return lax.rem(self.z + r, Z)

    def source(self, r):
        return lax.rem(self.z + Z - r, Z)

    def barrier(self):
        sem = pltpu.get_barrier_semaphore()
        for dev in (self.x, self.y, self.core) + tuple((self.d, self.peer(r)) for r in range(1, Z)):
            pl.semaphore_signal(sem, inc=1, device_id=dev, device_id_type=MESH)
        pl.semaphore_wait(sem, 6)

    def make(self, i, src, dst, dev):
        return pltpu.make_async_remote_copy(
            src_ref=src, dst_ref=dst, send_sem=self.send.at[i], recv_sem=self.recv.at[i], device_id=dev, device_id_type=MESH
        )

    def plan(self, name, src, dst, dev):
        self.copies[name] = self.make(len(self.copies), src, dst, dev)

    def go(self, *names):
        for name in names:
            self.copies[name].start()

    def start(self, name, src, dst, dev):
        self.plan(name, src, dst, dev)
        self.go(name)

    def keep(self, name, src, dst):
        copy = pltpu.make_async_copy(src, dst, self.local.at[len(self.own)])
        copy.start()
        self.own[name] = copy

    def got(self, *names):
        for name in names:
            self.copies[name].wait_recv()

    def kept(self, name):
        self.own[name].wait()

    def left(self, name):
        self.copies[name].wait_send()
        self.gone.add(name)

    def finish(self):
        for name, copy in self.copies.items():
            if name not in self.gone:
                copy.wait_send()


def plan_gather(net, tag, own, slab, halves):
    kx, ky = flip(net.yx, 1), flip(net.yx, 2)
    net.plan(tag + "x", own, slab(net.yx), net.x)
    net.plan(tag + "y", own, slab(net.yx), net.y)
    net.plan(tag + "l", slab(kx).at[:, halves[0]], slab(kx).at[:, halves[0]], net.y)
    net.plan(tag + "r", slab(ky).at[:, halves[1]], slab(ky).at[:, halves[1]], net.x)


def spread(net, tag):
    net.go(tag + "x", tag + "y")


def relay(net, tag):
    net.got(tag + "x")
    net.go(tag + "l")
    net.got(tag + "y")
    net.go(tag + "r")


def all_sum(net, tag, own, boxes, last=False):
    def over_tp(src, out):
        for r in range(1, Z):
            net.start(f"{tag}z{r}", src, boxes.at[r - 1], (net.d, net.peer(r)))
        yield
        net.got(*(f"{tag}z{r}" for r in range(1, Z)))
        boxes[out] = src[...] + (boxes[0] + boxes[1] + boxes[2])

    def over_dp(src, outs):
        for i, (name, dev) in enumerate((("x", net.x), ("y", net.y), ("c", net.core))):
            net.start(tag + name, src, boxes.at[3 + i], dev)
            yield
            net.got(tag + name)
            boxes[outs[i]] = src[...] + boxes[3 + i]
            src = boxes.at[outs[i]]

    if last:
        yield from over_dp(own, (6, 7, 8))
        yield from over_tp(boxes.at[8], 9)
    else:
        yield from over_tp(own, 6)
        yield from over_dp(boxes.at[6], (7, 8, 9))
    yield


def lane_pairs(stage, hw):
    low = lax.broadcasted_iota(jnp.int32, (1, 128), 1) < HEAD
    parts = [[stage[z][:, c * 128 : (c + 1) * 128] for z in PAIRS] for c in range(4)]
    for j in range(Z // 2):
        for g in range(2):
            cols = slice(512 + g * 128, 640 + g * 128)
            a, b = stage[2 * j][:, cols].astype(F32), stage[2 * j + 1][:, cols].astype(F32)
            parts[2 * g].append(jnp.where(low, a, pltpu.roll(b, HEAD, 1)).astype(BF16))
            parts[2 * g + 1].append(jnp.where(low, pltpu.roll(a, HEAD, 1), b).astype(BF16))
    return parts


class Reduce:
    def __init__(self, net, base, data, use, credit, rc, r1x, r1y, r2l, r2r):
        self.net, self.base, self.data, self.use, self.credit = net, base, data, use, credit
        self.rc, self.r1x, self.r1y, self.r2l, self.r2r = rc, r1x, r1y, r2l, r2r
        self.x, self.y = lax.rem(net.yx, 2), net.yx // 2
        half = data.shape[-1] // 2
        self.lo, self.hi = slice(0, half), slice(half, 2 * half)

    def slot(self, i):
        return self.rc.at[lax.rem(self.use(i), 2), :, :, :, 0 : self.data.shape[-1]]

    def copies0(self, g, i):
        return [self.net.make(self.base + i, self.data.at[g, :, :, 1 - self.net.c], self.slot(i), self.net.core)]

    def copies1(self, g, i):
        net, c = self.net, self.net.c
        return [
            net.make(self.base + 4 + i, self.data.at[g, :, 1 - self.x, c, :, self.lo], self.r1x.at[i], net.x),
            net.make(self.base + 8 + i, self.data.at[g, 1 - self.y, :, c, :, self.hi], self.r1y.at[i], net.y),
        ]

    def copies2(self, g, i):
        net, c = self.net, self.net.c
        return [
            net.make(self.base + 12 + i, self.data.at[g, 1 - self.y, self.x, c, :, self.lo], self.r2l.at[i], net.y),
            net.make(self.base + 16 + i, self.data.at[g, self.y, 1 - self.x, c, :, self.hi], self.r2r.at[i], net.x),
        ]

    def add(self, at, value):
        self.data[at] = (self.data[at].astype(F32) + value.astype(F32)).astype(BF16)

    def p0(self, g, i):
        @pl.when(self.use(i) >= 2)
        def _():
            pl.semaphore_wait(self.credit, 1)

        for copy in self.copies0(g, i):
            copy.start()

    def p1(self, g, i):
        for copy in self.copies0(g, i):
            copy.wait_recv()
        for y in range(2):
            for x in range(2):
                self.add((g, y, x, self.net.c), self.slot(i)[y, x])

        @pl.when(self.use(i) < 6)
        def _():
            pl.semaphore_signal(self.credit, inc=1, device_id=self.net.core, device_id_type=MESH)

        for copy in self.copies1(g, i):
            copy.start()

    def p2(self, g, i):
        for copy in self.copies1(g, i):
            copy.wait_recv()
        for k in range(2):
            self.add((g, k, self.x, self.net.c, slice(None), self.lo), self.r1x[i, k])
            self.add((g, self.y, k, self.net.c, slice(None), self.hi), self.r1y[i, k])
        for copy in self.copies2(g, i):
            copy.start()

    def p3(self, g, i):
        for copy in self.copies2(g, i):
            copy.wait_recv()
        self.add((g, self.y, self.x, self.net.c, slice(None), self.lo), self.r2l[i])
        self.add((g, self.y, self.x, self.net.c, slice(None), self.hi), self.r2r[i])

    def own(self, g):
        return self.data.at[g, self.y, self.x, self.net.c]

    def sent(self, g, i):
        for copy in self.copies0(g, i) + self.copies1(g, i) + self.copies2(g, i):
            copy.wait_send()


def packed_thirds(own):
    low = lax.broadcasted_iota(jnp.int32, (1, 128), 1) < HEAD
    for z in range(Z):
        s, u = z % 2, z // 2
        third = [own(2)[:, c * 256 + u * 128 : c * 256 + u * 128 + 128].astype(F32) for c in range(3)]
        third.append(own(3)[:, 512 + u * 128 : 512 + u * 128 + 128].astype(F32))
        for j in range(2):
            a, b = third[2 * j], third[2 * j + 1]
            both = jnp.where(low, a, pltpu.roll(b, HEAD, 1)) if s == 0 else jnp.where(low, pltpu.roll(a, HEAD, 1), b)
            yield z, j, both.astype(BF16)


def layer_kernel(len_ref, gs_ref, was_h, tok_h, cot_h, wms_h, cos_h, sin_h,
                 lo_out, gx_out, grads_out, gg_ref, q_h, k_h, hid_h,
                 x_ref, cot_ref, cos_ref, sin_ref, wa_ref, gm_ref, ctxt_ref, lse_ref, hid_ref,
                 b1, b2, lo_ref, t1, t2, wide, f1, dlt_ref, gains_ref, gsum_ref, boxes_ref, boxes2_ref, pack_ref,
                 mc, mx, my, ml, mr, mz, ga_ref, ax, ay, al, ar, az,
                 send, recv, local, credit):
    t, d = x_ref.shape
    part = t // Z
    f = gm_ref.shape[-1] // 3
    net = Net(send, recv, local)
    z, yx, c = net.z, net.yx, net.c
    length = len_ref[z]
    spot = (net.d * Z + z) * gs_ref.shape[1]
    px, py = lax.rem(yx, 2), yx // 2
    mine = pl.ds(pl.multiple_of(z * part, part), part)
    kd = flip(flip(yx, 1), 2)
    order = ((1, 0, 2, 3), (0, 1, 2, 3), (3, 2, 1, 0), (2, 3, 1, 0))

    def chunk(i):
        if not isinstance(i, int):
            return sum((i == k).astype(jnp.int32) * chunk(k) for k in range(Z))
        return sum((z == k).astype(jnp.int32) * order[k][i] for k in range(Z))

    a_half = (slice(0, 2 * d), slice(2 * d, 4 * d))
    m_half = (slice(0, 3 * f // 2), slice(3 * f // 2, 3 * f))
    a_slab = lambda k: wa_ref.at[k, c]
    m_slab = lambda i: lambda k: gm_ref.at[chunk(i), k // 2, lax.rem(k, 2), c]
    mine_slab = lambda i: m_slab(i)(yx)

    def line(k, right):
        shard = z - (k - 1) if right else z + (k - 1)
        place = gm_ref.at[shard, py, px, c]
        return net.make(76 + 2 * k + right, wms_h if k == 1 else place, place, (net.d, z + 1 if right else z - 1))

    def came(k, right):
        place = gm_ref.at[z - k if right else z + k, py, px, c]
        return net.make(76 + 2 * k + right, place, place, (net.d, z - 1 if right else z + 1))

    def line_go(k):
        pl.when((z >= k - 1) & (z <= Z - 2))(lambda: line(k, 1).start())
        pl.when((z <= Z - k) & (z >= 1))(lambda: line(k, 0).start())

    def line_wait(k):
        pl.when(z >= k)(lambda: came(k, 1).wait_recv())
        pl.when(z <= Z - 1 - k)(lambda: came(k, 0).wait_recv())

    def line_left(k):
        pl.when((z >= k - 1) & (z <= Z - 2))(lambda: line(k, 1).wait_send())
        pl.when((z <= Z - k) & (z >= 1))(lambda: line(k, 0).wait_send())

    def chunk_out(i):
        net.got(f"m{i}l", f"m{i}r")
        net.go(f"m{i}c")

    plan_gather(net, "a", wa_ref.at[yx, c], a_slab, a_half)
    for i in range(Z):
        plan_gather(net, f"m{i}", wms_h if i == 1 else mine_slab(i), m_slab(i), m_half)
        rows = gm_ref.at[chunk(i), :, :, c]
        net.plan(f"m{i}c", rows, rows, net.core)

    gsum_ref[...] = jnp.zeros_like(gsum_ref)
    gsum_ref[0:2, 0 : gs_ref.shape[1]] = gs_ref[...]
    gains_ref[...] = pltpu.roll(gsum_ref[...], spot, 1)
    net.barrier()
    gains_steps = all_sum(net, "g", gains_ref, boxes_ref)
    next(gains_steps)
    for r in range(1, Z):
        net.start(f"az{r}", was_h, pack_ref.at[z], (net.d, net.peer(r)))
    net.keep("a", was_h, pack_ref.at[z])
    net.keep("m", wms_h, gm_ref.at[z, py, px, c])
    net.keep("t", tok_h.at[z], x_ref.at[mine])
    net.keep("c", cot_h.at[z], cot_ref.at[mine])
    net.keep("cos", cos_h, cos_ref)
    net.keep("sin", sin_h, sin_ref)
    next(gains_steps)
    net.got("az1", "az2", "az3")
    line_go(1)
    for r in range(1, Z):
        net.start(f"t{r}", tok_h.at[net.peer(r)], x_ref.at[mine], (net.d, net.peer(r)))
    net.kept("a")
    for i, heads in enumerate(lane_pairs(pack_ref, 4 * d // Z)):
        for j, value in enumerate(heads):
            wa_ref[yx, c, :, i * d + j * 128 : i * d + (j + 1) * 128] = value
    spread(net, "a")
    net.start("ac0", wa_ref.at[yx, c], wa_ref.at[yx, c], net.core)
    for _ in range(3):
        next(gains_steps)
    for r in range(1, Z):
        net.left(f"gz{r}")
    gains_ref[...] = boxes_ref[9]
    relay(net, "a")
    spread(net, "m1")
    net.start("ac1", a_slab(flip(yx, 1)), a_slab(flip(yx, 1)), net.core)
    net.start("ac2", a_slab(flip(yx, 2)), a_slab(flip(yx, 2)), net.core)
    net.got("al", "ar")
    net.start("ac3", a_slab(kd), a_slab(kd), net.core)
    net.kept("m")
    line_wait(1)
    net.got("t1", "t2", "t3")
    net.kept("t")
    line_go(2)
    spread(net, "m0")
    n1_ref = b1
    norm_stage(t, x_ref, gains_ref, n1_ref)
    net.kept("cos")
    net.kept("sin")
    net.got("ac0", "ac1", "ac2", "ac3")

    q_ref, k_ref, v_ref = (wide.at[:, i * d : (i + 1) * d] for i in range(3))
    qkv_stage(t, d, n1_ref, wa_ref, cos_ref, sin_ref, (q_ref, k_ref, v_ref))
    for name, src, dst in (("q", q_ref, q_h), ("k", k_ref, k_h)):
        net.keep(name, src, dst)
    for r in range(1, Z):
        net.start(f"c{r}", cot_h.at[net.peer(r)], cot_ref.at[mine], (net.d, net.peer(r)))
    relay(net, "m1")
    attend = functools.partial(attend_stage, t, d, length, q_ref, k_ref, v_ref, ctxt_ref, lse_ref)
    attend(0, 3)
    line_wait(2)
    line_go(3)
    spread(net, "m2")
    relay(net, "m0")
    chunk_out(1)
    attend(3, d // 128)
    chunk_out(0)
    out_stage(t, d, length, x_ref, wa_ref, ctxt_ref, hid_ref)

    mred = Reduce(net, 86, gm_ref, lambda i: i, credit, mc, mx, my, ml, mr)
    ared = Reduce(net, 106, ga_ref, lambda i: 4 + lax.rem(i + 1, 4), credit, mc, ax, ay, al, ar)

    def mz_copy(w, r):
        return net.make(126 + r, mred.own(w), mz.at[r - 1], (net.d, w))

    def mz_out(i):
        w = chunk(i)
        mz_copy(w, lax.rem(w + Z - z, Z)).start()

    net.keep("hid", hid_ref, hid_h)
    hid_back = pltpu.make_async_copy(hid_h, hid_ref, local.at[15])
    n2_ref, dm_ref, n2t_ref, dmt_ref = b1, b2, t1, t2

    @pl.loop(0, t // BLK)
    def _(m):
        rs = rows_of(m)
        unit, _ = norm_rows(hid_ref[rs, :], None)
        n2 = jnp.where(token_mask(m, length), unit * gains_ref[1:2, :], 0.0).astype(BF16)
        n2_ref[rs, :] = n2
        n2t_ref[:, rs] = n2.T

    def chunk_left(i):
        for tag in ("x", "y", "l", "r", "c"):
            net.left(f"m{i}{tag}")

    def last_shard():
        line_wait(3)
        spread(net, "m3")

    arrived = (
        (lambda: net.got("m1c"),),
        (lambda: relay(net, "m3"), lambda: net.got("m2c")),
        (lambda: net.got("m3c"),),
        (),
    )
    middle = (
        (lambda: line_left(1), lambda: line_left(2), lambda: chunk_out(2)),
        (lambda: line_left(3), lambda: chunk_out(3), lambda: mred.p1(chunk(0), 0)),
        (lambda: mred.p2(chunk(0), 0), lambda: mred.p1(chunk(1), 1)),
        (lambda: mred.p3(chunk(0), 0), lambda: mz_out(0), lambda: mred.p1(chunk(2), 2)),
    )

    def at(i, steps):
        for k in range(Z):
            if steps[k]:

                @pl.when(i == k)
                def _():
                    for step in steps[k]:
                        step()

    f1[...] = jnp.zeros_like(f1)
    net.kept("hid")
    net.kept("q")
    net.kept("k")
    relay(net, "m2")
    net.got("m0c")
    mlp_out(f, d, gm_ref.at[chunk(0)], n2_ref, wide, hid_ref)
    peer_rows = [rows_of(net.peer(j)) for j in range(Z)]
    for j in range(1, Z):
        net.plan(f"lo{j}", lo_ref.at[peer_rows[j]], lo_out.at[z], (net.d, net.peer(j)))

    @pl.loop(0, Z)
    def _(i):
        at(i, arrived)
        ahead = gm_ref.at[chunk(i + 1)]
        pl.when(i < Z - 1)(lambda: mlp_out(f, d, ahead, n2_ref, wide, hid_ref))

        @pl.when(i == 0)
        def _():
            last_shard()
            net.got("c1", "c2", "c3")
            net.kept("c")

            for m in range(t // BLK):
                rs = slice(m * BLK, (m + 1) * BLK)
                dm = jnp.where(token_mask(m, length), cot_ref[rs, :], jnp.zeros((), BF16))
                dm_ref[rs, :] = dm
                dmt_ref[:, rs] = dm.T

        @pl.when(i == Z - 2)
        def _():
            for j in (2, 1, 3, 0):
                rs = peer_rows[j]
                lo_ref[rs, :] = hid_ref[rs, :].astype(BF16)
                if j:
                    net.go(f"lo{j}")
            hid_back.start()

        gm = gm_ref.at[chunk(i)]
        mlp_front(f, d, gm, n2_ref, dm_ref, wide)
        at(i, middle)
        at(i, tuple((functools.partial(chunk_left, k),) for k in range(Z)))
        mlp_back(f, d, gm, n2t_ref, dmt_ref, wide, f1)
        mred.p0(chunk(i), i)

    net.keep("lo", lo_ref.at[peer_rows[0]], lo_out.at[z])
    for name, src, dst in (("q2", q_h, q_ref), ("k2", k_h, k_ref)):
        net.keep(name, src, dst)
    gsum_ref[...] = jnp.zeros_like(gsum_ref)
    dh_ref, da_ref = hid_ref, b1
    hid_back.wait()

    @pl.loop(0, t // BLK)
    def _(m):
        rs = rows_of(m)
        hid = hid_ref[rs, :]
        ok = token_mask(m, length)
        unit, r = norm_rows(hid, None)
        dn2 = f1[rs, :]
        gsum_ref[1:2, :] += jnp.sum(dn2 * unit, axis=0, keepdims=True)
        e2 = dn2 * gains_ref[1:2, :]
        dh = cot_ref[rs, :].astype(F32) + r * (e2 - unit * jnp.mean(e2 * unit, axis=-1, keepdims=True))
        dh_ref[rs, :] = dh
        da_ref[rs, :] = jnp.where(ok, dh, 0.0).astype(BF16)

    mred.p2(chunk(1), 1)
    mred.p1(chunk(3), 3)

    dat_ref, n1t_ref, dctx_ref = t1, t2, cot_ref
    dat_ref[...] = da_ref[...].T
    shape = ga_ref.shape[1:5]

    @pl.loop(0, d // 256)
    def _(j):
        rs = pl.ds(pl.multiple_of(j * 256, 256), 256)
        cols = pl.ds(pl.multiple_of(3 * d + j * 256, 256), 256)
        ga_ref[3, :, :, :, :, rs] = nt(dat_ref[...], ctxt_ref[rs, :]).astype(BF16).reshape(shape + (256,))
        dctx = nn(da_ref[...], wa_cols(wa_ref, cols)).astype(BF16)
        dctx_ref[:, rs] = dctx
        prod = dctx.T.astype(F32) * ctxt_ref[rs, :].astype(F32)
        for h in range(4):
            dlt_ref[pl.ds(j * 4 + h, 1), :] = jnp.sum(prod[h * HEAD : (h + 1) * HEAD], axis=0, keepdims=True)

    mred.p2(chunk(2), 2)
    ared.p0(3, 3)

    @pl.loop(0, t // BLK)
    def _(m):
        rs = rows_of(m)
        unit, _ = norm_rows(x_ref[rs, :].astype(F32), None)
        n1t_ref[:, rs] = (unit * gains_ref[0:1, :]).astype(BF16).T

    net.kept("q2")
    net.kept("k2")
    dk_acc, dv_acc = f1.at[:, 0:128], f1.at[:, 128:256]
    lanes = dict(o=slice(512 - 128, 512), q=slice(0, 384), t=slice(512, 768))

    def to_owner(base, w, tag):
        r = lax.rem(w + Z - z, Z)

        @pl.when(r != 0)
        def _():
            net.make(base + r - 1, pack_ref.at[w, :, lanes[tag]], az.at[r - 1, :, lanes[tag]], (net.d, w)).start()

    def pack_out():
        for w in range(Z):
            at = PAIRS.index(w) * 128
            pack_ref[w, :, lanes["o"]] = ared.own(3)[:, at : at + 128]
            to_owner(132, w, "o")

    def pack_pairs(g):
        for s in range(2):
            w = PAIRS[2 * g + s]
            for k in range(3):
                pack_ref[w, :, k * 128 : (k + 1) * 128] = ared.own(g)[:, k * 256 + s * 128 : k * 256 + s * 128 + 128]
            to_owner(135, w, "q")

    def pack_thirds():
        for w, j, value in packed_thirds(ared.own):
            pack_ref[w, :, 512 + j * 128 : 640 + j * 128] = value
        for w in range(Z):
            to_owner(138, w, "t")

    def heads_out(g):
        for k in range(3):
            cols = pl.ds(pl.multiple_of(k * d + g * 256, 256), 256)
            ga_ref[g, :, :, :, :, k * 256 : (k + 1) * 256] = nn(n1t_ref[...], wide[:, cols]).astype(BF16).reshape(shape + (256,))
        ared.p0(g, g)

    first = (
        (lambda: ared.p1(3, 3),),
        (lambda: ared.p2(3, 3), lambda: ared.p1(0, 0)),
        (lambda: ared.p2(0, 0), lambda: ared.p1(1, 1)),
    )
    second = (
        (lambda: mred.p3(chunk(2), 2), lambda: mz_out(2), lambda: mred.p2(chunk(3), 3)),
        (lambda: mred.p3(chunk(3), 3), lambda: mz_out(3), lambda: ared.p3(3, 3), pack_out),
        (lambda: ared.p3(0, 0), lambda: pack_pairs(0), lambda: mred.p3(chunk(1), 1)),
    )

    @pl.loop(0, 3)
    def _(g):
        @pl.loop(0, 2)
        def _(s):
            p = 2 * g + s
            attend_back(t, d, length, q_ref, k_ref, v_ref, dctx_ref, lse_ref, dlt_ref, cos_ref, sin_ref, wide, dk_acc, dv_acc, p, p + 1)
            for k in range(3):
                for steps, which in ((first, 0), (second, 1)):

                    @pl.when((g == k) & (s == which))
                    def _():
                        for step in steps[k]:
                            step()

        heads_out(g)

    gx_ref = b1
    for j in (2, 1, 3, 0):
        m = net.peer(j)
        rs = rows_of(m)
        dn1 = nt(wide[rs, :], wa_cols(wa_ref, slice(0, 3 * d)))
        unit, r = norm_rows(x_ref[rs, :].astype(F32), None)
        gsum_ref[0:1, :] += jnp.sum(dn1 * unit, axis=0, keepdims=True)
        e1 = dn1 * gains_ref[0:1, :]
        gx_ref[rs, :] = (dh_ref[rs, :] + r * (e1 - unit * jnp.mean(e1 * unit, axis=-1, keepdims=True))).astype(BF16)
        if j:
            net.start(f"gx{j}", gx_ref.at[rs], gx_out.at[z], (net.d, m))
        else:
            net.keep("gx", gx_ref.at[rs], gx_out.at[z])
        if j == 2:
            ared.p2(1, 1)
            ared.p1(2, 2)
        elif j == 3:
            ared.p3(1, 1)
            pack_pairs(1)
        elif j == 0:
            ared.p2(2, 2)
    steps = all_sum(net, "s", gsum_ref, boxes2_ref, last=True)
    next(steps)
    next(steps)
    ared.p3(2, 2)
    pack_thirds()
    next(steps)
    next(steps)
    total = mred.own(z)[...].astype(F32)
    for r in range(1, Z):
        mz_copy(net.peer(r), r).wait_recv()
        total = total + mz[r - 1].astype(F32)
    rows, half = total.shape[0], total.shape[1] // 2
    f1[0:rows, :] = total[:, :half]
    f1[rows : 2 * rows, :] = total[:, half:]

    parts = [
        net.make(base + r - 1, pack_ref.at[net.peer(r), :, lanes[tag]], az.at[r - 1, :, lanes[tag]], (net.d, net.peer(r)))
        for base, tag in ((132, "o"), (135, "q"), (138, "t"))
        for r in range(1, Z)
    ]
    for copy in parts:
        copy.wait_recv()
    total = pack_ref[z].astype(F32)
    for i in range(Z - 1):
        total = total + az[i].astype(F32)
    f1[2 * rows : 3 * rows, :] = total
    net.keep("grads", f1.at[0 : 3 * rows], grads_out)
    next(steps)
    gg_ref[...] = pltpu.roll(boxes2_ref[9], d - spot, 1)[0:2, 0 : gs_ref.shape[1]]
    net.got(*(f"{n}{j}" for n in ("lo", "gx") for j in range(1, Z)))
    for name in ("lo", "gx", "grads"):
        net.kept(name)
    for i in range(Z):
        mred.sent(chunk(i), i)
        ared.sent(i, i)
    for copy in parts:
        copy.wait_send()
    for r in range(1, Z):
        mz_copy(net.peer(r), r).wait_send()
    net.finish()


VM = pl.BlockSpec(memory_space=pltpu.VMEM)
SM = pl.BlockSpec(memory_space=pltpu.SMEM)


def call(kernel, ins, outs, scratch):
    return pl.pallas_call(
        kernel,
        out_shape=[jax.ShapeDtypeStruct(s, dt) for s, dt in outs],
        in_specs=[SM] + [VM] * (len(ins) - 1),
        out_specs=[VM] * len(outs),
        scratch_shapes=[pltpu.VMEM(s, dt) for s, dt in scratch],
        compiler_params=pltpu.CompilerParams(vmem_limit_bytes=60 * 2**20),
    )(*ins)


def backward(length, x, cot, gains, wa, wm, cosine, sine, q, k, v, ctxt, lse, hid):
    t, d = x.shape
    f = wm.shape[-1] // 3
    heads = lse.shape[0]
    td, dt = ((t, d), BF16), ((d, t), BF16)
    lo, dh, da, gm, gg2 = call(
        k2,
        (length, cot, gains, hid, wm),
        (td, ((t, d), F32), td, (wm.shape, BF16), ((1, d), F32)),
        (td, td, dt, dt, ((t, 3 * f), BF16), ((t, d), F32), ((t, d), F32)),
    )
    gx, ga, gg1 = call(
        k3,
        (length, x, gains, wa, cosine, sine, q, k, v, ctxt, lse, dh, da),
        (td, (wa.shape, BF16), ((1, d), F32)),
        (td, dt, dt, td, ((heads, t), F32), ((t, 3 * d), BF16), ((t, 128), F32), ((t, 128), F32), ((t, d), F32)),
    )
    return lo, gx, ga, gm, jnp.concatenate([gg1, gg2])


def one_sequence(length, x, cot, gains, wa, wm, cosine, sine):
    t, d = x.shape
    heads = -(-d // HEAD // 8) * 8
    td, dt = ((t, d), BF16), ((d, t), BF16)
    kept = call(k1_alone, (length, x, gains, wa, cosine, sine), (td, td, td, dt, ((heads, t), F32), ((t, d), F32)), (td,))
    return backward(length, x, cot, gains, wa, wm, cosine, sine, *kept)


def pack_weights(w_qkv, w_out, w_gate_up, w_down):
    attn = jnp.stack([w_qkv[0], w_qkv[1], w_qkv[2], w_out.T], axis=1)
    mlp = jnp.concatenate([w_gate_up[0], w_gate_up[1], w_down.T], axis=1)
    return attn, mlp


def unpack_grads(g_attn, g_mlp, fw):
    g_qkv = jnp.transpose(g_attn[:, :3], (1, 0, 2))
    g_gate_up = jnp.stack([g_mlp[:, i * fw : (i + 1) * fw] for i in range(2)])
    return g_qkv, g_attn[:, 3].T, g_gate_up, g_mlp[:, 2 * fw :].T


def to_sequences(local):
    return lax.all_to_all(local, "tp", split_axis=0, concat_axis=1, tiled=True)


def to_positions(whole):
    return lax.all_to_all(whole, "tp", split_axis=1, concat_axis=0, tiled=True)


def fused_layer(lengths, tokens, cotangent, attn, mlp, gains, cosine, sine):
    batch, part, d = tokens.shape
    t, rows, f3 = part * Z, attn.shape[0], mlp.shape[1]
    heads = -(-d // HEAD // 8) * 8
    pairs = 2 * HEAD
    was = jnp.concatenate(
        [attn[:, :, :pairs].reshape(rows, 4 * pairs), attn[:, :, pairs:].reshape(rows, 4 * HEAD)], axis=1
    )
    hbm = pl.BlockSpec(memory_space=pl.ANY)
    moved = ((Z, part, d), BF16)
    td, dt, big, small = ((t, d), BF16), ((d, t), BF16), ((t, d), F32), ((8, d), F32)
    outs = (moved, moved, ((3 * rows, d), F32), (gains.shape, F32), td, td, big)

    def boxes(cols, last=Z - 1):
        pair = ((4, 2, rows, cols // 2), BF16)
        one = ((4, rows, cols // 2), BF16)
        return [pair, pair, one, one, ((last, rows, cols), BF16)]

    wm = ((Z, 2, 2, 2, rows, f3), BF16)
    stage = ((Z, rows, d), BF16)
    lse = ((heads, t), F32)
    scratch = [td, td] + [(cosine.shape, F32)] * 2 + [((4, 2, rows, 4 * d), BF16), wm, dt, lse, big]
    scratch += [td, td, td, dt, dt, ((t, 3 * d), BF16), big, lse, small, small, ((10, 8, d), F32), ((10, 8, d), F32), stage]
    scratch += [((2, 2, 2, rows, f3), BF16)] + boxes(f3) + [((4, 2, 2, 2, rows, d), BF16)] + boxes(d)
    return pl.pallas_call(
        layer_kernel,
        out_shape=[jax.ShapeDtypeStruct(s, dt_) for s, dt_ in outs],
        in_specs=[SM, VM] + [hbm] * 6,
        out_specs=[hbm, hbm, hbm, VM, hbm, hbm, hbm],
        scratch_shapes=[pltpu.VMEM(s, dt_) for s, dt_ in scratch]
        + [pltpu.SemaphoreType.DMA((144,)), pltpu.SemaphoreType.DMA((144,)), pltpu.SemaphoreType.DMA((16,)), pltpu.SemaphoreType.REGULAR],
        compiler_params=pltpu.CompilerParams(collective_id=0, has_side_effects=True, vmem_limit_bytes=62 * 2**20),
    )(lengths, gains, was, tokens, cotangent, mlp, cosine, sine)[:4]


def fits(mesh_dp, tokens, w_qkv, w_gate_up):
    tp = lax.axis_size("tp")
    rows, hw = w_qkv.shape[1:]
    return (
        mesh_dp == 8 and tp == Z and tokens.shape[0] == Z and hw == 3 * HEAD and rows % 16 == 0
        and w_gate_up.shape[2] % 256 == 0 and 3 * w_gate_up.shape[2] <= 2 * tokens.shape[2] and tokens.shape[1] % BLK == 0
    )


def body(tokens, lengths, w_qkv, w_out, w_gate_up, w_down, gains, cotangent):
    tp, dp = lax.axis_size("tp"), lax.axis_size("dp")
    batch, part, d = tokens.shape
    n, t = batch // tp, part * tp
    fw = w_gate_up.shape[2]
    cosine, sine = map(jnp.asarray, rope_np(t))
    attn, mlp = pack_weights(w_qkv, w_out, w_gate_up, w_down)
    own = lax.dynamic_slice_in_dim(lengths, lax.axis_index("tp") * n, n)
    if fits(dp, tokens, w_qkv, w_gate_up):
        out, gx, grads, s_gains = fused_layer(lengths, tokens, cotangent, attn, mlp, gains, cosine, sine)
        pairs, rows = 2 * HEAD, attn.shape[0]
        s_mlp = jnp.concatenate([grads[:rows], grads[rows : 2 * rows]], axis=1)
        s_attn = grads[2 * rows :]
        first, third = s_attn[:, : 4 * pairs], s_attn[:, 4 * pairs :]
        s_attn = jnp.concatenate([first.reshape(-1, 4, pairs), third.reshape(-1, 4, HEAD)], axis=2)
        gx = gx.astype(F32)
    else:
        full_gains = lax.all_gather(gains, ("dp", "tp"), axis=1, tiled=True)
        full_gains = jnp.pad(full_gains, ((0, 6), (0, 0)))
        x16 = to_sequences(tokens)
        wa = lax.all_gather(attn, "tp", axis=2, tiled=True).reshape(attn.shape[0], 4 * d)
        wa = lax.all_gather(wa, "dp", axis=0, tiled=True).reshape(1, 1, d, 4 * d)
        wm = lax.all_gather(lax.all_gather(mlp, "tp", axis=0), "dp", axis=1, tiled=True).reshape(tp, 1, 1, d, 3 * fw)
        cot16 = to_sequences(cotangent)
        los, gxs, ga, gm, gg = [], [], 0.0, 0.0, 0.0
        for i in range(n):
            lo, gx, a, m, g = one_sequence(own[i : i + 1], x16[i], cot16[i], full_gains, wa, wm, cosine, sine)
            los.append(lo)
            gxs.append(gx)
            ga, gm, gg = ga + a.astype(F32), gm + m.astype(F32), gg + g
        out = to_positions(jnp.stack(los))
        gx = to_positions(jnp.stack(gxs)).astype(F32)
        ga, gm = ga.reshape(d, 4, d), gm.reshape(tp, d, 3 * fw)
        s_mlp = lax.psum_scatter(lax.psum_scatter(gm, "dp", scatter_dimension=1, tiled=True), "tp", scatter_dimension=0)
        s_attn = lax.psum_scatter(ga.reshape(d, 4 * d), "dp", scatter_dimension=0, tiled=True)
        s_attn = lax.psum_scatter(s_attn.reshape(-1, 4, d), "tp", scatter_dimension=2, tiled=True)
        s_gains = lax.psum_scatter(gg, ("dp", "tp"), scatter_dimension=1, tiled=True)
    return (out, gx) + unpack_grads(s_attn, s_mlp, fw) + (s_gains,)


def solution(mesh):
    act = P("dp", "tp", None)
    cols, rows, gain = P(None, "dp", "tp"), P("tp", "dp"), P(None, ("dp", "tp"))
    return jax.shard_map(
        body,
        mesh=mesh,
        in_specs=(act, P("dp"), cols, rows, cols, rows, gain, act),
        out_specs=(act, act, cols, rows, cols, rows, gain),
        check_vma=False,
    )
```

```python
import functools

import numpy as np
import jax
import jax.numpy as jnp
from jax import lax
from jax.experimental import pallas as pl
from jax.experimental.pallas import tpu as pltpu
from jax.sharding import PartitionSpec as P

F32 = jnp.float32
BF16 = jnp.bfloat16
HEAD = 64
EPS = 1e-6
LOG2E = 1.4426950408889634
C2 = LOG2E * HEAD**-0.5
NEG = -1e30
BLK = 256


def dg(a, b, ca, cb):
    return lax.dot_general(a, b, (((ca,), (cb,)), ((), ())), preferred_element_type=F32)


def nn(a, b):
    return dg(a, b, 1, 0)


def nt(a, b):
    return dg(a, b, 1, 1)


def tn(a, b):
    return dg(a, b, 0, 0)


def rows_of(m):
    return pl.ds(pl.multiple_of(m * BLK, BLK), BLK)


def wa_cols(wa_ref, cols):
    part = wa_ref[:, :, :, cols]
    return part.reshape(-1, part.shape[-1])


def half_lane():
    return lax.broadcasted_iota(jnp.int32, (1, 128), 1) % HEAD < HEAD // 2


def head_lane(h):
    lane = lax.broadcasted_iota(jnp.int32, (1, 128), 1)
    return lane < HEAD if h == 0 else lane >= HEAD


def turned(v):
    return jnp.where(half_lane(), pltpu.roll(v, 96, 1), pltpu.roll(v, 32, 1))


def norm_rows(x, gain):
    r = lax.rsqrt(jnp.mean(x * x, axis=-1, keepdims=True) + EPS)
    return x * r, r


def norm_stage(t, x_ref, gains_ref, n1_ref):
    @pl.loop(0, t // BLK)
    def _(m):
        rs = rows_of(m)
        unit, _ = norm_rows(x_ref[rs, :].astype(F32), None)
        n1_ref[rs, :] = (unit * gains_ref[0:1, :]).astype(BF16)


def qkv_stage(t, d, n1_ref, wa_ref, cos_ref, sin_ref, outs):
    for c, out in enumerate(outs):
        if out is None:
            continue

        @pl.loop(0, d // 256)
        def _(j, c=c, out=out):
            cols = pl.ds(pl.multiple_of(c * d + j * 256, 256), 256)
            raw = nn(n1_ref[...], wa_cols(wa_ref, cols))
            for s in range(2):
                part = raw[:, s * 128 : (s + 1) * 128]
                if c < 2:
                    part = part * cos_ref[...] + turned(part) * sin_ref[...]
                out[:, pl.ds(pl.multiple_of(j * 256 + s * 128, 128), 128)] = part.astype(BF16)


def key_bias(t, length):
    pos = lax.broadcasted_iota(jnp.int32, (t, 1), 0)
    return jnp.where(pos < length, 0.0, NEG).astype(BF16)


def causal_block():
    key = lax.broadcasted_iota(jnp.int32, (BLK, BLK), 0)
    query = lax.broadcasted_iota(jnp.int32, (BLK, BLK), 1)
    return key <= query


def score_operands(h, qp, kp, bias):
    mine = head_lane(h)
    lane = lax.broadcasted_iota(jnp.int32, (1, 128), 1)
    spare = lane == (HEAD if h == 0 else 0)
    zero = jnp.zeros((), BF16)
    q_m = jnp.where(mine, qp, zero)
    k_m = jnp.where(mine, kp, zero)
    q_s = jnp.where(spare, jnp.ones((), BF16), q_m)
    k_s = jnp.where(spare, bias, k_m)
    return q_m, k_m, q_s, k_s


def mask_diag(s, i):
    if i == 0:
        return jnp.where(causal_block(), s, NEG)
    return jnp.concatenate([s[: i * BLK], jnp.where(causal_block(), s[i * BLK :], NEG)], axis=0)


def attend_stage(t, d, length, q_ref, k_ref, v_ref, ctxt_ref, lse_ref, first, last):
    bias = key_bias(t, length)

    @pl.loop(first, last)
    def _(p):
        cols = pl.ds(pl.multiple_of(p * 128, 128), 128)
        qp, kp, vp = q_ref[:, cols], k_ref[:, cols], v_ref[:, cols]
        for h in range(2):
            _, _, q_s, k_s = score_operands(h, qp, kp, bias)
            for i in range(t // BLK):
                n = (i + 1) * BLK
                s = mask_diag(nt(k_s[:n], q_s[i * BLK : n]), i)
                top = jnp.max(s, axis=0, keepdims=True)
                e = jnp.exp2((s - top) * C2)
                total = jnp.sum(e, axis=0, keepdims=True)
                o = tn(vp[:n], e.astype(BF16))[h * HEAD : (h + 1) * HEAD] / total
                ctxt_ref[pl.ds(pl.multiple_of(p * 128 + h * HEAD, HEAD), HEAD), i * BLK : n] = o.astype(BF16)
                lse_ref[pl.ds(p * 2 + h, 1), i * BLK : n] = top * C2 + jnp.log2(total)


def out_stage(t, d, length, x_ref, wa_ref, ctxt_ref, hid_ref):
    out = dg(ctxt_ref[...], wa_cols(wa_ref, slice(3 * d, 4 * d)), 0, 1)
    pos = lax.broadcasted_iota(jnp.int32, (t, 1), 0)
    hid_ref[...] = x_ref[...].astype(F32) + jnp.where(pos < length, out, 0.0)


def k1_alone(len_ref, x_ref, gains_ref, wa_ref, cos_ref, sin_ref, q_ref, k_ref, v_ref, ctxt_ref, lse_ref, hid_ref, n1_ref):
    t, d = x_ref.shape
    length = len_ref[0]
    norm_stage(t, x_ref, gains_ref, n1_ref)
    qkv_stage(t, d, n1_ref, wa_ref, cos_ref, sin_ref, (q_ref, k_ref, v_ref))
    attend_stage(t, d, length, q_ref, k_ref, v_ref, ctxt_ref, lse_ref, 0, d // 128)
    out_stage(t, d, length, x_ref, wa_ref, ctxt_ref, hid_ref)


def token_mask(m, length):
    pos = m * BLK + lax.broadcasted_iota(jnp.int32, (BLK, 1), 0)
    return pos < length


def chunk_cols(wm, d, lo, hi):
    return wm[..., lo:hi].reshape(d, hi - lo)


def mlp_front(f, d, wm, n2_ref, dm_ref, wide):
    w = 256
    for j in range(f // w):
        lo, hi = j * w, (j + 1) * w
        gate = nn(n2_ref[...], chunk_cols(wm, d, lo, hi))
        up = nn(n2_ref[...], chunk_cols(wm, d, f + lo, f + hi))
        d_act = nn(dm_ref[...], chunk_cols(wm, d, 2 * f + lo, 2 * f + hi))
        s = 1.0 / (1.0 + jnp.exp2(gate * (-LOG2E)))
        sw = gate * s
        wide[:, 2 * f + lo : 2 * f + hi] = (sw * up).astype(BF16)
        wide[:, lo:hi] = (d_act * up * (s + sw * (1.0 - s))).astype(BF16)
        wide[:, f + lo : f + hi] = (d_act * sw).astype(BF16)


def mlp_out(f, d, wm, n2_ref, wide, mlp_ref):
    w = 256
    for j in range(f // w):
        lo, hi = j * w, (j + 1) * w
        gate = nn(n2_ref[...], chunk_cols(wm, d, lo, hi))
        up = nn(n2_ref[...], chunk_cols(wm, d, f + lo, f + hi))
        wide[:, lo:hi] = (gate * up / (1.0 + jnp.exp2(gate * (-LOG2E)))).astype(BF16)
    mlp_ref[...] += nt(wide[:, :f], chunk_cols(wm, d, 2 * f, 3 * f))


def mlp_back(f, d, wm, n2t_ref, dmt_ref, wide, dn2_ref):
    w = 256
    dn2_ref[...] += nt(wide[:, : 2 * f], chunk_cols(wm, d, 0, 2 * f))
    for j in range(3 * f // w):
        cols = slice(j * w, (j + 1) * w)
        left = n2t_ref if j * w < 2 * f else dmt_ref
        wm[..., cols] = nn(left[...], wide[:, cols]).astype(BF16).reshape(wm.shape[:-1] + (w,))


def k2(len_ref, cot_ref, gains_ref, hid_ref, wm_ref, lo_ref, dh_ref, da_ref, gm_ref, gg_ref,
       n2_ref, dm_ref, n2t_ref, dmt_ref, wide, mlp_ref, dn2_ref):
    t, d = cot_ref.shape
    tp, f = wm_ref.shape[0], wm_ref.shape[-1] // 3
    length = len_ref[0]

    @pl.loop(0, t // BLK)
    def _(m):
        rs = rows_of(m)
        unit, _ = norm_rows(hid_ref[rs, :], None)
        n2 = (unit * gains_ref[1:2, :]).astype(BF16)
        n2_ref[rs, :] = n2
        n2t_ref[:, rs] = n2.T
        dm = jnp.where(token_mask(m, length), cot_ref[rs, :], jnp.zeros((), BF16))
        dm_ref[rs, :] = dm
        dmt_ref[:, rs] = dm.T

    mlp_ref[...] = jnp.zeros_like(mlp_ref)
    dn2_ref[...] = jnp.zeros_like(dn2_ref)

    @pl.loop(0, tp)
    def _(z):
        gm_ref[z] = wm_ref[z]
        mlp_out(f, d, gm_ref.at[z], n2_ref, wide, mlp_ref)
        mlp_front(f, d, gm_ref.at[z], n2_ref, dm_ref, wide)
        mlp_back(f, d, gm_ref.at[z], n2t_ref, dmt_ref, wide, dn2_ref)

    gg_ref[...] = jnp.zeros_like(gg_ref)

    @pl.loop(0, t // BLK)
    def _(m):
        rs = rows_of(m)
        hid = hid_ref[rs, :]
        ok = token_mask(m, length)
        lo_ref[rs, :] = (hid + jnp.where(ok, mlp_ref[rs, :], 0.0)).astype(BF16)
        unit, r = norm_rows(hid, None)
        dn2 = dn2_ref[rs, :]
        gg_ref[...] += jnp.sum(dn2 * unit, axis=0, keepdims=True)
        e2 = dn2 * gains_ref[1:2, :]
        dh = cot_ref[rs, :].astype(F32) + r * (e2 - unit * jnp.mean(e2 * unit, axis=-1, keepdims=True))
        dh_ref[rs, :] = dh
        da_ref[rs, :] = jnp.where(ok, dh, 0.0).astype(BF16)


def attend_back(t, d, length, q_ref, k_ref, v_ref, dctx_ref, lse_ref, dlt_ref, cos_ref, sin_ref, dqkv_ref, dk_acc, dv_acc, first, last):
    bias = key_bias(t, length)

    @pl.loop(first, last)
    def _(p):
        cols = pl.ds(pl.multiple_of(p * 128, 128), 128)
        qp, kp, vp, gp = q_ref[:, cols], k_ref[:, cols], v_ref[:, cols], dctx_ref[:, cols]
        dk_acc[...] = jnp.zeros_like(dk_acc)
        dv_acc[...] = jnp.zeros_like(dv_acc)
        ops = [score_operands(h, qp, kp, bias) for h in range(2)]
        for i in range(t // BLK):
            n = (i + 1) * BLK
            qs = slice(i * BLK, n)
            dq = None
            for h in range(2):
                q_m, k_m, q_s, k_s = ops[h]
                g_m = jnp.where(head_lane(h), gp[qs], jnp.zeros((), BF16))
                s = mask_diag(nt(k_s[:n], q_s[qs]), i)
                pr = jnp.exp2(s * C2 - lse_ref[pl.ds(p * 2 + h, 1), qs])
                dp = nt(vp[:n], g_m)
                ds = (pr * (dp - dlt_ref[pl.ds(p * 2 + h, 1), qs])).astype(BF16)
                dv_acc[:n, :] += nn(pr.astype(BF16), g_m)
                dk_acc[:n, :] += nn(ds, q_m[qs])
                part = tn(ds, k_m[:n])
                dq = part if dq is None else dq + part
            dq = dq * (HEAD**-0.5)
            dqkv_ref[qs, cols] = (dq * cos_ref[qs, :] - turned(dq) * sin_ref[qs, :]).astype(BF16)
        dk = dk_acc[...] * (HEAD**-0.5)
        dqkv_ref[:, pl.ds(pl.multiple_of(d + p * 128, 128), 128)] = (dk * cos_ref[...] - turned(dk) * sin_ref[...]).astype(BF16)
        dqkv_ref[:, pl.ds(pl.multiple_of(2 * d + p * 128, 128), 128)] = dv_acc[...].astype(BF16)


def k3(len_ref, x_ref, gains_ref, wa_ref, cos_ref, sin_ref, q_ref, k_ref, v_ref, ctxt_ref, lse_ref, dh_ref, da_ref,
       gx_ref, ga_ref, gg_ref, n1_ref, n1t_ref, dat_ref, dctx_ref, dlt_ref, dqkv_ref, dk_acc, dv_acc, dn1_ref):
    t, d = x_ref.shape
    length = len_ref[0]

    dat_ref[...] = da_ref[...].T

    @pl.loop(0, d // 256)
    def _(j):
        rs = pl.ds(pl.multiple_of(j * 256, 256), 256)
        cols = pl.ds(pl.multiple_of(3 * d + j * 256, 256), 256)
        ga_ref[:, :, :, cols] = nt(dat_ref[...], ctxt_ref[rs, :]).astype(BF16).reshape(ga_ref.shape[:3] + (256,))
        dctx = nn(da_ref[...], wa_cols(wa_ref, cols)).astype(BF16)
        dctx_ref[:, rs] = dctx
        prod = dctx.T.astype(F32) * ctxt_ref[rs, :].astype(F32)
        for h in range(4):
            dlt_ref[pl.ds(j * 4 + h, 1), :] = jnp.sum(prod[h * HEAD : (h + 1) * HEAD], axis=0, keepdims=True)

    attend_back(t, d, length, q_ref, k_ref, v_ref, dctx_ref, lse_ref, dlt_ref, cos_ref, sin_ref, dqkv_ref, dk_acc, dv_acc, 0, d // 128)

    @pl.loop(0, t // BLK)
    def _(m):
        rs = rows_of(m)
        unit, _ = norm_rows(x_ref[rs, :].astype(F32), None)
        n1t_ref[:, rs] = (unit * gains_ref[0:1, :]).astype(BF16).T

    @pl.loop(0, 3 * d // 256)
    def _(j):
        cols = pl.ds(pl.multiple_of(j * 256, 256), 256)
        ga_ref[:, :, :, cols] = nn(n1t_ref[...], dqkv_ref[:, cols]).astype(BF16).reshape(ga_ref.shape[:3] + (256,))

    dn1_ref[...] = nt(dqkv_ref[...], wa_cols(wa_ref, slice(0, 3 * d)))

    gg_ref[...] = jnp.zeros_like(gg_ref)

    @pl.loop(0, t // BLK)
    def _(m):
        rs = rows_of(m)
        unit, r = norm_rows(x_ref[rs, :].astype(F32), None)
        dn1 = dn1_ref[rs, :]
        gg_ref[...] += jnp.sum(dn1 * unit, axis=0, keepdims=True)
        e1 = dn1 * gains_ref[0:1, :]
        gx_ref[rs, :] = (dh_ref[rs, :] + r * (e1 - unit * jnp.mean(e1 * unit, axis=-1, keepdims=True))).astype(BF16)


def rope_np(t):
    half = HEAD // 2
    freqs = np.float32(10000.0) ** (np.float32(-2.0) * np.arange(half, dtype=np.float32) / np.float32(HEAD))
    ang = np.arange(t, dtype=np.float32)[:, None] * freqs[None, :].astype(np.float32)
    c, s = np.cos(ang), np.sin(ang)
    return np.concatenate([c, c, c, c], 1).astype(np.float32), np.concatenate([-s, s, -s, s], 1).astype(np.float32)


MESH = pl.DeviceIdType.MESH
Z = 4
PAIRS = (0, 2, 1, 3)


def flip(d, bit):
    return d + bit - 2 * bit * lax.rem(d // bit, 2)


class Net:
    def __init__(self, send, recv, local):
        self.d, self.z = lax.axis_index("dp"), lax.axis_index("tp")
        self.yx, self.c = self.d // 2, lax.rem(self.d, 2)
        self.x, self.y, self.core = ((flip(self.d, b), self.z) for b in (2, 4, 1))
        self.send, self.recv, self.local = send, recv, local
        self.copies, self.own, self.gone = {}, {}, set()

    def peer(self, r):
        return lax.rem(self.z + r, Z)

    def source(self, r):
        return lax.rem(self.z + Z - r, Z)

    def barrier(self):
        sem = pltpu.get_barrier_semaphore()
        for dev in (self.x, self.y, self.core) + tuple((self.d, self.peer(r)) for r in range(1, Z)):
            pl.semaphore_signal(sem, inc=1, device_id=dev, device_id_type=MESH)
        pl.semaphore_wait(sem, 6)

    def make(self, i, src, dst, dev):
        return pltpu.make_async_remote_copy(
            src_ref=src, dst_ref=dst, send_sem=self.send.at[i], recv_sem=self.recv.at[i], device_id=dev, device_id_type=MESH
        )

    def plan(self, name, src, dst, dev):
        self.copies[name] = self.make(len(self.copies), src, dst, dev)

    def go(self, *names):
        for name in names:
            self.copies[name].start()

    def start(self, name, src, dst, dev):
        self.plan(name, src, dst, dev)
        self.go(name)

    def keep(self, name, src, dst):
        copy = pltpu.make_async_copy(src, dst, self.local.at[len(self.own)])
        copy.start()
        self.own[name] = copy

    def got(self, *names):
        for name in names:
            self.copies[name].wait_recv()

    def kept(self, name):
        self.own[name].wait()

    def left(self, name):
        self.copies[name].wait_send()
        self.gone.add(name)

    def finish(self):
        for name, copy in self.copies.items():
            if name not in self.gone:
                copy.wait_send()


def plan_gather(net, tag, own, slab, halves):
    kx, ky = flip(net.yx, 1), flip(net.yx, 2)
    net.plan(tag + "x", own, slab(net.yx), net.x)
    net.plan(tag + "y", own, slab(net.yx), net.y)
    net.plan(tag + "l", slab(kx).at[:, halves[0]], slab(kx).at[:, halves[0]], net.y)
    net.plan(tag + "r", slab(ky).at[:, halves[1]], slab(ky).at[:, halves[1]], net.x)


def spread(net, tag):
    net.go(tag + "x", tag + "y")


def relay(net, tag):
    net.got(tag + "x")
    net.go(tag + "l")
    net.got(tag + "y")
    net.go(tag + "r")


def all_sum(net, tag, own, boxes, last=False):
    def over_tp(src, out):
        for r in range(1, Z):
            net.start(f"{tag}z{r}", src, boxes.at[r - 1], (net.d, net.peer(r)))
        yield
        net.got(*(f"{tag}z{r}" for r in range(1, Z)))
        boxes[out] = src[...] + (boxes[0] + boxes[1] + boxes[2])

    def over_dp(src, outs):
        for i, (name, dev) in enumerate((("x", net.x), ("y", net.y), ("c", net.core))):
            net.start(tag + name, src, boxes.at[3 + i], dev)
            yield
            net.got(tag + name)
            boxes[outs[i]] = src[...] + boxes[3 + i]
            src = boxes.at[outs[i]]

    if last:
        yield from over_dp(own, (6, 7, 8))
        yield from over_tp(boxes.at[8], 9)
    else:
        yield from over_tp(own, 6)
        yield from over_dp(boxes.at[6], (7, 8, 9))
    yield


def lane_pairs(stage, hw):
    low = lax.broadcasted_iota(jnp.int32, (1, 128), 1) < HEAD
    parts = [[stage[z][:, c * 128 : (c + 1) * 128] for z in PAIRS] for c in range(4)]
    for j in range(Z // 2):
        for g in range(2):
            cols = slice(512 + g * 128, 640 + g * 128)
            a, b = stage[2 * j][:, cols].astype(F32), stage[2 * j + 1][:, cols].astype(F32)
            parts[2 * g].append(jnp.where(low, a, pltpu.roll(b, HEAD, 1)).astype(BF16))
            parts[2 * g + 1].append(jnp.where(low, pltpu.roll(a, HEAD, 1), b).astype(BF16))
    return parts


class Reduce:
    def __init__(self, net, base, data, use, credit, rc, r1x, r1y, r2l, r2r):
        self.net, self.base, self.data, self.use, self.credit = net, base, data, use, credit
        self.rc, self.r1x, self.r1y, self.r2l, self.r2r = rc, r1x, r1y, r2l, r2r
        self.x, self.y = lax.rem(net.yx, 2), net.yx // 2
        half = data.shape[-1] // 2
        self.lo, self.hi = slice(0, half), slice(half, 2 * half)

    def slot(self, i):
        return self.rc.at[lax.rem(self.use(i), 2), :, :, :, 0 : self.data.shape[-1]]

    def copies0(self, g, i):
        return [self.net.make(self.base + i, self.data.at[g, :, :, 1 - self.net.c], self.slot(i), self.net.core)]

    def copies1(self, g, i):
        net, c = self.net, self.net.c
        return [
            net.make(self.base + 4 + i, self.data.at[g, :, 1 - self.x, c, :, self.lo], self.r1x.at[i], net.x),
            net.make(self.base + 8 + i, self.data.at[g, 1 - self.y, :, c, :, self.hi], self.r1y.at[i], net.y),
        ]

    def copies2(self, g, i):
        net, c = self.net, self.net.c
        return [
            net.make(self.base + 12 + i, self.data.at[g, 1 - self.y, self.x, c, :, self.lo], self.r2l.at[i], net.y),
            net.make(self.base + 16 + i, self.data.at[g, self.y, 1 - self.x, c, :, self.hi], self.r2r.at[i], net.x),
        ]

    def add(self, at, value):
        self.data[at] = (self.data[at].astype(F32) + value.astype(F32)).astype(BF16)

    def p0(self, g, i):
        @pl.when(self.use(i) >= 2)
        def _():
            pl.semaphore_wait(self.credit, 1)

        for copy in self.copies0(g, i):
            copy.start()

    def p1(self, g, i):
        for copy in self.copies0(g, i):
            copy.wait_recv()
        for y in range(2):
            for x in range(2):
                self.add((g, y, x, self.net.c), self.slot(i)[y, x])

        @pl.when(self.use(i) < 6)
        def _():
            pl.semaphore_signal(self.credit, inc=1, device_id=self.net.core, device_id_type=MESH)

        for copy in self.copies1(g, i):
            copy.start()

    def p2(self, g, i):
        for copy in self.copies1(g, i):
            copy.wait_recv()
        for k in range(2):
            self.add((g, k, self.x, self.net.c, slice(None), self.lo), self.r1x[i, k])
            self.add((g, self.y, k, self.net.c, slice(None), self.hi), self.r1y[i, k])
        for copy in self.copies2(g, i):
            copy.start()

    def p3(self, g, i):
        for copy in self.copies2(g, i):
            copy.wait_recv()
        self.add((g, self.y, self.x, self.net.c, slice(None), self.lo), self.r2l[i])
        self.add((g, self.y, self.x, self.net.c, slice(None), self.hi), self.r2r[i])

    def own(self, g):
        return self.data.at[g, self.y, self.x, self.net.c]

    def sent(self, g, i):
        for copy in self.copies0(g, i) + self.copies1(g, i) + self.copies2(g, i):
            copy.wait_send()


def packed_thirds(own):
    low = lax.broadcasted_iota(jnp.int32, (1, 128), 1) < HEAD
    for z in range(Z):
        s, u = z % 2, z // 2
        third = [own(2)[:, c * 256 + u * 128 : c * 256 + u * 128 + 128].astype(F32) for c in range(3)]
        third.append(own(3)[:, 512 + u * 128 : 512 + u * 128 + 128].astype(F32))
        for j in range(2):
            a, b = third[2 * j], third[2 * j + 1]
            both = jnp.where(low, a, pltpu.roll(b, HEAD, 1)) if s == 0 else jnp.where(low, pltpu.roll(a, HEAD, 1), b)
            yield z, j, both.astype(BF16)


def layer_kernel(len_ref, gs_ref, was_h, tok_h, cot_h, wgu_h, wd_h, cos_h, sin_h,
                 lo_out, gx_out, grads_out, gg_ref, q_h, k_h, hid_h,
                 x_ref, cot_ref, cos_ref, sin_ref, wa_ref, gm_ref, ctxt_ref, lse_ref, hid_ref,
                 b1, b2, lo_ref, t1, t2, wide, f1, dlt_ref, gains_ref, gsum_ref, boxes_ref, boxes2_ref, pack_ref,
                 mc, mx, my, ml, mr, mz, ga_ref, ax, ay, al, ar, az,
                 send, recv, local, credit):
    t, d = x_ref.shape
    part = t // Z
    f = gm_ref.shape[-1] // 3
    net = Net(send, recv, local)
    z, yx, c = net.z, net.yx, net.c
    length = len_ref[z]
    spot = (net.d * Z + z) * gs_ref.shape[1]
    px, py = lax.rem(yx, 2), yx // 2
    mine = pl.ds(pl.multiple_of(z * part, part), part)
    kd = flip(flip(yx, 1), 2)
    order = ((1, 0, 2, 3), (0, 1, 2, 3), (3, 2, 1, 0), (2, 3, 1, 0))

    def chunk(i):
        if not isinstance(i, int):
            return sum((i == k).astype(jnp.int32) * chunk(k) for k in range(Z))
        return sum((z == k).astype(jnp.int32) * order[k][i] for k in range(Z))

    a_half = (slice(0, 2 * d), slice(2 * d, 4 * d))
    m_half = (slice(0, 3 * f // 2), slice(3 * f // 2, 3 * f))
    a_slab = lambda k: wa_ref.at[k, c]
    m_slab = lambda i: lambda k: gm_ref.at[chunk(i), k // 2, lax.rem(k, 2), c]
    mine_slab = lambda i: m_slab(i)(yx)

    def line(k, right):
        shard = z - (k - 1) if right else z + (k - 1)
        place = gm_ref.at[shard, py, px, c]
        return net.make(76 + 2 * k + right, place, place, (net.d, z + 1 if right else z - 1))

    def came(k, right):
        place = gm_ref.at[z - k if right else z + k, py, px, c]
        return net.make(76 + 2 * k + right, place, place, (net.d, z - 1 if right else z + 1))

    def line_go(k):
        pl.when((z >= k - 1) & (z <= Z - 2))(lambda: line(k, 1).start())
        pl.when((z <= Z - k) & (z >= 1))(lambda: line(k, 0).start())

    def line_wait(k):
        pl.when(z >= k)(lambda: came(k, 1).wait_recv())
        pl.when(z <= Z - 1 - k)(lambda: came(k, 0).wait_recv())

    def line_left(k):
        pl.when((z >= k - 1) & (z <= Z - 2))(lambda: line(k, 1).wait_send())
        pl.when((z <= Z - k) & (z >= 1))(lambda: line(k, 0).wait_send())

    def chunk_out(i):
        net.got(f"m{i}l", f"m{i}r")
        net.go(f"m{i}c")

    plan_gather(net, "a", wa_ref.at[yx, c], a_slab, a_half)
    for i in range(Z):
        plan_gather(net, f"m{i}", mine_slab(i), m_slab(i), m_half)
        rows = gm_ref.at[chunk(i), :, :, c]
        net.plan(f"m{i}c", rows, rows, net.core)

    gsum_ref[...] = jnp.zeros_like(gsum_ref)
    gsum_ref[0:2, 0 : gs_ref.shape[1]] = gs_ref[...]
    gains_ref[...] = pltpu.roll(gsum_ref[...], spot, 1)
    net.barrier()
    gains_steps = all_sum(net, "g", gains_ref, boxes_ref)
    next(gains_steps)
    for r in range(1, Z):
        net.start(f"az{r}", was_h, pack_ref.at[z], (net.d, net.peer(r)))
    net.keep("a", was_h, pack_ref.at[z])
    net.keep("mg", wgu_h.at[0], gm_ref.at[z, py, px, c, :, 0:f])
    net.keep("mu", wgu_h.at[1], gm_ref.at[z, py, px, c, :, f : 2 * f])
    net.keep("md", wd_h, gm_ref.at[z, py, px, c, :, 2 * f : 3 * f])
    net.keep("t", tok_h.at[z], x_ref.at[mine])
    net.keep("c", cot_h.at[z], cot_ref.at[mine])
    net.keep("cos", cos_h, cos_ref)
    net.keep("sin", sin_h, sin_ref)
    next(gains_steps)
    for name in ("mg", "mu", "md"):
        net.kept(name)
    net.got("az1", "az2", "az3")
    line_go(1)
    for r in range(1, Z):
        net.start(f"t{r}", tok_h.at[net.peer(r)], x_ref.at[mine], (net.d, net.peer(r)))
    net.kept("a")
    for i, heads in enumerate(lane_pairs(pack_ref, 4 * d // Z)):
        for j, value in enumerate(heads):
            wa_ref[yx, c, :, i * d + j * 128 : i * d + (j + 1) * 128] = value
    spread(net, "a")
    net.start("ac0", wa_ref.at[yx, c], wa_ref.at[yx, c], net.core)
    for _ in range(3):
        next(gains_steps)
    for r in range(1, Z):
        net.left(f"gz{r}")
    gains_ref[...] = boxes_ref[9]
    relay(net, "a")
    spread(net, "m1")
    net.start("ac1", a_slab(flip(yx, 1)), a_slab(flip(yx, 1)), net.core)
    net.start("ac2", a_slab(flip(yx, 2)), a_slab(flip(yx, 2)), net.core)
    net.got("al", "ar")
    net.start("ac3", a_slab(kd), a_slab(kd), net.core)
    line_wait(1)
    net.got("t1", "t2", "t3")
    net.kept("t")
    line_go(2)
    spread(net, "m0")
    n1_ref = b1
    norm_stage(t, x_ref, gains_ref, n1_ref)
    net.kept("cos")
    net.kept("sin")
    net.got("ac0", "ac1", "ac2", "ac3")

    q_ref, k_ref, v_ref = (wide.at[:, i * d : (i + 1) * d] for i in range(3))
    qkv_stage(t, d, n1_ref, wa_ref, cos_ref, sin_ref, (q_ref, k_ref, v_ref))
    for name, src, dst in (("q", q_ref, q_h), ("k", k_ref, k_h)):
        net.keep(name, src, dst)
    for r in range(1, Z):
        net.start(f"c{r}", cot_h.at[net.peer(r)], cot_ref.at[mine], (net.d, net.peer(r)))
    relay(net, "m1")
    attend = functools.partial(attend_stage, t, d, length, q_ref, k_ref, v_ref, ctxt_ref, lse_ref)
    attend(0, 3)
    line_wait(2)
    line_go(3)
    spread(net, "m2")
    relay(net, "m0")
    chunk_out(1)
    attend(3, d // 128)
    chunk_out(0)
    out_stage(t, d, length, x_ref, wa_ref, ctxt_ref, hid_ref)

    mred = Reduce(net, 86, gm_ref, lambda i: i, credit, mc, mx, my, ml, mr)
    ared = Reduce(net, 106, ga_ref, lambda i: 4 + lax.rem(i + 1, 4), credit, mc, ax, ay, al, ar)

    def mz_copy(w, r):
        return net.make(126 + r, mred.own(w), mz.at[r - 1], (net.d, w))

    def mz_out(i):
        w = chunk(i)
        mz_copy(w, lax.rem(w + Z - z, Z)).start()

    net.keep("hid", hid_ref, hid_h)
    hid_back = pltpu.make_async_copy(hid_h, hid_ref, local.at[23])
    n2_ref, dm_ref, n2t_ref, dmt_ref = b1, b2, t1, t2

    @pl.loop(0, t // BLK)
    def _(m):
        rs = rows_of(m)
        unit, _ = norm_rows(hid_ref[rs, :], None)
        n2 = jnp.where(token_mask(m, length), unit * gains_ref[1:2, :], 0.0).astype(BF16)
        n2_ref[rs, :] = n2
        n2t_ref[:, rs] = n2.T

    def chunk_left(i):
        for tag in ("x", "y", "l", "r", "c"):
            net.left(f"m{i}{tag}")

    def last_shard():
        line_wait(3)
        spread(net, "m3")

    arrived = (
        (lambda: net.got("m1c"),),
        (lambda: relay(net, "m3"), lambda: net.got("m2c")),
        (lambda: net.got("m3c"),),
        (),
    )
    middle = (
        (lambda: line_left(1), lambda: line_left(2), lambda: chunk_out(2)),
        (lambda: line_left(3), lambda: chunk_out(3), lambda: mred.p1(chunk(0), 0)),
        (lambda: mred.p2(chunk(0), 0), lambda: mred.p1(chunk(1), 1)),
        (lambda: mred.p3(chunk(0), 0), lambda: mz_out(0), lambda: mred.p1(chunk(2), 2)),
    )

    def at(i, steps):
        for k in range(Z):
            if steps[k]:

                @pl.when(i == k)
                def _():
                    for step in steps[k]:
                        step()

    f1[...] = jnp.zeros_like(f1)
    net.kept("hid")
    net.kept("q")
    net.kept("k")
    relay(net, "m2")
    net.got("m0c")
    mlp_out(f, d, gm_ref.at[chunk(0)], n2_ref, wide, hid_ref)
    peer_rows = [rows_of(net.peer(j)) for j in range(Z)]
    for j in range(1, Z):
        net.plan(f"lo{j}", lo_ref.at[peer_rows[j]], lo_out.at[z], (net.d, net.peer(j)))

    @pl.loop(0, Z)
    def _(i):
        at(i, arrived)
        ahead = gm_ref.at[chunk(i + 1)]
        pl.when(i < Z - 1)(lambda: mlp_out(f, d, ahead, n2_ref, wide, hid_ref))

        @pl.when(i == 0)
        def _():
            last_shard()
            net.got("c1", "c2", "c3")
            net.kept("c")

            for m in range(t // BLK):
                rs = slice(m * BLK, (m + 1) * BLK)
                dm = jnp.where(token_mask(m, length), cot_ref[rs, :], jnp.zeros((), BF16))
                dm_ref[rs, :] = dm
                dmt_ref[:, rs] = dm.T

        @pl.when(i == Z - 2)
        def _():
            for j in (2, 1, 3, 0):
                rs = peer_rows[j]
                lo_ref[rs, :] = hid_ref[rs, :].astype(BF16)
                if j:
                    net.go(f"lo{j}")
            hid_back.start()

        gm = gm_ref.at[chunk(i)]
        mlp_front(f, d, gm, n2_ref, dm_ref, wide)
        at(i, middle)
        at(i, tuple((functools.partial(chunk_left, k),) for k in range(Z)))
        mlp_back(f, d, gm, n2t_ref, dmt_ref, wide, f1)
        mred.p0(chunk(i), i)

    net.keep("lo", lo_ref.at[peer_rows[0]], lo_out.at[z])
    for name, src, dst in (("q2", q_h, q_ref), ("k2", k_h, k_ref)):
        net.keep(name, src, dst)
    gsum_ref[...] = jnp.zeros_like(gsum_ref)
    dh_ref, da_ref = hid_ref, b1
    hid_back.wait()

    @pl.loop(0, t // BLK)
    def _(m):
        rs = rows_of(m)
        hid = hid_ref[rs, :]
        ok = token_mask(m, length)
        unit, r = norm_rows(hid, None)
        dn2 = f1[rs, :]
        gsum_ref[1:2, :] += jnp.sum(dn2 * unit, axis=0, keepdims=True)
        e2 = dn2 * gains_ref[1:2, :]
        dh = cot_ref[rs, :].astype(F32) + r * (e2 - unit * jnp.mean(e2 * unit, axis=-1, keepdims=True))
        dh_ref[rs, :] = dh
        da_ref[rs, :] = jnp.where(ok, dh, 0.0).astype(BF16)

    mred.p2(chunk(1), 1)
    mred.p1(chunk(3), 3)

    dat_ref, n1t_ref, dctx_ref = t1, t2, cot_ref
    dat_ref[...] = da_ref[...].T
    shape = ga_ref.shape[1:5]

    @pl.loop(0, d // 256)
    def _(j):
        rs = pl.ds(pl.multiple_of(j * 256, 256), 256)
        cols = pl.ds(pl.multiple_of(3 * d + j * 256, 256), 256)
        ga_ref[3, :, :, :, :, rs] = nt(dat_ref[...], ctxt_ref[rs, :]).astype(BF16).reshape(shape + (256,))
        dctx = nn(da_ref[...], wa_cols(wa_ref, cols)).astype(BF16)
        dctx_ref[:, rs] = dctx
        prod = dctx.T.astype(F32) * ctxt_ref[rs, :].astype(F32)
        for h in range(4):
            dlt_ref[pl.ds(j * 4 + h, 1), :] = jnp.sum(prod[h * HEAD : (h + 1) * HEAD], axis=0, keepdims=True)

    mred.p2(chunk(2), 2)
    ared.p0(3, 3)

    @pl.loop(0, t // BLK)
    def _(m):
        rs = rows_of(m)
        unit, _ = norm_rows(x_ref[rs, :].astype(F32), None)
        n1t_ref[:, rs] = (unit * gains_ref[0:1, :]).astype(BF16).T

    net.kept("q2")
    net.kept("k2")
    dk_acc, dv_acc = f1.at[:, 0:128], f1.at[:, 128:256]
    lanes = dict(o=slice(512 - 128, 512), q=slice(0, 384), t=slice(512, 768))

    def to_owner(base, w, tag):
        r = lax.rem(w + Z - z, Z)

        @pl.when(r != 0)
        def _():
            net.make(base + r - 1, pack_ref.at[w, :, lanes[tag]], az.at[r - 1, :, lanes[tag]], (net.d, w)).start()

    def pack_out():
        for w in range(Z):
            at = PAIRS.index(w) * 128
            pack_ref[w, :, lanes["o"]] = ared.own(3)[:, at : at + 128]
            to_owner(132, w, "o")

    def pack_pairs(g):
        for s in range(2):
            w = PAIRS[2 * g + s]
            for k in range(3):
                pack_ref[w, :, k * 128 : (k + 1) * 128] = ared.own(g)[:, k * 256 + s * 128 : k * 256 + s * 128 + 128]
            to_owner(135, w, "q")

    def pack_thirds():
        for w, j, value in packed_thirds(ared.own):
            pack_ref[w, :, 512 + j * 128 : 640 + j * 128] = value
        for w in range(Z):
            to_owner(138, w, "t")

    def heads_out(g):
        for k in range(3):
            cols = pl.ds(pl.multiple_of(k * d + g * 256, 256), 256)
            ga_ref[g, :, :, :, :, k * 256 : (k + 1) * 256] = nn(n1t_ref[...], wide[:, cols]).astype(BF16).reshape(shape + (256,))
        ared.p0(g, g)

    first = (
        (lambda: ared.p1(3, 3),),
        (lambda: ared.p2(3, 3), lambda: ared.p1(0, 0)),
        (lambda: ared.p2(0, 0), lambda: ared.p1(1, 1)),
    )
    second = (
        (lambda: mred.p3(chunk(2), 2), lambda: mz_out(2), lambda: mred.p2(chunk(3), 3)),
        (lambda: mred.p3(chunk(3), 3), lambda: mz_out(3), lambda: ared.p3(3, 3), pack_out),
        (lambda: ared.p3(0, 0), lambda: pack_pairs(0), lambda: mred.p3(chunk(1), 1)),
    )

    @pl.loop(0, 3)
    def _(g):
        @pl.loop(0, 2)
        def _(s):
            p = 2 * g + s
            attend_back(t, d, length, q_ref, k_ref, v_ref, dctx_ref, lse_ref, dlt_ref, cos_ref, sin_ref, wide, dk_acc, dv_acc, p, p + 1)
            for k in range(3):
                for steps, which in ((first, 0), (second, 1)):

                    @pl.when((g == k) & (s == which))
                    def _():
                        for step in steps[k]:
                            step()

        heads_out(g)

    gx_ref = b1
    for j in (2, 1, 3, 0):
        m = net.peer(j)
        rs = rows_of(m)
        dn1 = nt(wide[rs, :], wa_cols(wa_ref, slice(0, 3 * d)))
        unit, r = norm_rows(x_ref[rs, :].astype(F32), None)
        gsum_ref[0:1, :] += jnp.sum(dn1 * unit, axis=0, keepdims=True)
        e1 = dn1 * gains_ref[0:1, :]
        gx_ref[rs, :] = (dh_ref[rs, :] + r * (e1 - unit * jnp.mean(e1 * unit, axis=-1, keepdims=True))).astype(BF16)
        if j:
            net.start(f"gx{j}", gx_ref.at[rs], gx_out.at[z], (net.d, m))
        else:
            net.keep("gx", gx_ref.at[rs], gx_out.at[z])
        if j == 2:
            ared.p2(1, 1)
            ared.p1(2, 2)
        elif j == 3:
            ared.p3(1, 1)
            pack_pairs(1)
        elif j == 0:
            ared.p2(2, 2)
    steps = all_sum(net, "s", gsum_ref, boxes2_ref, last=True)
    next(steps)
    next(steps)
    ared.p3(2, 2)
    pack_thirds()
    next(steps)
    next(steps)
    total = mred.own(z)[...].astype(F32)
    for r in range(1, Z):
        mz_copy(net.peer(r), r).wait_recv()
        total = total + mz[r - 1].astype(F32)
    rows, half = total.shape[0], total.shape[1] // 2
    f1[0:rows, :] = total[:, :half]
    f1[rows : 2 * rows, :] = total[:, half:]

    parts = [
        net.make(base + r - 1, pack_ref.at[net.peer(r), :, lanes[tag]], az.at[r - 1, :, lanes[tag]], (net.d, net.peer(r)))
        for base, tag in ((132, "o"), (135, "q"), (138, "t"))
        for r in range(1, Z)
    ]
    for copy in parts:
        copy.wait_recv()
    total = pack_ref[z].astype(F32)
    for i in range(Z - 1):
        total = total + az[i].astype(F32)
    f1[2 * rows : 3 * rows, :] = total
    net.keep("grads", f1.at[0 : 3 * rows], grads_out)
    next(steps)
    gg_ref[...] = pltpu.roll(boxes2_ref[9], d - spot, 1)[0:2, 0 : gs_ref.shape[1]]
    net.got(*(f"{n}{j}" for n in ("lo", "gx") for j in range(1, Z)))
    for name in ("lo", "gx", "grads"):
        net.kept(name)
    for i in range(Z):
        mred.sent(chunk(i), i)
        ared.sent(i, i)
    for copy in parts:
        copy.wait_send()
    for r in range(1, Z):
        mz_copy(net.peer(r), r).wait_send()
    net.finish()


VM = pl.BlockSpec(memory_space=pltpu.VMEM)
SM = pl.BlockSpec(memory_space=pltpu.SMEM)


def call(kernel, ins, outs, scratch):
    return pl.pallas_call(
        kernel,
        out_shape=[jax.ShapeDtypeStruct(s, dt) for s, dt in outs],
        in_specs=[SM] + [VM] * (len(ins) - 1),
        out_specs=[VM] * len(outs),
        scratch_shapes=[pltpu.VMEM(s, dt) for s, dt in scratch],
        compiler_params=pltpu.CompilerParams(vmem_limit_bytes=60 * 2**20),
    )(*ins)


def backward(length, x, cot, gains, wa, wm, cosine, sine, q, k, v, ctxt, lse, hid):
    t, d = x.shape
    f = wm.shape[-1] // 3
    heads = lse.shape[0]
    td, dt = ((t, d), BF16), ((d, t), BF16)
    lo, dh, da, gm, gg2 = call(
        k2,
        (length, cot, gains, hid, wm),
        (td, ((t, d), F32), td, (wm.shape, BF16), ((1, d), F32)),
        (td, td, dt, dt, ((t, 3 * f), BF16), ((t, d), F32), ((t, d), F32)),
    )
    gx, ga, gg1 = call(
        k3,
        (length, x, gains, wa, cosine, sine, q, k, v, ctxt, lse, dh, da),
        (td, (wa.shape, BF16), ((1, d), F32)),
        (td, dt, dt, td, ((heads, t), F32), ((t, 3 * d), BF16), ((t, 128), F32), ((t, 128), F32), ((t, d), F32)),
    )
    return lo, gx, ga, gm, jnp.concatenate([gg1, gg2])


def one_sequence(length, x, cot, gains, wa, wm, cosine, sine):
    t, d = x.shape
    heads = -(-d // HEAD // 8) * 8
    td, dt = ((t, d), BF16), ((d, t), BF16)
    kept = call(k1_alone, (length, x, gains, wa, cosine, sine), (td, td, td, dt, ((heads, t), F32), ((t, d), F32)), (td,))
    return backward(length, x, cot, gains, wa, wm, cosine, sine, *kept)


def pack_weights(w_qkv, w_out, w_gate_up, w_down):
    attn = jnp.stack([w_qkv[0], w_qkv[1], w_qkv[2], w_out.T], axis=1)
    mlp = jnp.concatenate([w_gate_up[0], w_gate_up[1], w_down.T], axis=1)
    return attn, mlp


def unpack_grads(g_attn, g_mlp, fw):
    g_qkv = jnp.transpose(g_attn[:, :3], (1, 0, 2))
    g_gate_up = jnp.stack([g_mlp[:, i * fw : (i + 1) * fw] for i in range(2)])
    return g_qkv, g_attn[:, 3].T, g_gate_up, g_mlp[:, 2 * fw :].T


def to_sequences(local):
    return lax.all_to_all(local, "tp", split_axis=0, concat_axis=1, tiled=True)


def to_positions(whole):
    return lax.all_to_all(whole, "tp", split_axis=1, concat_axis=0, tiled=True)


def fused_layer(lengths, tokens, cotangent, w_qkv, w_out, w_gate_up, w_down, gains, cosine, sine):
    batch, part, d = tokens.shape
    t, rows, f3 = part * Z, w_qkv.shape[1], 3 * w_gate_up.shape[2]
    heads = -(-d // HEAD // 8) * 8
    pairs = 2 * HEAD
    four = (w_qkv[0], w_qkv[1], w_qkv[2], w_out.T)
    was = jnp.concatenate([w[:, :pairs] for w in four] + [w[:, pairs:] for w in four], axis=1)
    hbm = pl.BlockSpec(memory_space=pl.ANY)
    moved = ((Z, part, d), BF16)
    td, dt, big, small = ((t, d), BF16), ((d, t), BF16), ((t, d), F32), ((8, d), F32)
    outs = (moved, moved, ((3 * rows, d), F32), (gains.shape, F32), td, td, big)

    def boxes(cols, last=Z - 1):
        pair = ((4, 2, rows, cols // 2), BF16)
        one = ((4, rows, cols // 2), BF16)
        return [pair, pair, one, one, ((last, rows, cols), BF16)]

    wm = ((Z, 2, 2, 2, rows, f3), BF16)
    stage = ((Z, rows, d), BF16)
    lse = ((heads, t), F32)
    scratch = [td, td] + [(cosine.shape, F32)] * 2 + [((4, 2, rows, 4 * d), BF16), wm, dt, lse, big]
    scratch += [td, td, td, dt, dt, ((t, 3 * d), BF16), big, lse, small, small, ((10, 8, d), F32), ((10, 8, d), F32), stage]
    scratch += [((2, 2, 2, rows, f3), BF16)] + boxes(f3) + [((4, 2, 2, 2, rows, d), BF16)] + boxes(d)
    return pl.pallas_call(
        layer_kernel,
        out_shape=[jax.ShapeDtypeStruct(s, dt_) for s, dt_ in outs],
        in_specs=[SM, VM] + [hbm] * 7,
        out_specs=[hbm, hbm, hbm, VM, hbm, hbm, hbm],
        scratch_shapes=[pltpu.VMEM(s, dt_) for s, dt_ in scratch]
        + [pltpu.SemaphoreType.DMA((144,)), pltpu.SemaphoreType.DMA((144,)), pltpu.SemaphoreType.DMA((24,)), pltpu.SemaphoreType.REGULAR],
        compiler_params=pltpu.CompilerParams(collective_id=0, has_side_effects=True, vmem_limit_bytes=62 * 2**20),
    )(lengths, gains, was, tokens, cotangent, w_gate_up, w_down.T, cosine, sine)[:4]


def fits(mesh_dp, tokens, w_qkv, w_gate_up):
    tp = lax.axis_size("tp")
    rows, hw = w_qkv.shape[1:]
    return (
        mesh_dp == 8 and tp == Z and tokens.shape[0] == Z and hw == 3 * HEAD and rows % 16 == 0
        and w_gate_up.shape[2] % 256 == 0 and 3 * w_gate_up.shape[2] <= 2 * tokens.shape[2] and tokens.shape[1] % BLK == 0
    )


def body(tokens, lengths, w_qkv, w_out, w_gate_up, w_down, gains, cotangent):
    tp, dp = lax.axis_size("tp"), lax.axis_size("dp")
    batch, part, d = tokens.shape
    n, t = batch // tp, part * tp
    fw = w_gate_up.shape[2]
    cosine, sine = map(jnp.asarray, rope_np(t))
    attn, mlp = pack_weights(w_qkv, w_out, w_gate_up, w_down)
    own = lax.dynamic_slice_in_dim(lengths, lax.axis_index("tp") * n, n)
    if fits(dp, tokens, w_qkv, w_gate_up):
        out, gx, grads, s_gains = fused_layer(lengths, tokens, cotangent, w_qkv, w_out, w_gate_up, w_down, gains, cosine, sine)
        pairs, rows = 2 * HEAD, w_qkv.shape[1]
        s_mlp = jnp.concatenate([grads[:rows], grads[rows : 2 * rows]], axis=1)
        s_attn = grads[2 * rows :]
        first, third = s_attn[:, : 4 * pairs], s_attn[:, 4 * pairs :]
        s_attn = jnp.concatenate([first.reshape(-1, 4, pairs), third.reshape(-1, 4, HEAD)], axis=2)
        gx = gx.astype(F32)
    else:
        full_gains = lax.all_gather(gains, ("dp", "tp"), axis=1, tiled=True)
        full_gains = jnp.pad(full_gains, ((0, 6), (0, 0)))
        x16 = to_sequences(tokens)
        wa = lax.all_gather(attn, "tp", axis=2, tiled=True).reshape(attn.shape[0], 4 * d)
        wa = lax.all_gather(wa, "dp", axis=0, tiled=True).reshape(1, 1, d, 4 * d)
        wm = lax.all_gather(lax.all_gather(mlp, "tp", axis=0), "dp", axis=1, tiled=True).reshape(tp, 1, 1, d, 3 * fw)
        cot16 = to_sequences(cotangent)
        los, gxs, ga, gm, gg = [], [], 0.0, 0.0, 0.0
        for i in range(n):
            lo, gx, a, m, g = one_sequence(own[i : i + 1], x16[i], cot16[i], full_gains, wa, wm, cosine, sine)
            los.append(lo)
            gxs.append(gx)
            ga, gm, gg = ga + a.astype(F32), gm + m.astype(F32), gg + g
        out = to_positions(jnp.stack(los))
        gx = to_positions(jnp.stack(gxs)).astype(F32)
        ga, gm = ga.reshape(d, 4, d), gm.reshape(tp, d, 3 * fw)
        s_mlp = lax.psum_scatter(lax.psum_scatter(gm, "dp", scatter_dimension=1, tiled=True), "tp", scatter_dimension=0)
        s_attn = lax.psum_scatter(ga.reshape(d, 4 * d), "dp", scatter_dimension=0, tiled=True)
        s_attn = lax.psum_scatter(s_attn.reshape(-1, 4, d), "tp", scatter_dimension=2, tiled=True)
        s_gains = lax.psum_scatter(gg, ("dp", "tp"), scatter_dimension=1, tiled=True)
    return (out, gx) + unpack_grads(s_attn, s_mlp, fw) + (s_gains,)


def solution(mesh):
    act = P("dp", "tp", None)
    cols, rows, gain = P(None, "dp", "tp"), P("tp", "dp"), P(None, ("dp", "tp"))
    return jax.shard_map(
        body,
        mesh=mesh,
        in_specs=(act, P("dp"), cols, rows, cols, rows, gain, act),
        out_specs=(act, act, cols, rows, cols, rows, gain),
        check_vma=False,
    )
```

```python
import functools

import numpy as np
import jax
import jax.numpy as jnp
from jax import lax
from jax.experimental import pallas as pl
from jax.experimental.pallas import tpu as pltpu
from jax.sharding import PartitionSpec as P

F32 = jnp.float32
BF16 = jnp.bfloat16
HEAD = 64
EPS = 1e-6
LOG2E = 1.4426950408889634
C2 = LOG2E * HEAD**-0.5
NEG = -1e30
BLK = 256


def dg(a, b, ca, cb):
    return lax.dot_general(a, b, (((ca,), (cb,)), ((), ())), preferred_element_type=F32)


def nn(a, b):
    return dg(a, b, 1, 0)


def nt(a, b):
    return dg(a, b, 1, 1)


def tn(a, b):
    return dg(a, b, 0, 0)


def rows_of(m):
    return pl.ds(pl.multiple_of(m * BLK, BLK), BLK)


def wa_cols(wa_ref, cols):
    part = wa_ref[:, :, :, cols]
    return part.reshape(-1, part.shape[-1])


def half_lane():
    return lax.broadcasted_iota(jnp.int32, (1, 128), 1) % HEAD < HEAD // 2


def head_lane(h):
    lane = lax.broadcasted_iota(jnp.int32, (1, 128), 1)
    return lane < HEAD if h == 0 else lane >= HEAD


def turned(v):
    return jnp.where(half_lane(), pltpu.roll(v, 96, 1), pltpu.roll(v, 32, 1))


def norm_rows(x, gain):
    r = lax.rsqrt(jnp.mean(x * x, axis=-1, keepdims=True) + EPS)
    return x * r, r


def norm_stage(t, x_ref, gains_ref, n1_ref):
    @pl.loop(0, t // BLK)
    def _(m):
        rs = rows_of(m)
        unit, _ = norm_rows(x_ref[rs, :].astype(F32), None)
        n1_ref[rs, :] = (unit * gains_ref[0:1, :]).astype(BF16)


def qkv_stage(t, d, n1_ref, wa_ref, cos_ref, sin_ref, outs):
    for c, out in enumerate(outs):
        if out is None:
            continue

        @pl.loop(0, d // 256)
        def _(j, c=c, out=out):
            cols = pl.ds(pl.multiple_of(c * d + j * 256, 256), 256)
            raw = nn(n1_ref[...], wa_cols(wa_ref, cols))
            for s in range(2):
                part = raw[:, s * 128 : (s + 1) * 128]
                if c < 2:
                    part = part * cos_ref[...] + turned(part) * sin_ref[...]
                out[:, pl.ds(pl.multiple_of(j * 256 + s * 128, 128), 128)] = part.astype(BF16)


def key_bias(t, length):
    pos = lax.broadcasted_iota(jnp.int32, (t, 1), 0)
    return jnp.where(pos < length, 0.0, NEG).astype(BF16)


def causal_block():
    key = lax.broadcasted_iota(jnp.int32, (BLK, BLK), 0)
    query = lax.broadcasted_iota(jnp.int32, (BLK, BLK), 1)
    return key <= query


def score_operands(h, qp, kp, bias):
    mine = head_lane(h)
    lane = lax.broadcasted_iota(jnp.int32, (1, 128), 1)
    spare = lane == (HEAD if h == 0 else 0)
    zero = jnp.zeros((), BF16)
    q_m = jnp.where(mine, qp, zero)
    k_m = jnp.where(mine, kp, zero)
    q_s = jnp.where(spare, jnp.ones((), BF16), q_m)
    k_s = jnp.where(spare, bias, k_m)
    return q_m, k_m, q_s, k_s


def mask_diag(s, i):
    if i == 0:
        return jnp.where(causal_block(), s, NEG)
    return jnp.concatenate([s[: i * BLK], jnp.where(causal_block(), s[i * BLK :], NEG)], axis=0)


def attend_stage(t, d, length, q_ref, k_ref, v_ref, ctxt_ref, lse_ref, first, last):
    bias = key_bias(t, length)

    @pl.loop(first, last)
    def _(p):
        cols = pl.ds(pl.multiple_of(p * 128, 128), 128)
        qp, kp, vp = q_ref[:, cols], k_ref[:, cols], v_ref[:, cols]
        for h in range(2):
            _, _, q_s, k_s = score_operands(h, qp, kp, bias)
            for i in range(t // BLK):
                n = (i + 1) * BLK
                s = mask_diag(nt(k_s[:n], q_s[i * BLK : n]), i)
                top = jnp.max(s, axis=0, keepdims=True)
                e = jnp.exp2((s - top) * C2)
                total = jnp.sum(e, axis=0, keepdims=True)
                o = tn(vp[:n], e.astype(BF16))[h * HEAD : (h + 1) * HEAD] / total
                ctxt_ref[pl.ds(pl.multiple_of(p * 128 + h * HEAD, HEAD), HEAD), i * BLK : n] = o.astype(BF16)
                lse_ref[pl.ds(p * 2 + h, 1), i * BLK : n] = top * C2 + jnp.log2(total)


def out_stage(t, d, length, x_ref, wa_ref, ctxt_ref, hid_ref):
    out = dg(ctxt_ref[...], wa_cols(wa_ref, slice(3 * d, 4 * d)), 0, 1)
    pos = lax.broadcasted_iota(jnp.int32, (t, 1), 0)
    hid_ref[...] = x_ref[...].astype(F32) + jnp.where(pos < length, out, 0.0)


def k1_alone(len_ref, x_ref, gains_ref, wa_ref, cos_ref, sin_ref, q_ref, k_ref, v_ref, ctxt_ref, lse_ref, hid_ref, n1_ref):
    t, d = x_ref.shape
    length = len_ref[0]
    norm_stage(t, x_ref, gains_ref, n1_ref)
    qkv_stage(t, d, n1_ref, wa_ref, cos_ref, sin_ref, (q_ref, k_ref, v_ref))
    attend_stage(t, d, length, q_ref, k_ref, v_ref, ctxt_ref, lse_ref, 0, d // 128)
    out_stage(t, d, length, x_ref, wa_ref, ctxt_ref, hid_ref)


def token_mask(m, length):
    pos = m * BLK + lax.broadcasted_iota(jnp.int32, (BLK, 1), 0)
    return pos < length


def chunk_cols(wm, d, lo, hi):
    return wm[..., lo:hi].reshape(d, hi - lo)


def mlp_front(f, d, wm, n2_ref, dm_ref, wide):
    w = 256
    for j in range(f // w):
        lo, hi = j * w, (j + 1) * w
        gate = nn(n2_ref[...], chunk_cols(wm, d, lo, hi))
        up = nn(n2_ref[...], chunk_cols(wm, d, f + lo, f + hi))
        d_act = nn(dm_ref[...], chunk_cols(wm, d, 2 * f + lo, 2 * f + hi))
        s = 1.0 / (1.0 + jnp.exp2(gate * (-LOG2E)))
        sw = gate * s
        wide[:, 2 * f + lo : 2 * f + hi] = (sw * up).astype(BF16)
        wide[:, lo:hi] = (d_act * up * (s + sw * (1.0 - s))).astype(BF16)
        wide[:, f + lo : f + hi] = (d_act * sw).astype(BF16)


def mlp_out(f, d, wm, n2_ref, wide, mlp_ref):
    w = 256
    for j in range(f // w):
        lo, hi = j * w, (j + 1) * w
        gate = nn(n2_ref[...], chunk_cols(wm, d, lo, hi))
        up = nn(n2_ref[...], chunk_cols(wm, d, f + lo, f + hi))
        wide[:, lo:hi] = (gate * up / (1.0 + jnp.exp2(gate * (-LOG2E)))).astype(BF16)
    mlp_ref[...] += nt(wide[:, :f], chunk_cols(wm, d, 2 * f, 3 * f))


def mlp_back(f, d, wm, n2t_ref, dmt_ref, wide, dn2_ref):
    w = 256
    dn2_ref[...] += nt(wide[:, : 2 * f], chunk_cols(wm, d, 0, 2 * f))
    for j in range(3 * f // w):
        cols = slice(j * w, (j + 1) * w)
        left = n2t_ref if j * w < 2 * f else dmt_ref
        wm[..., cols] = nn(left[...], wide[:, cols]).astype(BF16).reshape(wm.shape[:-1] + (w,))


def k2(len_ref, cot_ref, gains_ref, hid_ref, wm_ref, lo_ref, dh_ref, da_ref, gm_ref, gg_ref,
       n2_ref, dm_ref, n2t_ref, dmt_ref, wide, mlp_ref, dn2_ref):
    t, d = cot_ref.shape
    tp, f = wm_ref.shape[0], wm_ref.shape[-1] // 3
    length = len_ref[0]

    @pl.loop(0, t // BLK)
    def _(m):
        rs = rows_of(m)
        unit, _ = norm_rows(hid_ref[rs, :], None)
        n2 = (unit * gains_ref[1:2, :]).astype(BF16)
        n2_ref[rs, :] = n2
        n2t_ref[:, rs] = n2.T
        dm = jnp.where(token_mask(m, length), cot_ref[rs, :], jnp.zeros((), BF16))
        dm_ref[rs, :] = dm
        dmt_ref[:, rs] = dm.T

    mlp_ref[...] = jnp.zeros_like(mlp_ref)
    dn2_ref[...] = jnp.zeros_like(dn2_ref)

    @pl.loop(0, tp)
    def _(z):
        gm_ref[z] = wm_ref[z]
        mlp_out(f, d, gm_ref.at[z], n2_ref, wide, mlp_ref)
        mlp_front(f, d, gm_ref.at[z], n2_ref, dm_ref, wide)
        mlp_back(f, d, gm_ref.at[z], n2t_ref, dmt_ref, wide, dn2_ref)

    gg_ref[...] = jnp.zeros_like(gg_ref)

    @pl.loop(0, t // BLK)
    def _(m):
        rs = rows_of(m)
        hid = hid_ref[rs, :]
        ok = token_mask(m, length)
        lo_ref[rs, :] = (hid + jnp.where(ok, mlp_ref[rs, :], 0.0)).astype(BF16)
        unit, r = norm_rows(hid, None)
        dn2 = dn2_ref[rs, :]
        gg_ref[...] += jnp.sum(dn2 * unit, axis=0, keepdims=True)
        e2 = dn2 * gains_ref[1:2, :]
        dh = cot_ref[rs, :].astype(F32) + r * (e2 - unit * jnp.mean(e2 * unit, axis=-1, keepdims=True))
        dh_ref[rs, :] = dh
        da_ref[rs, :] = jnp.where(ok, dh, 0.0).astype(BF16)


def attend_back(t, d, length, q_ref, k_ref, v_ref, dctx_ref, lse_ref, dlt_ref, cos_ref, sin_ref, dqkv_ref, dk_acc, dv_acc, first, last):
    bias = key_bias(t, length)

    @pl.loop(first, last)
    def _(p):
        cols = pl.ds(pl.multiple_of(p * 128, 128), 128)
        qp, kp, vp, gp = q_ref[:, cols], k_ref[:, cols], v_ref[:, cols], dctx_ref[:, cols]
        dk_acc[...] = jnp.zeros_like(dk_acc)
        dv_acc[...] = jnp.zeros_like(dv_acc)
        ops = [score_operands(h, qp, kp, bias) for h in range(2)]
        for i in range(t // BLK):
            n = (i + 1) * BLK
            qs = slice(i * BLK, n)
            dq = None
            for h in range(2):
                q_m, k_m, q_s, k_s = ops[h]
                g_m = jnp.where(head_lane(h), gp[qs], jnp.zeros((), BF16))
                s = mask_diag(nt(k_s[:n], q_s[qs]), i)
                pr = jnp.exp2(s * C2 - lse_ref[pl.ds(p * 2 + h, 1), qs])
                dp = nt(vp[:n], g_m)
                ds = (pr * (dp - dlt_ref[pl.ds(p * 2 + h, 1), qs])).astype(BF16)
                dv_acc[:n, :] += nn(pr.astype(BF16), g_m)
                dk_acc[:n, :] += nn(ds, q_m[qs])
                part = tn(ds, k_m[:n])
                dq = part if dq is None else dq + part
            dq = dq * (HEAD**-0.5)
            dqkv_ref[qs, cols] = (dq * cos_ref[qs, :] - turned(dq) * sin_ref[qs, :]).astype(BF16)
        dk = dk_acc[...] * (HEAD**-0.5)
        dqkv_ref[:, pl.ds(pl.multiple_of(d + p * 128, 128), 128)] = (dk * cos_ref[...] - turned(dk) * sin_ref[...]).astype(BF16)
        dqkv_ref[:, pl.ds(pl.multiple_of(2 * d + p * 128, 128), 128)] = dv_acc[...].astype(BF16)


def k3(len_ref, x_ref, gains_ref, wa_ref, cos_ref, sin_ref, q_ref, k_ref, v_ref, ctxt_ref, lse_ref, dh_ref, da_ref,
       gx_ref, ga_ref, gg_ref, n1_ref, n1t_ref, dat_ref, dctx_ref, dlt_ref, dqkv_ref, dk_acc, dv_acc, dn1_ref):
    t, d = x_ref.shape
    length = len_ref[0]

    dat_ref[...] = da_ref[...].T

    @pl.loop(0, d // 256)
    def _(j):
        rs = pl.ds(pl.multiple_of(j * 256, 256), 256)
        cols = pl.ds(pl.multiple_of(3 * d + j * 256, 256), 256)
        ga_ref[:, :, :, cols] = nt(dat_ref[...], ctxt_ref[rs, :]).astype(BF16).reshape(ga_ref.shape[:3] + (256,))
        dctx = nn(da_ref[...], wa_cols(wa_ref, cols)).astype(BF16)
        dctx_ref[:, rs] = dctx
        prod = dctx.T.astype(F32) * ctxt_ref[rs, :].astype(F32)
        for h in range(4):
            dlt_ref[pl.ds(j * 4 + h, 1), :] = jnp.sum(prod[h * HEAD : (h + 1) * HEAD], axis=0, keepdims=True)

    attend_back(t, d, length, q_ref, k_ref, v_ref, dctx_ref, lse_ref, dlt_ref, cos_ref, sin_ref, dqkv_ref, dk_acc, dv_acc, 0, d // 128)

    @pl.loop(0, t // BLK)
    def _(m):
        rs = rows_of(m)
        unit, _ = norm_rows(x_ref[rs, :].astype(F32), None)
        n1t_ref[:, rs] = (unit * gains_ref[0:1, :]).astype(BF16).T

    @pl.loop(0, 3 * d // 256)
    def _(j):
        cols = pl.ds(pl.multiple_of(j * 256, 256), 256)
        ga_ref[:, :, :, cols] = nn(n1t_ref[...], dqkv_ref[:, cols]).astype(BF16).reshape(ga_ref.shape[:3] + (256,))

    dn1_ref[...] = nt(dqkv_ref[...], wa_cols(wa_ref, slice(0, 3 * d)))

    gg_ref[...] = jnp.zeros_like(gg_ref)

    @pl.loop(0, t // BLK)
    def _(m):
        rs = rows_of(m)
        unit, r = norm_rows(x_ref[rs, :].astype(F32), None)
        dn1 = dn1_ref[rs, :]
        gg_ref[...] += jnp.sum(dn1 * unit, axis=0, keepdims=True)
        e1 = dn1 * gains_ref[0:1, :]
        gx_ref[rs, :] = (dh_ref[rs, :] + r * (e1 - unit * jnp.mean(e1 * unit, axis=-1, keepdims=True))).astype(BF16)


def rope_np(t):
    half = HEAD // 2
    freqs = np.float32(10000.0) ** (np.float32(-2.0) * np.arange(half, dtype=np.float32) / np.float32(HEAD))
    ang = np.arange(t, dtype=np.float32)[:, None] * freqs[None, :].astype(np.float32)
    c, s = np.cos(ang), np.sin(ang)
    return np.concatenate([c, c, c, c], 1).astype(np.float32), np.concatenate([-s, s, -s, s], 1).astype(np.float32)


MESH = pl.DeviceIdType.MESH
Z = 4
PAIRS = (0, 2, 1, 3)


def flip(d, bit):
    return d + bit - 2 * bit * lax.rem(d // bit, 2)


class Net:
    def __init__(self, send, recv, local):
        self.d, self.z = lax.axis_index("dp"), lax.axis_index("tp")
        self.yx, self.c = self.d // 2, lax.rem(self.d, 2)
        self.x, self.y, self.core = ((flip(self.d, b), self.z) for b in (2, 4, 1))
        self.send, self.recv, self.local = send, recv, local
        self.copies, self.own, self.gone = {}, {}, set()

    def peer(self, r):
        return lax.rem(self.z + r, Z)

    def source(self, r):
        return lax.rem(self.z + Z - r, Z)

    def barrier(self):
        sem = pltpu.get_barrier_semaphore()
        for dev in (self.x, self.y, self.core) + tuple((self.d, self.peer(r)) for r in range(1, Z)):
            pl.semaphore_signal(sem, inc=1, device_id=dev, device_id_type=MESH)
        pl.semaphore_wait(sem, 6)

    def make(self, i, src, dst, dev):
        return pltpu.make_async_remote_copy(
            src_ref=src, dst_ref=dst, send_sem=self.send.at[i], recv_sem=self.recv.at[i], device_id=dev, device_id_type=MESH
        )

    def plan(self, name, src, dst, dev):
        self.copies[name] = self.make(len(self.copies), src, dst, dev)

    def go(self, *names):
        for name in names:
            self.copies[name].start()

    def start(self, name, src, dst, dev):
        self.plan(name, src, dst, dev)
        self.go(name)

    def keep(self, name, src, dst):
        copy = pltpu.make_async_copy(src, dst, self.local.at[len(self.own)])
        copy.start()
        self.own[name] = copy

    def got(self, *names):
        for name in names:
            self.copies[name].wait_recv()

    def kept(self, name):
        self.own[name].wait()

    def left(self, name):
        self.copies[name].wait_send()
        self.gone.add(name)

    def finish(self):
        for name, copy in self.copies.items():
            if name not in self.gone:
                copy.wait_send()


def plan_gather(net, tag, own, slab, halves):
    kx, ky = flip(net.yx, 1), flip(net.yx, 2)
    net.plan(tag + "x", own, slab(net.yx), net.x)
    net.plan(tag + "y", own, slab(net.yx), net.y)
    net.plan(tag + "l", slab(kx).at[:, halves[0]], slab(kx).at[:, halves[0]], net.y)
    net.plan(tag + "r", slab(ky).at[:, halves[1]], slab(ky).at[:, halves[1]], net.x)


def spread(net, tag):
    net.go(tag + "x", tag + "y")


def relay(net, tag):
    net.got(tag + "x")
    net.go(tag + "l")
    net.got(tag + "y")
    net.go(tag + "r")


def all_sum(net, tag, own, boxes, last=False):
    def over_tp(src, out):
        for r in range(1, Z):
            net.start(f"{tag}z{r}", src, boxes.at[r - 1], (net.d, net.peer(r)))
        yield
        net.got(*(f"{tag}z{r}" for r in range(1, Z)))
        boxes[out] = src[...] + (boxes[0] + boxes[1] + boxes[2])

    def over_dp(src, outs):
        for i, (name, dev) in enumerate((("x", net.x), ("y", net.y), ("c", net.core))):
            net.start(tag + name, src, boxes.at[3 + i], dev)
            yield
            net.got(tag + name)
            boxes[outs[i]] = src[...] + boxes[3 + i]
            src = boxes.at[outs[i]]

    if last:
        yield from over_dp(own, (6, 7, 8))
        yield from over_tp(boxes.at[8], 9)
    else:
        yield from over_tp(own, 6)
        yield from over_dp(boxes.at[6], (7, 8, 9))
    yield


def lane_pairs(stage, hw):
    low = lax.broadcasted_iota(jnp.int32, (1, 128), 1) < HEAD
    parts = [[stage[z][:, c * 128 : (c + 1) * 128] for z in PAIRS] for c in range(4)]
    for j in range(Z // 2):
        for g in range(2):
            cols = slice(512 + g * 128, 640 + g * 128)
            a, b = stage[2 * j][:, cols].astype(F32), stage[2 * j + 1][:, cols].astype(F32)
            parts[2 * g].append(jnp.where(low, a, pltpu.roll(b, HEAD, 1)).astype(BF16))
            parts[2 * g + 1].append(jnp.where(low, pltpu.roll(a, HEAD, 1), b).astype(BF16))
    return parts


class Reduce:
    def __init__(self, net, base, data, use, credit, rc, r1x, r1y, r2l, r2r):
        self.net, self.base, self.data, self.use, self.credit = net, base, data, use, credit
        self.rc, self.r1x, self.r1y, self.r2l, self.r2r = rc, r1x, r1y, r2l, r2r
        self.x, self.y = lax.rem(net.yx, 2), net.yx // 2
        half = data.shape[-1] // 2
        self.lo, self.hi = slice(0, half), slice(half, 2 * half)

    def slot(self, i):
        return self.rc.at[lax.rem(self.use(i), 2), :, :, :, 0 : self.data.shape[-1]]

    def copies0(self, g, i):
        return [self.net.make(self.base + i, self.data.at[g, :, :, 1 - self.net.c], self.slot(i), self.net.core)]

    def copies1(self, g, i):
        net, c = self.net, self.net.c
        return [
            net.make(self.base + 4 + i, self.data.at[g, :, 1 - self.x, c, :, self.lo], self.r1x.at[i], net.x),
            net.make(self.base + 8 + i, self.data.at[g, 1 - self.y, :, c, :, self.hi], self.r1y.at[i], net.y),
        ]

    def copies2(self, g, i):
        net, c = self.net, self.net.c
        return [
            net.make(self.base + 12 + i, self.data.at[g, 1 - self.y, self.x, c, :, self.lo], self.r2l.at[i], net.y),
            net.make(self.base + 16 + i, self.data.at[g, self.y, 1 - self.x, c, :, self.hi], self.r2r.at[i], net.x),
        ]

    def add(self, at, value):
        self.data[at] = (self.data[at].astype(F32) + value.astype(F32)).astype(BF16)

    def p0(self, g, i):
        @pl.when(self.use(i) >= 2)
        def _():
            pl.semaphore_wait(self.credit, 1)

        for copy in self.copies0(g, i):
            copy.start()

    def p1(self, g, i):
        for copy in self.copies0(g, i):
            copy.wait_recv()
        for y in range(2):
            for x in range(2):
                self.add((g, y, x, self.net.c), self.slot(i)[y, x])

        @pl.when(self.use(i) < 6)
        def _():
            pl.semaphore_signal(self.credit, inc=1, device_id=self.net.core, device_id_type=MESH)

        for copy in self.copies1(g, i):
            copy.start()

    def p2(self, g, i):
        for copy in self.copies1(g, i):
            copy.wait_recv()
        for k in range(2):
            self.add((g, k, self.x, self.net.c, slice(None), self.lo), self.r1x[i, k])
            self.add((g, self.y, k, self.net.c, slice(None), self.hi), self.r1y[i, k])
        for copy in self.copies2(g, i):
            copy.start()

    def p3(self, g, i):
        for copy in self.copies2(g, i):
            copy.wait_recv()
        self.add((g, self.y, self.x, self.net.c, slice(None), self.lo), self.r2l[i])
        self.add((g, self.y, self.x, self.net.c, slice(None), self.hi), self.r2r[i])

    def own(self, g):
        return self.data.at[g, self.y, self.x, self.net.c]

    def sent(self, g, i):
        for copy in self.copies0(g, i) + self.copies1(g, i) + self.copies2(g, i):
            copy.wait_send()


def packed_thirds(own):
    low = lax.broadcasted_iota(jnp.int32, (1, 128), 1) < HEAD
    for z in range(Z):
        s, u = z % 2, z // 2
        third = [own(2)[:, c * 256 + u * 128 : c * 256 + u * 128 + 128].astype(F32) for c in range(3)]
        third.append(own(3)[:, 512 + u * 128 : 512 + u * 128 + 128].astype(F32))
        for j in range(2):
            a, b = third[2 * j], third[2 * j + 1]
            both = jnp.where(low, a, pltpu.roll(b, HEAD, 1)) if s == 0 else jnp.where(low, pltpu.roll(a, HEAD, 1), b)
            yield z, j, both.astype(BF16)


def layer_kernel(len_ref, gs_ref, was_h, tok_h, cot_h, wgu_h, wd_h, cos_h, sin_h,
                 lo_out, gx_out, grads_out, gg_ref, q_h, k_h, hid_h,
                 x_ref, cot_ref, cos_ref, sin_ref, wa_ref, gm_ref, ctxt_ref, lse_ref, hid_ref,
                 b1, b2, lo_ref, t1, t2, wide, f1, dlt_ref, gains_ref, gsum_ref, boxes_ref, boxes2_ref, pack_ref,
                 mc, mx, my, ml, mr, mz, ga_ref, ax, ay, al, ar, az,
                 send, recv, local, credit):
    t, d = x_ref.shape
    part = t // Z
    f = gm_ref.shape[-1] // 3
    net = Net(send, recv, local)
    z, yx, c = net.z, net.yx, net.c
    length = len_ref[z]
    spot = (net.d * Z + z) * gs_ref.shape[1]
    px, py = lax.rem(yx, 2), yx // 2
    mine = pl.ds(pl.multiple_of(z * part, part), part)
    kd = flip(flip(yx, 1), 2)
    order = ((1, 0, 2, 3), (0, 1, 2, 3), (3, 2, 1, 0), (2, 3, 1, 0))

    def chunk(i):
        if not isinstance(i, int):
            return sum((i == k).astype(jnp.int32) * chunk(k) for k in range(Z))
        return sum((z == k).astype(jnp.int32) * order[k][i] for k in range(Z))

    a_half = (slice(0, 2 * d), slice(2 * d, 4 * d))
    m_half = (slice(0, 3 * f // 2), slice(3 * f // 2, 3 * f))
    a_slab = lambda k: wa_ref.at[k, c]
    m_slab = lambda i: lambda k: gm_ref.at[chunk(i), k // 2, lax.rem(k, 2), c]
    mine_slab = lambda i: m_slab(i)(yx)

    def line(k, right):
        shard = z - (k - 1) if right else z + (k - 1)
        place = gm_ref.at[shard, py, px, c]
        return net.make(76 + 2 * k + right, place, place, (net.d, z + 1 if right else z - 1))

    def came(k, right):
        place = gm_ref.at[z - k if right else z + k, py, px, c]
        return net.make(76 + 2 * k + right, place, place, (net.d, z - 1 if right else z + 1))

    def line_go(k):
        pl.when((z >= k - 1) & (z <= Z - 2))(lambda: line(k, 1).start())
        pl.when((z <= Z - k) & (z >= 1))(lambda: line(k, 0).start())

    def line_wait(k):
        pl.when(z >= k)(lambda: came(k, 1).wait_recv())
        pl.when(z <= Z - 1 - k)(lambda: came(k, 0).wait_recv())

    def line_left(k):
        pl.when((z >= k - 1) & (z <= Z - 2))(lambda: line(k, 1).wait_send())
        pl.when((z <= Z - k) & (z >= 1))(lambda: line(k, 0).wait_send())

    def chunk_out(i):
        net.got(f"m{i}l", f"m{i}r")
        net.go(f"m{i}c")

    plan_gather(net, "a", wa_ref.at[yx, c], a_slab, a_half)
    for i in range(Z):
        plan_gather(net, f"m{i}", mine_slab(i), m_slab(i), m_half)
        rows = gm_ref.at[chunk(i), :, :, c]
        net.plan(f"m{i}c", rows, rows, net.core)

    gsum_ref[...] = jnp.zeros_like(gsum_ref)
    gsum_ref[0:2, 0 : gs_ref.shape[1]] = gs_ref[...]
    gains_ref[...] = pltpu.roll(gsum_ref[...], spot, 1)
    net.barrier()
    gains_steps = all_sum(net, "g", gains_ref, boxes_ref)
    next(gains_steps)
    for r in range(1, Z):
        net.start(f"az{r}", was_h, pack_ref.at[z], (net.d, net.peer(r)))
    net.keep("a", was_h, pack_ref.at[z])
    net.keep("mg", wgu_h.at[0], gm_ref.at[z, py, px, c, :, 0:f])
    net.keep("mu", wgu_h.at[1], gm_ref.at[z, py, px, c, :, f : 2 * f])
    net.keep("md", wd_h, gm_ref.at[z, py, px, c, :, 2 * f : 3 * f])
    net.keep("t", tok_h.at[z], x_ref.at[mine])
    net.keep("c", cot_h.at[z], cot_ref.at[mine])
    net.keep("cos", cos_h, cos_ref)
    net.keep("sin", sin_h, sin_ref)
    next(gains_steps)
    for name in ("mg", "mu", "md"):
        net.kept(name)
    net.got("az1", "az2", "az3")
    line_go(1)
    for r in range(1, Z):
        net.start(f"t{r}", tok_h.at[net.peer(r)], x_ref.at[mine], (net.d, net.peer(r)))
    net.kept("a")
    for i, heads in enumerate(lane_pairs(pack_ref, 4 * d // Z)):
        for j, value in enumerate(heads):
            wa_ref[yx, c, :, i * d + j * 128 : i * d + (j + 1) * 128] = value
    spread(net, "a")
    net.start("ac0", wa_ref.at[yx, c], wa_ref.at[yx, c], net.core)
    for _ in range(3):
        next(gains_steps)
    for r in range(1, Z):
        net.left(f"gz{r}")
    gains_ref[...] = boxes_ref[9]
    relay(net, "a")
    spread(net, "m1")
    net.start("ac1", a_slab(flip(yx, 1)), a_slab(flip(yx, 1)), net.core)
    net.start("ac2", a_slab(flip(yx, 2)), a_slab(flip(yx, 2)), net.core)
    net.got("al", "ar")
    net.start("ac3", a_slab(kd), a_slab(kd), net.core)
    line_wait(1)
    net.got("t1", "t2", "t3")
    net.kept("t")
    line_go(2)
    for r in range(1, Z):
        net.plan(f"c{r}", cot_h.at[net.peer(r)], cot_ref.at[mine], (net.d, net.peer(r)))
    pl.when(lax.rem(z, 2) == 1)(lambda: net.go("c1", "c2", "c3"))
    spread(net, "m0")
    n1_ref = b1
    norm_stage(t, x_ref, gains_ref, n1_ref)
    net.kept("cos")
    net.kept("sin")
    net.got("ac0", "ac1", "ac2", "ac3")

    q_ref, k_ref, v_ref = (wide.at[:, i * d : (i + 1) * d] for i in range(3))
    qkv_stage(t, d, n1_ref, wa_ref, cos_ref, sin_ref, (q_ref, k_ref, v_ref))
    for name, src, dst in (("q", q_ref, q_h), ("k", k_ref, k_h)):
        net.keep(name, src, dst)
    pl.when(lax.rem(z, 2) == 0)(lambda: net.go("c1", "c2", "c3"))
    relay(net, "m1")
    attend = functools.partial(attend_stage, t, d, length, q_ref, k_ref, v_ref, ctxt_ref, lse_ref)
    attend(0, 3)
    line_wait(2)
    line_go(3)
    spread(net, "m2")
    relay(net, "m0")
    chunk_out(1)
    attend(3, d // 128)
    chunk_out(0)
    out_stage(t, d, length, x_ref, wa_ref, ctxt_ref, hid_ref)

    mred = Reduce(net, 86, gm_ref, lambda i: i, credit, mc, mx, my, ml, mr)
    ared = Reduce(net, 106, ga_ref, lambda i: 4 + lax.rem(i + 1, 4), credit, mc, ax, ay, al, ar)

    def mz_copy(w, r):
        return net.make(126 + r, mred.own(w), mz.at[r - 1], (net.d, w))

    def mz_out(i):
        w = chunk(i)
        mz_copy(w, lax.rem(w + Z - z, Z)).start()

    net.keep("hid", hid_ref, hid_h)
    hid_back = pltpu.make_async_copy(hid_h, hid_ref, local.at[23])
    n2_ref, dm_ref, n2t_ref, dmt_ref = b1, b2, t1, t2

    @pl.loop(0, t // BLK)
    def _(m):
        rs = rows_of(m)
        unit, _ = norm_rows(hid_ref[rs, :], None)
        n2 = jnp.where(token_mask(m, length), unit * gains_ref[1:2, :], 0.0).astype(BF16)
        n2_ref[rs, :] = n2
        n2t_ref[:, rs] = n2.T

    def chunk_left(i):
        for tag in ("x", "y", "l", "r", "c"):
            net.left(f"m{i}{tag}")

    def last_shard():
        line_wait(3)
        spread(net, "m3")

    arrived = (
        (lambda: net.got("m1c"),),
        (lambda: relay(net, "m3"), lambda: net.got("m2c")),
        (lambda: net.got("m3c"),),
        (),
    )
    middle = (
        (lambda: line_left(1), lambda: line_left(2), lambda: chunk_out(2)),
        (lambda: line_left(3), lambda: chunk_out(3), lambda: mred.p1(chunk(0), 0)),
        (lambda: mred.p2(chunk(0), 0), lambda: mred.p1(chunk(1), 1)),
        (lambda: mred.p3(chunk(0), 0), lambda: mz_out(0), lambda: mred.p1(chunk(2), 2)),
    )

    def at(i, steps):
        for k in range(Z):
            if steps[k]:

                @pl.when(i == k)
                def _():
                    for step in steps[k]:
                        step()

    f1[...] = jnp.zeros_like(f1)
    net.kept("hid")
    net.kept("q")
    net.kept("k")
    relay(net, "m2")
    net.got("m0c")
    mlp_out(f, d, gm_ref.at[chunk(0)], n2_ref, wide, hid_ref)
    peer_rows = [rows_of(net.peer(j)) for j in range(Z)]
    for j in range(1, Z):
        net.plan(f"lo{j}", lo_ref.at[peer_rows[j]], lo_out.at[z], (net.d, net.peer(j)))

    @pl.loop(0, Z)
    def _(i):
        at(i, arrived)
        ahead = gm_ref.at[chunk(i + 1)]
        pl.when(i < Z - 1)(lambda: mlp_out(f, d, ahead, n2_ref, wide, hid_ref))

        @pl.when(i == 0)
        def _():
            last_shard()
            net.got("c1", "c2", "c3")
            net.kept("c")

            for m in range(t // BLK):
                rs = slice(m * BLK, (m + 1) * BLK)
                dm = jnp.where(token_mask(m, length), cot_ref[rs, :], jnp.zeros((), BF16))
                dm_ref[rs, :] = dm
                dmt_ref[:, rs] = dm.T

        @pl.when(i == Z - 2)
        def _():
            for j in (2, 1, 3, 0):
                rs = peer_rows[j]
                lo_ref[rs, :] = hid_ref[rs, :].astype(BF16)
                if j:
                    net.go(f"lo{j}")
            hid_back.start()

        gm = gm_ref.at[chunk(i)]
        mlp_front(f, d, gm, n2_ref, dm_ref, wide)
        at(i, middle)
        at(i, tuple((functools.partial(chunk_left, k),) for k in range(Z)))
        mlp_back(f, d, gm, n2t_ref, dmt_ref, wide, f1)
        mred.p0(chunk(i), i)

    net.keep("lo", lo_ref.at[peer_rows[0]], lo_out.at[z])
    for name, src, dst in (("q2", q_h, q_ref), ("k2", k_h, k_ref)):
        net.keep(name, src, dst)
    gsum_ref[...] = jnp.zeros_like(gsum_ref)
    dh_ref, da_ref = hid_ref, b1
    hid_back.wait()

    @pl.loop(0, t // BLK)
    def _(m):
        rs = rows_of(m)
        hid = hid_ref[rs, :]
        ok = token_mask(m, length)
        unit, r = norm_rows(hid, None)
        dn2 = f1[rs, :]
        gsum_ref[1:2, :] += jnp.sum(dn2 * unit, axis=0, keepdims=True)
        e2 = dn2 * gains_ref[1:2, :]
        dh = cot_ref[rs, :].astype(F32) + r * (e2 - unit * jnp.mean(e2 * unit, axis=-1, keepdims=True))
        dh_ref[rs, :] = dh
        da_ref[rs, :] = jnp.where(ok, dh, 0.0).astype(BF16)

    mred.p2(chunk(1), 1)
    mred.p1(chunk(3), 3)

    dat_ref, n1t_ref, dctx_ref = t1, t2, cot_ref
    dat_ref[...] = da_ref[...].T
    shape = ga_ref.shape[1:5]

    @pl.loop(0, d // 256)
    def _(j):
        rs = pl.ds(pl.multiple_of(j * 256, 256), 256)
        cols = pl.ds(pl.multiple_of(3 * d + j * 256, 256), 256)
        ga_ref[3, :, :, :, :, rs] = nt(dat_ref[...], ctxt_ref[rs, :]).astype(BF16).reshape(shape + (256,))
        dctx = nn(da_ref[...], wa_cols(wa_ref, cols)).astype(BF16)
        dctx_ref[:, rs] = dctx
        prod = dctx.T.astype(F32) * ctxt_ref[rs, :].astype(F32)
        for h in range(4):
            dlt_ref[pl.ds(j * 4 + h, 1), :] = jnp.sum(prod[h * HEAD : (h + 1) * HEAD], axis=0, keepdims=True)

    mred.p2(chunk(2), 2)
    ared.p0(3, 3)

    @pl.loop(0, t // BLK)
    def _(m):
        rs = rows_of(m)
        unit, _ = norm_rows(x_ref[rs, :].astype(F32), None)
        n1t_ref[:, rs] = (unit * gains_ref[0:1, :]).astype(BF16).T

    net.kept("q2")
    net.kept("k2")
    dk_acc, dv_acc = f1.at[:, 0:128], f1.at[:, 128:256]
    lanes = dict(o=slice(512 - 128, 512), q=slice(0, 384), t=slice(512, 768))

    def to_owner(base, w, tag):
        r = lax.rem(w + Z - z, Z)

        @pl.when(r != 0)
        def _():
            net.make(base + r - 1, pack_ref.at[w, :, lanes[tag]], az.at[r - 1, :, lanes[tag]], (net.d, w)).start()

    def pack_out():
        for w in range(Z):
            at = PAIRS.index(w) * 128
            pack_ref[w, :, lanes["o"]] = ared.own(3)[:, at : at + 128]
            to_owner(132, w, "o")

    def pack_pairs(g):
        for s in range(2):
            w = PAIRS[2 * g + s]
            for k in range(3):
                pack_ref[w, :, k * 128 : (k + 1) * 128] = ared.own(g)[:, k * 256 + s * 128 : k * 256 + s * 128 + 128]
            to_owner(135, w, "q")

    def pack_thirds():
        for w, j, value in packed_thirds(ared.own):
            pack_ref[w, :, 512 + j * 128 : 640 + j * 128] = value
        for w in range(Z):
            to_owner(138, w, "t")

    def heads_out(g):
        for k in range(3):
            cols = pl.ds(pl.multiple_of(k * d + g * 256, 256), 256)
            ga_ref[g, :, :, :, :, k * 256 : (k + 1) * 256] = nn(n1t_ref[...], wide[:, cols]).astype(BF16).reshape(shape + (256,))
        ared.p0(g, g)

    first = (
        (lambda: ared.p1(3, 3),),
        (lambda: ared.p2(3, 3), lambda: ared.p1(0, 0)),
        (lambda: ared.p2(0, 0), lambda: ared.p1(1, 1)),
    )
    second = (
        (lambda: mred.p3(chunk(2), 2), lambda: mz_out(2), lambda: mred.p2(chunk(3), 3)),
        (lambda: mred.p3(chunk(3), 3), lambda: mz_out(3), lambda: ared.p3(3, 3), pack_out),
        (lambda: ared.p3(0, 0), lambda: pack_pairs(0), lambda: mred.p3(chunk(1), 1)),
    )

    @pl.loop(0, 3)
    def _(g):
        @pl.loop(0, 2)
        def _(s):
            p = 2 * g + s
            attend_back(t, d, length, q_ref, k_ref, v_ref, dctx_ref, lse_ref, dlt_ref, cos_ref, sin_ref, wide, dk_acc, dv_acc, p, p + 1)
            for k in range(3):
                for steps, which in ((first, 0), (second, 1)):

                    @pl.when((g == k) & (s == which))
                    def _():
                        for step in steps[k]:
                            step()

        heads_out(g)

    gx_ref = b1
    for j in (2, 1, 3, 0):
        m = net.peer(j)
        rs = rows_of(m)
        dn1 = nt(wide[rs, :], wa_cols(wa_ref, slice(0, 3 * d)))
        unit, r = norm_rows(x_ref[rs, :].astype(F32), None)
        gsum_ref[0:1, :] += jnp.sum(dn1 * unit, axis=0, keepdims=True)
        e1 = dn1 * gains_ref[0:1, :]
        gx_ref[rs, :] = (dh_ref[rs, :] + r * (e1 - unit * jnp.mean(e1 * unit, axis=-1, keepdims=True))).astype(BF16)
        if j:
            net.start(f"gx{j}", gx_ref.at[rs], gx_out.at[z], (net.d, m))
        else:
            net.keep("gx", gx_ref.at[rs], gx_out.at[z])
        if j == 2:
            ared.p2(1, 1)
            ared.p1(2, 2)
        elif j == 3:
            ared.p3(1, 1)
            pack_pairs(1)
        elif j == 0:
            ared.p2(2, 2)
    steps = all_sum(net, "s", gsum_ref, boxes2_ref, last=True)
    next(steps)
    next(steps)
    ared.p3(2, 2)
    pack_thirds()
    next(steps)
    next(steps)
    total = mred.own(z)[...].astype(F32)
    for r in range(1, Z):
        mz_copy(net.peer(r), r).wait_recv()
        total = total + mz[r - 1].astype(F32)
    rows, half = total.shape[0], total.shape[1] // 2
    f1[0:rows, :] = total[:, :half]
    f1[rows : 2 * rows, :] = total[:, half:]

    parts = [
        net.make(base + r - 1, pack_ref.at[net.peer(r), :, lanes[tag]], az.at[r - 1, :, lanes[tag]], (net.d, net.peer(r)))
        for base, tag in ((132, "o"), (135, "q"), (138, "t"))
        for r in range(1, Z)
    ]
    for copy in parts:
        copy.wait_recv()
    total = pack_ref[z].astype(F32)
    for i in range(Z - 1):
        total = total + az[i].astype(F32)
    f1[2 * rows : 3 * rows, :] = total
    net.keep("grads", f1.at[0 : 3 * rows], grads_out)
    next(steps)
    gg_ref[...] = pltpu.roll(boxes2_ref[9], d - spot, 1)[0:2, 0 : gs_ref.shape[1]]
    net.got(*(f"{n}{j}" for n in ("lo", "gx") for j in range(1, Z)))
    for name in ("lo", "gx", "grads"):
        net.kept(name)
    for i in range(Z):
        mred.sent(chunk(i), i)
        ared.sent(i, i)
    for copy in parts:
        copy.wait_send()
    for r in range(1, Z):
        mz_copy(net.peer(r), r).wait_send()
    net.finish()


VM = pl.BlockSpec(memory_space=pltpu.VMEM)
SM = pl.BlockSpec(memory_space=pltpu.SMEM)


def call(kernel, ins, outs, scratch):
    return pl.pallas_call(
        kernel,
        out_shape=[jax.ShapeDtypeStruct(s, dt) for s, dt in outs],
        in_specs=[SM] + [VM] * (len(ins) - 1),
        out_specs=[VM] * len(outs),
        scratch_shapes=[pltpu.VMEM(s, dt) for s, dt in scratch],
        compiler_params=pltpu.CompilerParams(vmem_limit_bytes=60 * 2**20),
    )(*ins)


def backward(length, x, cot, gains, wa, wm, cosine, sine, q, k, v, ctxt, lse, hid):
    t, d = x.shape
    f = wm.shape[-1] // 3
    heads = lse.shape[0]
    td, dt = ((t, d), BF16), ((d, t), BF16)
    lo, dh, da, gm, gg2 = call(
        k2,
        (length, cot, gains, hid, wm),
        (td, ((t, d), F32), td, (wm.shape, BF16), ((1, d), F32)),
        (td, td, dt, dt, ((t, 3 * f), BF16), ((t, d), F32), ((t, d), F32)),
    )
    gx, ga, gg1 = call(
        k3,
        (length, x, gains, wa, cosine, sine, q, k, v, ctxt, lse, dh, da),
        (td, (wa.shape, BF16), ((1, d), F32)),
        (td, dt, dt, td, ((heads, t), F32), ((t, 3 * d), BF16), ((t, 128), F32), ((t, 128), F32), ((t, d), F32)),
    )
    return lo, gx, ga, gm, jnp.concatenate([gg1, gg2])


def one_sequence(length, x, cot, gains, wa, wm, cosine, sine):
    t, d = x.shape
    heads = -(-d // HEAD // 8) * 8
    td, dt = ((t, d), BF16), ((d, t), BF16)
    kept = call(k1_alone, (length, x, gains, wa, cosine, sine), (td, td, td, dt, ((heads, t), F32), ((t, d), F32)), (td,))
    return backward(length, x, cot, gains, wa, wm, cosine, sine, *kept)


def pack_weights(w_qkv, w_out, w_gate_up, w_down):
    attn = jnp.stack([w_qkv[0], w_qkv[1], w_qkv[2], w_out.T], axis=1)
    mlp = jnp.concatenate([w_gate_up[0], w_gate_up[1], w_down.T], axis=1)
    return attn, mlp


def unpack_grads(g_attn, g_mlp, fw):
    g_qkv = jnp.transpose(g_attn[:, :3], (1, 0, 2))
    g_gate_up = jnp.stack([g_mlp[:, i * fw : (i + 1) * fw] for i in range(2)])
    return g_qkv, g_attn[:, 3].T, g_gate_up, g_mlp[:, 2 * fw :].T


def to_sequences(local):
    return lax.all_to_all(local, "tp", split_axis=0, concat_axis=1, tiled=True)


def to_positions(whole):
    return lax.all_to_all(whole, "tp", split_axis=1, concat_axis=0, tiled=True)


def fused_layer(lengths, tokens, cotangent, w_qkv, w_out, w_gate_up, w_down, gains, cosine, sine):
    batch, part, d = tokens.shape
    t, rows, f3 = part * Z, w_qkv.shape[1], 3 * w_gate_up.shape[2]
    heads = -(-d // HEAD // 8) * 8
    pairs = 2 * HEAD
    four = (w_qkv[0], w_qkv[1], w_qkv[2], w_out.T)
    was = jnp.concatenate([w[:, :pairs] for w in four] + [w[:, pairs:] for w in four], axis=1)
    hbm = pl.BlockSpec(memory_space=pl.ANY)
    moved = ((Z, part, d), BF16)
    td, dt, big, small = ((t, d), BF16), ((d, t), BF16), ((t, d), F32), ((8, d), F32)
    outs = (moved, moved, ((3 * rows, d), F32), (gains.shape, F32), td, td, big)

    def boxes(cols, last=Z - 1):
        pair = ((4, 2, rows, cols // 2), BF16)
        one = ((4, rows, cols // 2), BF16)
        return [pair, pair, one, one, ((last, rows, cols), BF16)]

    wm = ((Z, 2, 2, 2, rows, f3), BF16)
    stage = ((Z, rows, d), BF16)
    lse = ((heads, t), F32)
    scratch = [td, td] + [(cosine.shape, F32)] * 2 + [((4, 2, rows, 4 * d), BF16), wm, dt, lse, big]
    scratch += [td, td, td, dt, dt, ((t, 3 * d), BF16), big, lse, small, small, ((10, 8, d), F32), ((10, 8, d), F32), stage]
    scratch += [((2, 2, 2, rows, f3), BF16)] + boxes(f3) + [((4, 2, 2, 2, rows, d), BF16)] + boxes(d)
    return pl.pallas_call(
        layer_kernel,
        out_shape=[jax.ShapeDtypeStruct(s, dt_) for s, dt_ in outs],
        in_specs=[SM, VM] + [hbm] * 7,
        out_specs=[hbm, hbm, hbm, VM, hbm, hbm, hbm],
        scratch_shapes=[pltpu.VMEM(s, dt_) for s, dt_ in scratch]
        + [pltpu.SemaphoreType.DMA((144,)), pltpu.SemaphoreType.DMA((144,)), pltpu.SemaphoreType.DMA((24,)), pltpu.SemaphoreType.REGULAR],
        compiler_params=pltpu.CompilerParams(collective_id=0, has_side_effects=True, vmem_limit_bytes=62 * 2**20),
    )(lengths, gains, was, tokens, cotangent, w_gate_up, w_down.T, cosine, sine)[:4]


def fits(mesh_dp, tokens, w_qkv, w_gate_up):
    tp = lax.axis_size("tp")
    rows, hw = w_qkv.shape[1:]
    return (
        mesh_dp == 8 and tp == Z and tokens.shape[0] == Z and hw == 3 * HEAD and rows % 16 == 0
        and w_gate_up.shape[2] % 256 == 0 and 3 * w_gate_up.shape[2] <= 2 * tokens.shape[2] and tokens.shape[1] % BLK == 0
    )


def body(tokens, lengths, w_qkv, w_out, w_gate_up, w_down, gains, cotangent):
    tp, dp = lax.axis_size("tp"), lax.axis_size("dp")
    batch, part, d = tokens.shape
    n, t = batch // tp, part * tp
    fw = w_gate_up.shape[2]
    cosine, sine = map(jnp.asarray, rope_np(t))
    attn, mlp = pack_weights(w_qkv, w_out, w_gate_up, w_down)
    own = lax.dynamic_slice_in_dim(lengths, lax.axis_index("tp") * n, n)
    if fits(dp, tokens, w_qkv, w_gate_up):
        out, gx, grads, s_gains = fused_layer(lengths, tokens, cotangent, w_qkv, w_out, w_gate_up, w_down, gains, cosine, sine)
        pairs, rows = 2 * HEAD, w_qkv.shape[1]
        s_mlp = jnp.concatenate([grads[:rows], grads[rows : 2 * rows]], axis=1)
        s_attn = grads[2 * rows :]
        first, third = s_attn[:, : 4 * pairs], s_attn[:, 4 * pairs :]
        s_attn = jnp.concatenate([first.reshape(-1, 4, pairs), third.reshape(-1, 4, HEAD)], axis=2)
        gx = gx.astype(F32)
    else:
        full_gains = lax.all_gather(gains, ("dp", "tp"), axis=1, tiled=True)
        full_gains = jnp.pad(full_gains, ((0, 6), (0, 0)))
        x16 = to_sequences(tokens)
        wa = lax.all_gather(attn, "tp", axis=2, tiled=True).reshape(attn.shape[0], 4 * d)
        wa = lax.all_gather(wa, "dp", axis=0, tiled=True).reshape(1, 1, d, 4 * d)
        wm = lax.all_gather(lax.all_gather(mlp, "tp", axis=0), "dp", axis=1, tiled=True).reshape(tp, 1, 1, d, 3 * fw)
        cot16 = to_sequences(cotangent)
        los, gxs, ga, gm, gg = [], [], 0.0, 0.0, 0.0
        for i in range(n):
            lo, gx, a, m, g = one_sequence(own[i : i + 1], x16[i], cot16[i], full_gains, wa, wm, cosine, sine)
            los.append(lo)
            gxs.append(gx)
            ga, gm, gg = ga + a.astype(F32), gm + m.astype(F32), gg + g
        out = to_positions(jnp.stack(los))
        gx = to_positions(jnp.stack(gxs)).astype(F32)
        ga, gm = ga.reshape(d, 4, d), gm.reshape(tp, d, 3 * fw)
        s_mlp = lax.psum_scatter(lax.psum_scatter(gm, "dp", scatter_dimension=1, tiled=True), "tp", scatter_dimension=0)
        s_attn = lax.psum_scatter(ga.reshape(d, 4 * d), "dp", scatter_dimension=0, tiled=True)
        s_attn = lax.psum_scatter(s_attn.reshape(-1, 4, d), "tp", scatter_dimension=2, tiled=True)
        s_gains = lax.psum_scatter(gg, ("dp", "tp"), scatter_dimension=1, tiled=True)
    return (out, gx) + unpack_grads(s_attn, s_mlp, fw) + (s_gains,)


def solution(mesh):
    act = P("dp", "tp", None)
    cols, rows, gain = P(None, "dp", "tp"), P("tp", "dp"), P(None, ("dp", "tp"))
    return jax.shard_map(
        body,
        mesh=mesh,
        in_specs=(act, P("dp"), cols, rows, cols, rows, gain, act),
        out_specs=(act, act, cols, rows, cols, rows, gain),
        check_vma=False,
    )
```
